32 devices in a mesh: tm: 8 (over y, x, core), freq: 4 (over z).
Axes of the slice: x: 2, y: 2, z: 4, core: 2. Of those that a mesh axis runs over, the one named last changes fastest.
Arguments:
- increments: float32 [1024, 4, 128], P('tm'), may hold values from -6 to 6
- projections: float32 [128, 3, 4096], P(None, None, 'freq'), may hold values from -0.5 to 0.5
- phases: float32 [3, 4096], P(None, 'freq'), may hold values from -3.140625 to 3.140625
- groups: int32 [4], replicated, may hold values from 0 to 1, as said below
Outputs:
- grad_increments: float32 [1024, 4, 128], P(('tm', 'freq'))
- grad_projections: float32 [128, 3, 4096], P('tm', None, 'freq')
The draws below stay inside these ranges and needn't reach their ends.
Inputs may be any that keep to these rules, and one draw needn't show every extreme that they name: `groups`: exactly 2 sequences have 1.
All inputs are finite; a program needn't handle non-finite values.
Results may differ from the reference program's by a relative error of at most 0.0003.
Values sent between devices are 32-bit elements; how exact they have to be, the bound alone decides.
No kernel may reach another device: no remote copies, remote signals or barrier semaphores. Data moves between devices by JAX's collectives and lax.ppermute only.
A program may use at most 64 MiB of HBM per device.

```python
import math
import jax
import jax.numpy as jnp
from jax import lax

CH = 128
FREQS = 4096
LEVELS = 3
BATCH = 4
LENGTH = 1024
N_FREQ = 4


def draw_groups(key, part):
    order = jax.random.permutation(key, BATCH)
    return (order < BATCH // 2).astype(jnp.int32)


def levels(rng, extent, cuts, least, largest):
    def one(position, parts):
        heights = jax.random.uniform(jax.random.fold_in(jax.random.fold_in(rng, 6), position), (parts,), jnp.float32, least / len(cuts), largest / len(cuts))
        return jnp.repeat(jnp.exp(heights), extent[position] // parts).reshape((-1,) + (1,) * (len(extent) - position - 1))

    level = one(*cuts[0])
    for cut in cuts[1:]:
        level = level * one(*cut)
    return level


def centred(own_key, shape, scale, reach, pieces=(), held_as=jnp.bfloat16):
    entries = scale * jax.random.normal(own_key, shape, jnp.float32)
    if pieces:
        entries = entries * levels(own_key, shape, pieces, -0.22, 0.18)
    return jnp.clip(entries, -reach, reach).astype(held_as)


def setup_inputs(seed: int = 0) -> dict:
    key_of = jax.random.split(jax.random.key(seed), 5)
    return {
        "increments": centred(key_of[0], (LENGTH, BATCH, CH), 1.0, 6.0, ((0, 8),), jnp.float32),
        "projections": centred(key_of[1], (CH, LEVELS, FREQS), CH ** -0.5, 0.5, ((2, 4),), jnp.float32),
        "phases": jnp.clip(jax.random.uniform(key_of[2], (LEVELS, FREQS), jnp.float32, -3.140625, 3.140625), -3.140625, 3.140625),
        "groups": draw_groups(jax.random.fold_in(key_of[4], 71), 0),
    }


highest = lax.Precision.HIGHEST

def before_sum(values):
    return jnp.cumsum(values, axis=0) - values

def after_sum(values):
    return lax.optimization_barrier(jnp.sum(values, axis=0, keepdims=True)) - jnp.cumsum(values, axis=0)

def reference(increments, projections, phases, groups):
    length, batch, chans = increments.shape
    amplitude = math.sqrt(2.0 / length)
    set_weight = jnp.where(groups == 1, 2.0 / batch, -2.0 / batch).astype(jnp.float32)[:, None]
    width = FREQS // N_FREQ
    block_proj = projections.reshape(chans, LEVELS, N_FREQ, width).transpose(2, 0, 1, 3)
    block_phase = phases.reshape(LEVELS, N_FREQ, width).transpose(1, 0, 2)

    def one_block(running, operands):
        proj_block, phase_block = operands
        angles = [jnp.einsum('tbc,cf->tbf', increments, proj_block[:, degree, :], precision=highest) + phase_block[degree][None, None, :] for degree in range(3)]
        waves = [amplitude * jnp.cos(angle) for angle in angles]
        front1 = before_sum(waves[0])
        term2 = front1 * waves[1]
        front2 = before_sum(term2)
        term3 = front2 * waves[2]
        totals = [lax.optimization_barrier(jnp.sum(waves[0], axis=0)), lax.optimization_barrier(jnp.sum(term2, axis=0)), lax.optimization_barrier(jnp.sum(term3, axis=0))]
        seeds = [2.0 * set_weight * lax.optimization_barrier(jnp.sum(set_weight * total, axis=0))[None, :] for total in totals]
        adjoint1 = seeds[1][None] + seeds[2][None] * after_sum(waves[2])
        adjoint0 = seeds[0][None] + after_sum(adjoint1 * waves[1])
        dirs = [adjoint0, adjoint1 * front1, seeds[2][None] * front2]
        slopes = [-amplitude * jnp.sin(angles[degree]) * dirs[degree] for degree in range(3)]
        grads = jnp.stack([jnp.einsum('tbc,tbf->cf', increments, slope, precision=highest) for slope in slopes], axis=1)
        update = running
        for degree in range(3):
            update = update + jnp.einsum('tbf,cf->tbc', slopes[degree], proj_block[:, degree, :], precision=highest)
        return (update, grads)
    start = jnp.zeros(increments.shape, jnp.float32)
    grad_increments, grads = lax.scan(one_block, start, (block_proj, block_phase))
    grad_projections = grads.transpose(1, 2, 0, 3).reshape(chans, LEVELS, FREQS)
    return (grad_increments, grad_projections)
```

```python
import math

import jax
import jax.numpy as jnp
from jax import lax
from jax.experimental import pallas as pl
from jax.experimental.pallas import tpu as pltpu
from jax.sharding import PartitionSpec as P

f32, bf16 = jnp.float32, jnp.bfloat16
SUB = 8
WIDE = 256
MAGIC = 12582912.0
SIN = (3.141582022150658, -5.167142796368909, 2.541899027590427, -0.5546361970970186)
COS = (
    0.9999999534666683,
    -4.934792858675264,
    4.058411914167107,
    -1.3318801612488937,
    0.2196967986036905,
)
NT = (((1,), (1,)), ((), ()))


def horner(z, coefs):
    acc = z * coefs[-1] + coefs[-2]
    for coef in coefs[-3::-1]:
        acc = acc * z + coef
    return acc


def split(value):
    high = value.astype(bf16)
    return high, (value - high.astype(f32)).astype(bf16)


def pair_rows(low, high):
    top = lax.broadcasted_iota(jnp.int32, low.shape, 0) < SUB // 2
    first = jnp.where(top, low, pltpu.roll(high, SUB // 2, 0))
    second = jnp.where(top, pltpu.roll(low, SUB // 2, 0), high)
    return first, second


def waves_kernel(amplitude, x_ref, p_ref, ph_ref, c_ref, s_ref, loc_ref, snd_ref, xs_ref, ang_ref):
    rows, chans = x_ref.shape
    half = rows // 2
    wide = p_ref.shape[2]
    inv = 1.0 / (2.0 * math.pi)
    root = math.sqrt(2.0 * amplitude)
    sin_coefs = [root * coef for coef in SIN]
    cos_coefs = [-root * coef for coef in COS]

    @pl.when(pl.program_id(0) == 0)
    def _():
        def one(k, _):
            at = pl.multiple_of(k * SUB, SUB)
            first, second = pair_rows(x_ref[pl.ds(at, SUB), :], x_ref[pl.ds(half + at, SUB), :])
            high, low = split(jnp.concatenate([first, second], axis=0))
            to = pl.ds(pl.multiple_of(k * 2 * SUB, 2 * SUB), 2 * SUB)
            xs_ref[to, :] = jnp.concatenate([high, low, high, low], axis=1)
            return 0

        lax.fori_loop(0, half // SUB, one, 0, unroll=4)

    for level in range(3):
        high, low = split(p_ref[level] * inv)
        stacked = jnp.concatenate([high, high, low, low], axis=0)
        turns = jnp.dot(xs_ref[...], stacked, preferred_element_type=f32)
        ang_ref[level] = turns + ph_ref[level : level + 1, :] * inv

    zero = jnp.zeros((SUB, wide), f32)

    def step(i, carry):
        s0, s1, s2, s01, s12, s012 = carry
        at = pl.ds(pl.multiple_of(i * SUB, SUB), SUB)
        cosines = []
        for level in range(3):
            turn = ang_ref[level, at, :]
            r = turn - ((turn + MAGIC) - MAGIC)
            z = r * r
            sine = r * horner(z, sin_coefs)
            cosine = horner(z, cos_coefs)
            wave = amplitude - sine * sine
            c_ref[0, level, at, :] = wave
            s_ref[0, level, at, :] = sine * cosine
            cosines.append(wave)
        c0, c1, c2 = cosines
        s012 = s012 + s01 * c2
        s12 = s12 + s1 * c2
        s01 = s01 + s0 * c1
        return (s0 + c0, s1 + c1, s2 + c2, s01, s12, s012)

    sums = lax.fori_loop(0, rows // SUB, step, (zero,) * 6, unroll=4)
    for k in range(6):
        loc_ref[SUB * k : SUB * (k + 1), :] = sums[k]
    hb = SUB // 2
    a0, a1, a2, a01, a12, a012 = [v[:hb] for v in sums]
    b0, b1, b2, b01, b12, b012 = [v[hb:] for v in sums]
    both = (
        a0 + b0,
        a1 + b1,
        a2 + b2,
        a01 + b01 + a0 * b1,
        a12 + b12 + a1 * b2,
        a012 + b012 + a0 * b12 + a01 * b2,
    )
    for k in range(6):
        snd_ref[hb * k : hb * (k + 1), :] = both[k]


def grads_kernel(sizes, place_ref, groups_ref, *refs):
    n_tm, n_freq, batch = sizes
    x_ref, p_ref, c_ref, s_ref, loc_ref = refs[:5]
    got = refs[5 : 5 + n_tm]
    gk_ref, gs_ref, gi_ref = refs[5 + n_tm : 8 + n_tm]
    xt_ref, all_ref, u1_ref, sh_ref, sl_ref, w_ref, gp_ref, acc_ref, flat_ref = refs[8 + n_tm :]
    rows, chans = x_ref.shape
    half = rows // 2
    wide = p_ref.shape[2]
    hb = SUB // 2
    me, z = place_ref[0], place_ref[1]
    chunk = pl.program_id(0)

    @pl.when(chunk == 0)
    def _():
        def one(k, _):
            at = pl.multiple_of(k * SUB, SUB)
            first, second = pair_rows(x_ref[pl.ds(at, SUB), :], x_ref[pl.ds(half + at, SUB), :])
            to = pl.multiple_of(k * 2 * SUB, 2 * SUB)
            flat_ref[pl.ds(to, SUB), :] = first
            flat_ref[pl.ds(to + SUB, SUB), :] = second
            return 0

        lax.fori_loop(0, half // SUB, one, 0, unroll=4)
        high, low = split(flat_ref[...].T)
        xt_ref[:chans, :] = high
        xt_ref[chans:, :] = low
        acc_ref[...] = jnp.zeros_like(acc_ref)

    for d in range(n_tm):
        all_ref[jnp.bitwise_xor(me, d)] = got[d][...]

    def sums_of(j):
        return [all_ref[j, hb * k : hb * (k + 1), :] for k in range(6)]

    def forward(j, carry):
        p0, p01, p012 = carry
        b0, b1, b2, b01, b12, b012 = sums_of(j)
        p012 = p012 + b012 + p0 * b12 + p01 * b2
        p01 = p01 + b01 + p0 * b1
        return (p0 + b0, p01, p012)

    def backward(step, carry):
        t1, t2, t12 = carry
        b0, b1, b2, b01, b12, b012 = sums_of(n_tm - 1 - step)
        t12 = t12 + b12 + b1 * t2
        return (t1 + b1, t2 + b2, t12)

    zero = jnp.zeros((hb, wide), f32)
    entry = lax.fori_loop(0, me, forward, (zero,) * 3)
    e1, e2 = entry[:2]
    totals = lax.fori_loop(me, n_tm, forward, entry)
    t1, t2, t12 = lax.fori_loop(0, n_tm - 1 - me, backward, (zero,) * 3)

    row = lax.broadcasted_iota(jnp.int32, (hb, wide), 0)
    weight = zero
    for b in range(batch):
        value = jnp.where(groups_ref[b] == 1, 2.0 / batch, -2.0 / batch)
        weight = jnp.where(row == b, value, weight)
    seeds = [2.0 * weight * jnp.sum(weight * total, axis=0, keepdims=True) for total in totals]

    def local(k):
        return loc_ref[SUB * k : SUB * k + hb, :], loc_ref[SUB * k + hb : SUB * (k + 1), :]

    a0, _ = local(0)
    a1, b1 = local(1)
    _, b2 = local(2)
    a01, _ = local(3)
    _, b12 = local(4)

    def tall(first, second):
        return jnp.concatenate([first, second], axis=0)

    front1 = tall(e1, e1 + a0)
    front2 = tall(e2, e2 + a01 + e1 * a1)
    tail2 = tall(t2 + b2, t2)
    tail1 = tall(t1 + b1, t1)
    tail12 = tall(t12 + b12 + b1 * t2, t12)
    d0, d1, d2 = [tall(seed, seed) for seed in seeds]
    adjoint1 = d1 + d2 * tail2
    adjoint0 = d0 + d1 * tail1 + d2 * tail12

    def fwd(pair, carry):
        f1, f2 = carry
        slopes = []
        for which in range(2):
            at = pl.ds(pl.multiple_of((2 * pair + which) * SUB, SUB), SUB)
            u1_ref[at, :] = s_ref[0, 1, at, :] * f1
            slopes.append(s_ref[0, 2, at, :] * (d2 * f2))
            f2 = f2 + f1 * c_ref[0, 1, at, :]
            f1 = f1 + c_ref[0, 0, at, :]
        at = pl.ds(pl.multiple_of(pair * 2 * SUB, 2 * SUB), 2 * SUB)
        high, low = split(jnp.concatenate(slopes, axis=0))
        sh_ref[at, 2 * wide :] = high
        sl_ref[at, 2 * wide :] = low
        return f1, f2

    lax.fori_loop(0, rows // (2 * SUB), fwd, (front1, front2), unroll=2)

    def bwd(step, carry):
        g1, g0 = carry
        pair = rows // (2 * SUB) - 1 - step
        slope0, slope1 = [], []
        for which in (1, 0):
            at = pl.ds(pl.multiple_of((2 * pair + which) * SUB, SUB), SUB)
            slope1.append(u1_ref[at, :] * g1)
            slope0.append(s_ref[0, 0, at, :] * g0)
            g0 = g0 + g1 * c_ref[0, 1, at, :]
            g1 = g1 + d2 * c_ref[0, 2, at, :]
        at = pl.ds(pl.multiple_of(pair * 2 * SUB, 2 * SUB), 2 * SUB)
        for level, slopes in enumerate((slope0, slope1)):
            high, low = split(jnp.concatenate(slopes[::-1], axis=0))
            sh_ref[at, level * wide : (level + 1) * wide] = high
            sl_ref[at, level * wide : (level + 1) * wide] = low
        return g1, g0

    lax.fori_loop(0, rows // (2 * SUB), bwd, (adjoint1, adjoint0), unroll=2)

    each = chans // n_tm
    for level in range(3):
        cols = slice(level * wide, (level + 1) * wide)
        high, low = split(p_ref[level])
        w_ref[:chans, cols] = high
        w_ref[chans:, cols] = low
        main = jnp.dot(xt_ref[...], sh_ref[:, cols], preferred_element_type=f32)
        rest = jnp.dot(xt_ref[:chans, :], sl_ref[:, cols], preferred_element_type=f32)
        grad = main[:chans] + main[chans:] + rest
        for d in range(n_tm):
            gp_ref[d] = grad[each * d : each * (d + 1)]
        for j in range(n_tm // 2):
            keep = jnp.bitwise_xor(me, 2 * j)
            gk_ref[j, level] = gp_ref[keep]
            gs_ref[j, level] = gp_ref[jnp.bitwise_xor(keep, 1)]

    main = lax.dot_general(sh_ref[...], w_ref[...], NT, preferred_element_type=f32)
    rest = lax.dot_general(sl_ref[...], w_ref[:chans, :], NT, preferred_element_type=f32)
    acc_ref[...] += main[:, :chans] + main[:, chans:] + rest

    @pl.when(chunk == pl.num_programs(0) - 1)
    def _():
        def one(k, _):
            at = pl.multiple_of(k * SUB, SUB)
            to = pl.multiple_of(k * 2 * SUB, 2 * SUB)
            low, high = pair_rows(acc_ref[pl.ds(to, SUB), :], acc_ref[pl.ds(to + SUB, SUB), :])
            flat_ref[pl.ds(at, SUB), :] = low
            flat_ref[pl.ds(half + at, SUB), :] = high
            return 0

        lax.fori_loop(0, half // SUB, one, 0, unroll=4)
        piece = rows // n_freq
        for j in range(n_freq):
            at = pl.multiple_of(jnp.bitwise_xor(z, j) * piece, piece)
            gi_ref[j] = flat_ref[pl.ds(at, piece), :]


def swap(value, axis, distance):
    count = lax.axis_size(axis)
    return lax.ppermute(value, axis, [(i, i ^ distance) for i in range(count)])


def on_device(increments, projections, phases, groups):
    steps, batch, chans = increments.shape
    freqs = phases.shape[1]
    n_tm, n_freq = lax.axis_size("tm"), lax.axis_size("freq")
    amplitude = math.sqrt(2.0 / (steps * n_tm))
    rows = steps * batch
    wide = min(WIDE, freqs)
    chunks = freqs // wide
    each = chans // n_tm
    x = increments.reshape(rows, chans)
    p = jnp.transpose(projections, (1, 0, 2))
    params = pltpu.CompilerParams(vmem_limit_bytes=48 * 1024 * 1024)

    def waves_body(*refs):
        waves_kernel(amplitude, *refs)

    tall = lambda n: pl.BlockSpec((n, wide), lambda i: (0, i))
    big = pl.BlockSpec((1, 3, rows, wide), lambda i: (i, 0, 0, 0))
    cosines, sines, local, own = pl.pallas_call(
        waves_body,
        grid=(chunks,),
        in_specs=[
            pl.BlockSpec((rows, chans), lambda i: (0, 0)),
            pl.BlockSpec((3, chans, wide), lambda i: (0, 0, i)),
            pl.BlockSpec((3, wide), lambda i: (0, i)),
        ],
        out_specs=[big, big, tall(6 * SUB), tall(3 * SUB)],
        out_shape=[
            jax.ShapeDtypeStruct((chunks, 3, rows, wide), f32),
            jax.ShapeDtypeStruct((chunks, 3, rows, wide), f32),
            jax.ShapeDtypeStruct((6 * SUB, freqs), f32),
            jax.ShapeDtypeStruct((3 * SUB, freqs), f32),
        ],
        scratch_shapes=[pltpu.VMEM((rows, 4 * chans), bf16), pltpu.VMEM((3, rows, wide), f32)],
        compiler_params=params,
        name="waves",
    )(x, p, phases)

    got = [own] + [swap(own, "tm", d) for d in range(1, n_tm)]
    place = jnp.stack([lax.axis_index("tm"), lax.axis_index("freq")]).astype(jnp.int32)

    def grads_body(*refs):
        grads_kernel((n_tm, n_freq, batch), *refs)

    fixed = lambda *shape: pl.BlockSpec(shape, lambda i, *_: (0,) * len(shape))
    tall = lambda n: pl.BlockSpec((n, wide), lambda i, *_: (0, i))
    big = pl.BlockSpec((1, 3, rows, wide), lambda i, *_: (i, 0, 0, 0))
    gspec = pl.BlockSpec((n_tm // 2, 3, each, wide), lambda i, *_: (0, 0, 0, i))
    gshape = jax.ShapeDtypeStruct((n_tm // 2, 3, each, freqs), f32)
    kept, sent, pieces = pl.pallas_call(
        grads_body,
        grid_spec=pltpu.PrefetchScalarGridSpec(
            num_scalar_prefetch=2,
            grid=(chunks,),
            in_specs=[
                fixed(rows, chans),
                pl.BlockSpec((3, chans, wide), lambda i, *_: (0, 0, i)),
                big,
                big,
                tall(6 * SUB),
            ]
            + [tall(3 * SUB)] * n_tm,
            out_specs=[gspec, gspec, fixed(n_freq, rows // n_freq, chans)],
            scratch_shapes=[
                pltpu.VMEM((2 * chans, rows), bf16),
                pltpu.VMEM((n_tm, 3 * SUB, wide), f32),
                pltpu.VMEM((rows, wide), f32),
                pltpu.VMEM((rows, 3 * wide), bf16),
                pltpu.VMEM((rows, 3 * wide), bf16),
                pltpu.VMEM((2 * chans, 3 * wide), bf16),
                pltpu.VMEM((n_tm, each, wide), f32),
                pltpu.VMEM((rows, chans), f32),
                pltpu.VMEM((rows, chans), f32),
            ],
        ),
        out_shape=[gshape, gshape, jax.ShapeDtypeStruct((n_freq, rows // n_freq, chans), f32)],
        compiler_params=params,
        name="grads",
    )(place, groups, x, p, cosines, sines, local, *got)

    mine = kept + swap(sent, "tm", 1)
    total = mine[0]
    for j in range(1, n_tm // 2):
        total = total + swap(mine[j], "tm", 2 * j)
    grad_projections = jnp.transpose(total, (1, 0, 2))
    result = pieces[0]
    for j in range(1, n_freq):
        result = result + swap(pieces[j], "freq", j)
    grad_increments = result.reshape(steps // n_freq, batch, chans)
    return (grad_increments, grad_projections)


def solution(mesh):
    placed = (P("tm", None, None), P(None, None, "freq"), P(None, "freq"), P())
    return jax.shard_map(
        on_device,
        mesh=mesh,
        in_specs=placed,
        out_specs=(P(("tm", "freq"), None, None), P("tm", None, "freq")),
        check_vma=False,
    )
```

```python
import math

import jax
import jax.numpy as jnp
from jax import lax
from jax.experimental import pallas as pl
from jax.experimental.pallas import tpu as pltpu
from jax.sharding import PartitionSpec as P

f32, bf16 = jnp.float32, jnp.bfloat16
SUB = 8
HALF = SUB // 2
WIDE = 256
MAGIC = 12582912.0
SIN = (3.141582022150658, -5.167142796368909, 2.541899027590427, -0.5546361970970186)
COS = (
    0.9999999534666683,
    -4.934792858675264,
    4.058411914167107,
    -1.3318801612488937,
    0.2196967986036905,
)
NT = (((1,), (1,)), ((), ()))


def horner(z, coefs):
    acc = z * coefs[-1] + coefs[-2]
    for coef in coefs[-3::-1]:
        acc = acc * z + coef
    return acc


def split(value):
    high = value.astype(bf16)
    return high, (value - high.astype(f32)).astype(bf16)


def pair_rows(low, high):
    top = lax.broadcasted_iota(jnp.int32, low.shape, 0) < HALF
    first = jnp.where(top, low, pltpu.roll(high, HALF, 0))
    second = jnp.where(top, pltpu.roll(low, HALF, 0), high)
    return first, second


def tile(i, count=1):
    return pl.ds(pl.multiple_of(i * (count * SUB), count * SUB), count * SUB)


def by_core(core, own, sibling, body):
    @pl.when(core == 0)
    def _():
        body(own, sibling)

    @pl.when(core == 1)
    def _():
        body(sibling, own)


def waves_kernel(amplitude, wide, place_ref, x_hbm, y_ref, p_hbm, ph_hbm, *rest):
    c_ref, s_ref, loc_ref, snd_ref, xt_ref, w_ref = rest[:6]
    xs_ref, ang_ref, flat_ref, x_ref, p_ref, ph_ref, sems = rest[6:]
    rows, chans = flat_ref.shape
    core = place_ref[0] & 1
    chunks = c_ref.shape[0]

    def columns(chunk):
        return pl.ds(pl.multiple_of((core * chunks + chunk) * wide, wide), wide)

    fetch_x = pltpu.make_async_copy(x_hbm, x_ref, sems.at[0])
    fetch_ph = pltpu.make_async_copy(ph_hbm, ph_ref, sems.at[1])
    fetch_p = [
        pltpu.make_async_copy(p_hbm.at[:, :, columns(k)], p_ref.at[k], sems.at[2 + k])
        for k in range(chunks)
    ]
    for copy in [fetch_x, fetch_ph] + fetch_p:
        copy.start()
    inv = 1.0 / (2.0 * math.pi)
    root = math.sqrt(2.0 * amplitude)
    sin_coefs = [root * coef for coef in SIN]
    cos_coefs = [-root * coef for coef in COS]

    lane = lax.broadcasted_iota(jnp.int32, (2 * SUB, chans), 1)
    ones = jnp.where(lane < 3, 1.0, 0.0).astype(bf16)

    def pairs(even_ref, odd_ref):
        def one(k, _):
            first, second = pair_rows(even_ref[tile(k), :], odd_ref[tile(k), :])
            both = jnp.concatenate([first, second], axis=0)
            flat_ref[tile(k, 2), :] = both
            high, low = split(both)
            xs_ref[tile(k, 2), :] = jnp.concatenate([high, low, high, ones], axis=1)
            return 0

        lax.fori_loop(0, rows // (2 * SUB), one, 0, unroll=4)

    fetch_x.wait()
    by_core(core, x_ref, y_ref, pairs)
    high, low = split(flat_ref[...].T)
    xt_ref[:chans, :] = high
    xt_ref[chans:, :] = low
    fetch_ph.wait()

    zero = jnp.zeros((SUB, wide), f32)
    row = lax.broadcasted_iota(jnp.int32, (chans, wide), 0)
    for chunk in range(chunks):
        fetch_p[chunk].wait()
        for level in range(3):
            high, low = split(p_ref[chunk, level])
            w_ref[chunk, :chans, level * wide : (level + 1) * wide] = high
            w_ref[chunk, chans:, level * wide : (level + 1) * wide] = low
            high, low = split(p_ref[chunk, level] * inv)
            phase = ph_ref[level : level + 1, columns(chunk)] * inv
            phase0 = phase.astype(bf16).astype(f32)
            phase1 = (phase - phase0).astype(bf16).astype(f32)
            phase2 = phase - phase0 - phase1
            extra = jnp.where(row == 0, phase0, jnp.where(row == 1, phase1, phase2))
            extra = jnp.where(row < 3, extra, 0.0).astype(bf16)
            stacked = jnp.concatenate([high, high, low, extra], axis=0)
            ang_ref[level] = jnp.dot(xs_ref[...], stacked, preferred_element_type=f32)

        def step(i, carry):
            s0, s1, s2, s01, s12, s012 = carry
            cosines = []
            for level in range(3):
                turn = ang_ref[level, tile(i), :]
                r = turn - ((turn + MAGIC) - MAGIC)
                z = r * r
                sine = r * horner(z, sin_coefs)
                cosine = horner(z, cos_coefs)
                wave = amplitude - sine * sine
                c_ref[chunk, level, tile(i), :] = wave
                s_ref[chunk, level, tile(i), :] = sine * cosine
                cosines.append(wave)
            c0, c1, c2 = cosines
            s012 = s012 + s01 * c2
            s12 = s12 + s1 * c2
            s01 = s01 + s0 * c1
            return (s0 + c0, s1 + c1, s2 + c2, s01, s12, s012)

        sums = lax.fori_loop(0, rows // SUB, step, (zero,) * 6, unroll=4)
        for k in range(6):
            loc_ref[chunk, SUB * k : SUB * (k + 1), :] = sums[k]
        a0, a1, a2, a01, a12, a012 = [v[:HALF] for v in sums]
        b0, b1, b2, b01, b12, b012 = [v[HALF:] for v in sums]
        both = (
            a0 + b0,
            a1 + b1,
            a2 + b2,
            a01 + b01 + a0 * b1,
            a12 + b12 + a1 * b2,
            a012 + b012 + a0 * b12 + a01 * b2,
        )
        for k in range(6):
            snd_ref[chunk, HALF * k : HALF * (k + 1), :] = both[k]


def grads_kernel(sizes, place_ref, c_ref, s_ref, loc_ref, xt_ref, w_ref, *refs):
    n_tm, n_freq, batch, wide = sizes
    chips = n_tm // 2
    got = refs[:chips]
    gp_ref, gk_ref, gs_ref = refs[chips : chips + 3]
    all_ref, u1_ref, sh_ref, sl_ref, acc_ref, flat_ref = refs[chips + 3 :]
    rows, chans = acc_ref.shape
    core, chip, z = place_ref[0] & 1, place_ref[0] >> 1, place_ref[1]
    chunks = c_ref.shape[0]
    each = chans // n_tm

    for d in range(chips):
        all_ref[jnp.bitwise_xor(chip, d)] = got[d][...]

    row = lax.broadcasted_iota(jnp.int32, (HALF, wide), 0)
    zero = jnp.zeros((HALF, wide), f32)
    weight = zero
    for b in range(batch):
        value = jnp.where(place_ref[2 + b] == 1, 2.0 / batch, -2.0 / batch)
        weight = jnp.where(row == b, value, weight)

    def tall(first, second):
        return jnp.concatenate([first, second], axis=0)

    for chunk in range(chunks):

        def sums_of(j):
            return [all_ref[j, chunk, HALF * k : HALF * (k + 1), :] for k in range(6)]

        def forward(j, carry):
            p0, p01, p012 = carry
            b0, b1, b2, b01, b12, b012 = sums_of(j)
            p012 = p012 + b012 + p0 * b12 + p01 * b2
            p01 = p01 + b01 + p0 * b1
            return (p0 + b0, p01, p012)

        def backward(step, carry):
            t1, t2, t12 = carry
            b0, b1, b2, b01, b12, b012 = sums_of(chips - 1 - step)
            t12 = t12 + b12 + b1 * t2
            return (t1 + b1, t2 + b2, t12)

        entry = lax.fori_loop(0, chip, forward, (zero,) * 3)
        e1, e2 = entry[:2]
        totals = lax.fori_loop(chip, chips, forward, entry)
        t1, t2, t12 = lax.fori_loop(0, chips - 1 - chip, backward, (zero,) * 3)
        seeds = [2.0 * weight * jnp.sum(weight * total, axis=0, keepdims=True) for total in totals]

        def local(k):
            value = loc_ref[chunk, SUB * k : SUB * (k + 1), :]
            return value[:HALF], value[HALF:]

        a0, _ = local(0)
        a1, b1 = local(1)
        _, b2 = local(2)
        a01, _ = local(3)
        _, b12 = local(4)
        front1 = tall(e1, e1 + a0)
        front2 = tall(e2, e2 + a01 + e1 * a1)
        tail2 = tall(t2 + b2, t2)
        tail1 = tall(t1 + b1, t1)
        tail12 = tall(t12 + b12 + b1 * t2, t12)
        d0, d1, d2 = [tall(seed, seed) for seed in seeds]
        adjoint1 = d1 + d2 * tail2
        adjoint0 = d0 + d1 * tail1 + d2 * tail12

        def fwd(pair, carry):
            f1, f2 = carry
            slopes = []
            for which in range(2):
                at = tile(2 * pair + which)
                u1_ref[at, :] = s_ref[chunk, 1, at, :] * f1
                slopes.append(s_ref[chunk, 2, at, :] * (d2 * f2))
                f2 = f2 + f1 * c_ref[chunk, 1, at, :]
                f1 = f1 + c_ref[chunk, 0, at, :]
            high, low = split(jnp.concatenate(slopes, axis=0))
            sh_ref[tile(pair, 2), 2 * wide :] = high
            sl_ref[tile(pair, 2), 2 * wide :] = low
            return f1, f2

        lax.fori_loop(0, rows // (2 * SUB), fwd, (front1, front2), unroll=2)

        def bwd(step, carry):
            g1, g0 = carry
            pair = rows // (2 * SUB) - 1 - step
            slope0, slope1 = [], []
            for which in (1, 0):
                at = tile(2 * pair + which)
                slope1.append(u1_ref[at, :] * g1)
                slope0.append(s_ref[chunk, 0, at, :] * g0)
                g0 = g0 + g1 * c_ref[chunk, 1, at, :]
                g1 = g1 + d2 * c_ref[chunk, 2, at, :]
            for level, slopes in enumerate((slope0, slope1)):
                high, low = split(jnp.concatenate(slopes[::-1], axis=0))
                sh_ref[tile(pair, 2), level * wide : (level + 1) * wide] = high
                sl_ref[tile(pair, 2), level * wide : (level + 1) * wide] = low
            return g1, g0

        lax.fori_loop(0, rows // (2 * SUB), bwd, (adjoint1, adjoint0), unroll=2)

        for level in range(3):
            cols = slice(level * wide, (level + 1) * wide)
            main = jnp.dot(xt_ref[...], sh_ref[:, cols], preferred_element_type=f32)
            rest = jnp.dot(xt_ref[:chans, :], sl_ref[:, cols], preferred_element_type=f32)
            grad = main[:chans] + main[chans:] + rest
            for d in range(n_tm):
                gp_ref[d, level, :, chunk * wide : (chunk + 1) * wide] = grad[each * d : each * (d + 1)]

        main = lax.dot_general(sh_ref[...], w_ref[chunk], NT, preferred_element_type=f32)
        rest = lax.dot_general(sl_ref[...], w_ref[chunk, :chans, :], NT, preferred_element_type=f32)
        total = main[:, :chans] + main[:, chans:] + rest
        if chunk == 0:
            acc_ref[...] = total
        else:
            acc_ref[...] += total

    def one(k, _):
        even, odd = pair_rows(acc_ref[tile(2 * k), :], acc_ref[tile(2 * k + 1), :])
        flat_ref[0, tile(k), :] = even
        flat_ref[1, tile(k), :] = odd
        return 0

    lax.fori_loop(0, rows // (2 * SUB), one, 0, unroll=4)
    piece = rows // 2 // n_freq
    for j in range(n_freq):
        at = pl.ds(pl.multiple_of(jnp.bitwise_xor(z, j) * piece, piece), piece)
        gk_ref[j] = flat_ref[core, at, :]
        gs_ref[j] = flat_ref[1 - core, at, :]


def swap(value, axis, distance):
    count = lax.axis_size(axis)
    return lax.ppermute(value, axis, [(i, i ^ distance) for i in range(count)])


def resident(value):
    return pltpu.with_memory_space_constraint(value, pltpu.HBM)


def on_device(increments, projections, phases, groups):
    steps, batch, chans = increments.shape
    freqs = phases.shape[1]
    n_tm, n_freq = lax.axis_size("tm"), lax.axis_size("freq")
    amplitude = math.sqrt(2.0 / (steps * n_tm))
    rows = 2 * steps * batch
    mine = freqs // 2
    wide = min(WIDE, mine)
    chunks = mine // wide
    each = chans // n_tm
    x = increments.reshape(rows // 2, chans)
    p = jnp.transpose(projections, (1, 0, 2))
    here = jnp.stack([lax.axis_index("tm"), lax.axis_index("freq")]).astype(jnp.int32)
    place = jnp.concatenate([here, groups])
    params = pltpu.CompilerParams(vmem_limit_bytes=32 * 1024 * 1024)
    scalars = pl.BlockSpec(memory_space=pltpu.SMEM)
    vectors = pl.BlockSpec(memory_space=pltpu.VMEM)

    def waves_body(*refs):
        waves_kernel(amplitude, wide, *refs)

    y = swap(x, "tm", 1)
    stay = pl.BlockSpec(memory_space=pltpu.HBM)
    cosines, sines, local, own, xt, weights = pl.pallas_call(
        waves_body,
        in_specs=[scalars, stay, vectors, stay, stay],
        out_specs=[vectors] * 6,
        out_shape=[
            pltpu.VMEM((chunks, 3, rows, wide), f32),
            pltpu.VMEM((chunks, 3, rows, wide), f32),
            pltpu.VMEM((chunks, 6 * SUB, wide), f32),
            jax.ShapeDtypeStruct((chunks, 3 * SUB, wide), f32),
            pltpu.VMEM((2 * chans, rows), bf16),
            pltpu.VMEM((chunks, 2 * chans, 3 * wide), bf16),
        ],
        scratch_shapes=[
            pltpu.VMEM((rows, 4 * chans), bf16),
            pltpu.VMEM((3, rows, wide), f32),
            pltpu.VMEM((rows, chans), f32),
            pltpu.VMEM((rows // 2, chans), f32),
            pltpu.VMEM((chunks, 3, chans, wide), f32),
            pltpu.VMEM((3, freqs), f32),
            pltpu.SemaphoreType.DMA((2 + chunks,)),
        ],
        compiler_params=params,
        name="waves",
    )(place, resident(x), y, resident(p), resident(phases))

    got = [own] + [swap(own, "tm", 2 * d) for d in range(1, n_tm // 2)]

    def grads_body(*refs):
        grads_kernel((n_tm, n_freq, batch, wide), *refs)

    gshape = jax.ShapeDtypeStruct((n_freq, rows // 2 // n_freq, chans), f32)
    parts, kept, sent = pl.pallas_call(
        grads_body,
        in_specs=[scalars] + [vectors] * (5 + n_tm // 2),
        out_specs=[vectors] * 3,
        out_shape=[jax.ShapeDtypeStruct((n_tm, 3, each, mine), f32), gshape, gshape],
        scratch_shapes=[
            pltpu.VMEM((n_tm // 2, chunks, 3 * SUB, wide), f32),
            pltpu.VMEM((rows, wide), f32),
            pltpu.VMEM((rows, 3 * wide), bf16),
            pltpu.VMEM((rows, 3 * wide), bf16),
            pltpu.VMEM((rows, chans), f32),
            pltpu.VMEM((2, rows // 2, chans), f32),
        ],
        compiler_params=params,
        name="grads",
    )(place, cosines, sines, local, xt, weights, *got)

    pieces = kept + swap(sent, "tm", 1)
    result = pieces[0]
    for j in range(1, n_freq):
        result = result + swap(pieces[j], "freq", j)
    grad_increments = result.reshape(steps // n_freq, batch, chans)
    parts = lax.all_to_all(parts, "tm", 0, 0, tiled=True)
    total = jnp.sum(parts.reshape(n_tm // 2, 2, 3, each, mine), axis=0)
    grad_projections = jnp.transpose(total, (2, 1, 0, 3)).reshape(each, 3, freqs)
    return (grad_increments, grad_projections)


def solution(mesh):
    placed = (P("tm", None, None), P(None, None, "freq"), P(None, "freq"), P())
    return jax.shard_map(
        on_device,
        mesh=mesh,
        in_specs=placed,
        out_specs=(P(("tm", "freq"), None, None), P("tm", None, "freq")),
        check_vma=False,
    )
```

```python
import math

import jax
import jax.numpy as jnp
from jax import lax
from jax.experimental import pallas as pl
from jax.experimental.pallas import tpu as pltpu
from jax.sharding import PartitionSpec as P

f32, bf16 = jnp.float32, jnp.bfloat16
SUB = 8
HALF = SUB // 2
WIDE = 256
MAGIC = 12582912.0
SIN = (3.141582022150658, -5.167142796368909, 2.541899027590427, -0.5546361970970186)
COS = (
    0.9999999534666683,
    -4.934792858675264,
    4.058411914167107,
    -1.3318801612488937,
    0.2196967986036905,
)
NT = (((1,), (1,)), ((), ()))
PARAMS = pltpu.CompilerParams(vmem_limit_bytes=24 * 1024 * 1024)
SCALARS = pl.BlockSpec(memory_space=pltpu.SMEM)
VECTORS = pl.BlockSpec(memory_space=pltpu.VMEM)
STAY = pl.BlockSpec(memory_space=pltpu.HBM)


def horner(z, coefs):
    acc = z * coefs[-1] + coefs[-2]
    for coef in coefs[-3::-1]:
        acc = acc * z + coef
    return acc


def split(value):
    high = value.astype(bf16)
    return high, (value - high.astype(f32)).astype(bf16)


def pair_rows(low, high):
    top = lax.broadcasted_iota(jnp.int32, low.shape, 0) < HALF
    first = jnp.where(top, low, pltpu.roll(high, HALF, 0))
    second = jnp.where(top, pltpu.roll(low, HALF, 0), high)
    return first, second


def tile(i, count=1):
    return pl.ds(pl.multiple_of(i * (count * SUB), count * SUB), count * SUB)


def tall(first, second):
    return jnp.concatenate([first, second], axis=0)


def call(body, name, ins, outs, scratch, *operands):
    return pl.pallas_call(
        body,
        in_specs=ins,
        out_specs=[VECTORS] * len(outs),
        out_shape=outs,
        scratch_shapes=scratch,
        compiler_params=PARAMS,
        name=name,
    )(*operands)


def prepare_kernel(place_ref, x_hbm, p_hbm, ph_hbm, x_ref, w_ref, r_ref, p_ref, ph_ref, sems):
    chunks, _, chans, wide = p_ref.shape
    core = place_ref[0] & 1
    inv = 1.0 / (2.0 * math.pi)

    def columns(chunk):
        return pl.ds(pl.multiple_of((core * chunks + chunk) * wide, wide), wide)

    fetch = [pltpu.make_async_copy(ph_hbm, ph_ref, sems.at[0])]
    for k in range(chunks):
        fetch.append(
            pltpu.make_async_copy(p_hbm.at[:, :, columns(k)], p_ref.at[k], sems.at[1 + k])
        )
    fetch_x = pltpu.make_async_copy(x_hbm, x_ref, sems.at[1 + chunks])
    for copy in fetch + [fetch_x]:
        copy.start()
    fetch[0].wait()
    row = lax.broadcasted_iota(jnp.int32, (chans, wide), 0)
    for chunk in range(chunks):
        fetch[1 + chunk].wait()
        for level in range(3):
            high, low = split(p_ref[chunk, level])
            w_ref[chunk, :chans, level * wide : (level + 1) * wide] = high
            w_ref[chunk, chans:, level * wide : (level + 1) * wide] = low
            high, low = split(p_ref[chunk, level] * inv)
            phase = ph_ref[level : level + 1, columns(chunk)] * inv
            phase0 = phase.astype(bf16).astype(f32)
            phase1 = (phase - phase0).astype(bf16).astype(f32)
            phase2 = phase - phase0 - phase1
            extra = jnp.where(row == 0, phase0, jnp.where(row == 1, phase1, phase2))
            extra = jnp.where(row < 3, extra, 0.0).astype(bf16)
            for k, part in enumerate((high, high, low, extra)):
                r_ref[chunk, level, chans * k : chans * (k + 1), :] = part
    fetch_x.wait()


def pairs_kernel(place_ref, x_ref, y_ref, xs_ref, xt_ref, flat_ref):
    rows, chans = flat_ref.shape
    core = place_ref[0] & 1
    lane = lax.broadcasted_iota(jnp.int32, (2 * SUB, chans), 1)
    ones = jnp.where(lane < 3, 1.0, 0.0).astype(bf16)

    def pairs(even_ref, odd_ref):
        def one(k, _):
            both = tall(*pair_rows(even_ref[tile(k), :], odd_ref[tile(k), :]))
            flat_ref[tile(k, 2), :] = both
            high, low = split(both)
            xs_ref[tile(k, 2), :] = jnp.concatenate([high, low, high, ones], axis=1)
            return 0

        lax.fori_loop(0, rows // (2 * SUB), one, 0, unroll=4)

    @pl.when(core == 0)
    def _():
        pairs(x_ref, y_ref)

    @pl.when(core == 1)
    def _():
        pairs(y_ref, x_ref)

    high, low = split(flat_ref[...].T)
    xt_ref[:chans, :] = high
    xt_ref[chans:, :] = low


def waves_kernel(amplitude, chunk, xs_ref, r_ref, c_ref, s_ref, loc_ref, snd_ref, ang_ref):
    _, rows, wide = ang_ref.shape
    root = math.sqrt(2.0 * amplitude)
    sin_coefs = [root * coef for coef in SIN]
    cos_coefs = [-root * coef for coef in COS]
    for level in range(3):
        ang_ref[level] = jnp.dot(xs_ref[...], r_ref[chunk, level], preferred_element_type=f32)

    def step(i, carry):
        s0, s1, s2, s01, s12, s012 = carry
        cosines = []
        for level in range(3):
            turn = ang_ref[level, tile(i), :]
            r = turn - ((turn + MAGIC) - MAGIC)
            z = r * r
            sine = r * horner(z, sin_coefs)
            cosine = horner(z, cos_coefs)
            wave = amplitude - sine * sine
            c_ref[level, tile(i), :] = wave
            s_ref[level, tile(i), :] = sine * cosine
            cosines.append(wave)
        c0, c1, c2 = cosines
        s012 = s012 + s01 * c2
        s12 = s12 + s1 * c2
        s01 = s01 + s0 * c1
        return (s0 + c0, s1 + c1, s2 + c2, s01, s12, s012)

    zero = jnp.zeros((SUB, wide), f32)
    sums = lax.fori_loop(0, rows // SUB, step, (zero,) * 6, unroll=4)
    for k in range(6):
        loc_ref[SUB * k : SUB * (k + 1), :] = sums[k]
    a0, a1, a2, a01, a12, a012 = [v[:HALF] for v in sums]
    b0, b1, b2, b01, b12, b012 = [v[HALF:] for v in sums]
    both = (
        a0 + b0,
        a1 + b1,
        a2 + b2,
        a01 + b01 + a0 * b1,
        a12 + b12 + a1 * b2,
        a012 + b012 + a0 * b12 + a01 * b2,
    )
    for k in range(6):
        snd_ref[HALF * k : HALF * (k + 1), :] = both[k]


def frequency_grads(xt_ref, sh_ref, sl_ref, gp_ref):
    count, _, each, wide = gp_ref.shape
    chans = count * each
    for level in range(3):
        cols = slice(level * wide, (level + 1) * wide)
        main = jnp.dot(xt_ref[...], sh_ref[:, cols], preferred_element_type=f32)
        rest = jnp.dot(xt_ref[:chans, :], sl_ref[:, cols], preferred_element_type=f32)
        grad = main[:chans] + main[chans:] + rest
        for d in range(count):
            gp_ref[d, level] = grad[each * d : each * (d + 1)]


def increment_grads(w_ref, sh_ref, sl_ref):
    chans = w_ref.shape[0] // 2
    main = lax.dot_general(sh_ref[...], w_ref[...], NT, preferred_element_type=f32)
    rest = lax.dot_general(sl_ref[...], w_ref[:chans, :], NT, preferred_element_type=f32)
    return main[:, :chans] + main[:, chans:] + rest


def slopes_kernel(sizes, chunk, place_ref, c_ref, s_ref, loc_ref, xt_ref, w_all_ref, *refs):
    n_tm, n_freq, batch, chunks = sizes
    chips = n_tm // 2
    got, refs = refs[:chips], refs[chips:]
    first, last = chunk == 0, chunk == chunks - 1
    before_ref = None
    if not first:
        before_ref, refs = refs[0], refs[1:]
    if last:
        gk_ref, gs_ref, sh_ref, sl_ref, all_ref, u1_ref, acc_ref, flat_ref = refs
    else:
        gp_ref, acc_ref, all_ref, u1_ref, sh_ref, sl_ref = refs
    rows, chans = acc_ref.shape
    wide = u1_ref.shape[1]
    w_ref = w_all_ref.at[chunk]
    core, chip = place_ref[0] & 1, place_ref[0] >> 1

    for d in range(chips):
        all_ref[jnp.bitwise_xor(chip, d)] = got[d][...]

    row = lax.broadcasted_iota(jnp.int32, (HALF, wide), 0)
    zero = jnp.zeros((HALF, wide), f32)
    weight = zero
    for b in range(batch):
        value = jnp.where(place_ref[2 + b] == 1, 2.0 / batch, -2.0 / batch)
        weight = jnp.where(row == b, value, weight)

    def sums_of(j):
        return [all_ref[j, HALF * k : HALF * (k + 1), :] for k in range(6)]

    def forward(j, carry):
        p0, p01, p012 = carry
        b0, b1, b2, b01, b12, b012 = sums_of(j)
        p012 = p012 + b012 + p0 * b12 + p01 * b2
        p01 = p01 + b01 + p0 * b1
        return (p0 + b0, p01, p012)

    def backward(step, carry):
        t1, t2, t12 = carry
        b0, b1, b2, b01, b12, b012 = sums_of(chips - 1 - step)
        t12 = t12 + b12 + b1 * t2
        return (t1 + b1, t2 + b2, t12)

    entry = lax.fori_loop(0, chip, forward, (zero,) * 3)
    e1, e2 = entry[:2]
    totals = lax.fori_loop(chip, chips, forward, entry)
    t1, t2, t12 = lax.fori_loop(0, chips - 1 - chip, backward, (zero,) * 3)
    seeds = [2.0 * weight * jnp.sum(weight * total, axis=0, keepdims=True) for total in totals]

    def local(k):
        value = loc_ref[SUB * k : SUB * (k + 1), :]
        return value[:HALF], value[HALF:]

    a0, _ = local(0)
    a1, b1 = local(1)
    _, b2 = local(2)
    a01, _ = local(3)
    _, b12 = local(4)
    front1 = tall(e1, e1 + a0)
    front2 = tall(e2, e2 + a01 + e1 * a1)
    tail2 = tall(t2 + b2, t2)
    tail1 = tall(t1 + b1, t1)
    tail12 = tall(t12 + b12 + b1 * t2, t12)
    d0, d1, d2 = [tall(seed, seed) for seed in seeds]
    adjoint1 = d1 + d2 * tail2
    adjoint0 = d0 + d1 * tail1 + d2 * tail12

    def fwd(pair, carry):
        f1, f2 = carry
        slopes = []
        for which in range(2):
            at = tile(2 * pair + which)
            u1_ref[at, :] = s_ref[1, at, :] * f1
            slopes.append(s_ref[2, at, :] * (d2 * f2))
            f2 = f2 + f1 * c_ref[1, at, :]
            f1 = f1 + c_ref[0, at, :]
        high, low = split(tall(*slopes))
        sh_ref[tile(pair, 2), 2 * wide :] = high
        sl_ref[tile(pair, 2), 2 * wide :] = low
        return f1, f2

    lax.fori_loop(0, rows // (2 * SUB), fwd, (front1, front2), unroll=2)

    def bwd(step, carry):
        g1, g0 = carry
        pair = rows // (2 * SUB) - 1 - step
        slope0, slope1 = [], []
        for which in (1, 0):
            at = tile(2 * pair + which)
            slope1.append(u1_ref[at, :] * g1)
            slope0.append(s_ref[0, at, :] * g0)
            g0 = g0 + g1 * c_ref[1, at, :]
            g1 = g1 + d2 * c_ref[2, at, :]
        for level, slopes in enumerate((slope0, slope1)):
            high, low = split(tall(*slopes[::-1]))
            sh_ref[tile(pair, 2), level * wide : (level + 1) * wide] = high
            sl_ref[tile(pair, 2), level * wide : (level + 1) * wide] = low
        return g1, g0

    lax.fori_loop(0, rows // (2 * SUB), bwd, (adjoint1, adjoint0), unroll=2)

    if not last:
        frequency_grads(xt_ref, sh_ref, sl_ref, gp_ref)
    total = increment_grads(w_ref, sh_ref, sl_ref)
    if not first:
        total = total + before_ref[...]
    acc_ref[...] = total
    if not last:
        return

    def one(k, _):
        even, odd = pair_rows(acc_ref[tile(2 * k), :], acc_ref[tile(2 * k + 1), :])
        flat_ref[0, tile(k), :] = even
        flat_ref[1, tile(k), :] = odd
        return 0

    lax.fori_loop(0, rows // (2 * SUB), one, 0, unroll=4)
    piece = rows // 2 // n_freq
    for j in range(n_freq):
        gk_ref[j] = flat_ref[core, piece * j : piece * (j + 1), :]
        gs_ref[j] = flat_ref[1 - core, piece * j : piece * (j + 1), :]


def swap(value, axis, distance):
    count = lax.axis_size(axis)
    return lax.ppermute(value, axis, [(i, i ^ distance) for i in range(count)])


def resident(value):
    return pltpu.with_memory_space_constraint(value, pltpu.HBM)


def on_device(increments, projections, phases, groups):
    steps, batch, chans = increments.shape
    freqs = phases.shape[1]
    n_tm, n_freq = lax.axis_size("tm"), lax.axis_size("freq")
    amplitude = math.sqrt(2.0 / (steps * n_tm))
    rows = 2 * steps * batch
    mine = freqs // 2
    wide = min(WIDE, mine)
    chunks = mine // wide
    each = chans // n_tm
    chips = n_tm // 2
    x = increments.reshape(rows // 2, chans)
    p = jnp.transpose(projections, (1, 0, 2))
    here = jnp.stack([lax.axis_index("tm"), lax.axis_index("freq")]).astype(jnp.int32)
    place = jnp.concatenate([here, groups])

    y = swap(x, "tm", 1)
    x, weights, turns = call(
        prepare_kernel,
        "prepare",
        [SCALARS] + [STAY] * 3,
        [
            pltpu.VMEM((rows // 2, chans), f32),
            pltpu.VMEM((chunks, 2 * chans, 3 * wide), bf16),
            pltpu.VMEM((chunks, 3, 4 * chans, wide), bf16),
        ],
        [
            pltpu.VMEM((chunks, 3, chans, wide), f32),
            pltpu.VMEM((3, freqs), f32),
            pltpu.SemaphoreType.DMA((2 + chunks,)),
        ],
        place,
        resident(x),
        resident(p),
        resident(phases),
    )
    xs, xt = call(
        pairs_kernel,
        "pairs",
        [SCALARS] + [VECTORS] * 2,
        [pltpu.VMEM((rows, 4 * chans), bf16), pltpu.VMEM((2 * chans, rows), bf16)],
        [pltpu.VMEM((rows, chans), f32)],
        place,
        x,
        y,
    )

    waves, got = [], []
    for chunk in range(chunks):

        def waves_body(*refs, chunk=chunk):
            waves_kernel(amplitude, chunk, *refs)

        *keep, own = call(
            waves_body,
            f"waves{chunk}",
            [VECTORS] * 2,
            [
                pltpu.VMEM((3, rows, wide), f32),
                pltpu.VMEM((3, rows, wide), f32),
                pltpu.VMEM((6 * SUB, wide), f32),
                jax.ShapeDtypeStruct((3 * SUB, wide), f32),
            ],
            [pltpu.VMEM((3, rows, wide), f32)],
            xs,
            turns,
        )
        waves.append(keep)
        got.append([own] + [swap(own, "tm", 2 * d) for d in range(1, chips)])

    parts = []
    before = []
    pshape = jax.ShapeDtypeStruct((n_tm, 3, each, wide), f32)
    gshape = jax.ShapeDtypeStruct((n_freq, rows // 2 // n_freq, chans), f32)
    slopes = [pltpu.VMEM((rows, 3 * wide), bf16)] * 2
    scratch = [pltpu.VMEM((chips, 3 * SUB, wide), f32), pltpu.VMEM((rows, wide), f32)]
    total = pltpu.VMEM((rows, chans), f32)
    for chunk in range(chunks):
        last = chunk == chunks - 1

        def slopes_body(*refs, chunk=chunk):
            slopes_kernel((n_tm, n_freq, batch, chunks), chunk, *refs)

        operands = [place, *waves[chunk], xt, weights, *got[chunk], *before]
        outs = call(
            slopes_body,
            f"slopes{chunk}",
            [SCALARS] + [VECTORS] * (len(operands) - 1),
            [gshape, gshape] + slopes if last else [pshape, total],
            scratch + ([total, pltpu.VMEM((2, rows // 2, chans), f32)] if last else slopes),
            *operands,
        )
        if last:
            kept, sent, high, low = outs
        else:
            parts.append(lax.all_to_all(outs[0], "tm", 0, 0, tiled=True))
            before = [outs[1]]

    other = swap(sent, "tm", 1)
    (final,) = call(frequency_grads, "last", [VECTORS] * 3, [pshape], [], xt, high, low)
    pieces, final = lax.optimization_barrier((kept + other, final))
    pieces = lax.all_to_all(pieces, "freq", 0, 0, tiled=True)
    parts.append(lax.all_to_all(final, "tm", 0, 0, tiled=True))

    grad_increments = jnp.sum(pieces, axis=0).reshape(steps // n_freq, batch, chans)
    sums = [jnp.sum(part.reshape(chips, 2, 3, each, wide), axis=0) for part in parts]
    total = jnp.concatenate(sums, axis=-1)
    grad_projections = jnp.transpose(total, (2, 1, 0, 3)).reshape(each, 3, freqs)
    return (grad_increments, grad_projections)


def solution(mesh):
    placed = (P("tm", None, None), P(None, None, "freq"), P(None, "freq"), P())
    return jax.shard_map(
        on_device,
        mesh=mesh,
        in_specs=placed,
        out_specs=(P(("tm", "freq"), None, None), P("tm", None, "freq")),
        check_vma=False,
    )
```

```python
import math

import jax
import jax.numpy as jnp
from jax import lax
from jax.experimental import pallas as pl
from jax.experimental.pallas import tpu as pltpu
from jax.sharding import PartitionSpec as P

f32, bf16 = jnp.float32, jnp.bfloat16
SUB = 8
HALF = SUB // 2
WIDE = 256
MAGIC = 12582912.0
SIN = (3.141582022150658, -5.167142796368909, 2.541899027590427, -0.5546361970970186)
COS = (
    0.9999999534666683,
    -4.934792858675264,
    4.058411914167107,
    -1.3318801612488937,
    0.2196967986036905,
)
NT = (((1,), (1,)), ((), ()))
PARAMS = pltpu.CompilerParams(vmem_limit_bytes=24 * 1024 * 1024)
VECTORS = pl.BlockSpec(memory_space=pltpu.VMEM)
STAY = pl.BlockSpec(memory_space=pltpu.HBM)


def horner(z, coefs):
    acc = z * coefs[-1] + coefs[-2]
    for coef in coefs[-3::-1]:
        acc = acc * z + coef
    return acc


def split(value):
    high = value.astype(bf16)
    return high, (value - high.astype(f32)).astype(bf16)


def pair_rows(low, high):
    top = lax.broadcasted_iota(jnp.int32, low.shape, 0) < HALF
    first = jnp.where(top, low, pltpu.roll(high, HALF, 0))
    second = jnp.where(top, pltpu.roll(low, HALF, 0), high)
    return first, second


def tile(i, count=1):
    return pl.ds(pl.multiple_of(i * (count * SUB), count * SUB), count * SUB)


def tall(first, second):
    return jnp.concatenate([first, second], axis=0)


def call(body, name, micros, ins, outs, scratch, *operands):
    return pl.pallas_call(
        body,
        in_specs=ins,
        out_specs=[VECTORS] * len(outs),
        out_shape=outs,
        scratch_shapes=scratch,
        compiler_params=PARAMS,
        cost_estimate=pl.CostEstimate(
            flops=int(micros * 1.1e9), bytes_accessed=int(micros * 3e6), transcendentals=0
        ),
        name=name,
    )(*operands)


def prepare_kernel(x_hbm, p_hbm, ph_hbm, g_hbm, x_ref, w_ref, r_ref, weight_ref, *rest):
    p_ref, ph_ref, g_ref, sems = rest
    chunks, _, chans, wide = p_ref.shape
    batch = g_ref.shape[0]
    core = lax.axis_index("tm") & 1
    inv = 1.0 / (2.0 * math.pi)

    def columns(chunk):
        return pl.ds(pl.multiple_of((core * chunks + chunk) * wide, wide), wide)

    fetch = [pltpu.make_async_copy(ph_hbm, ph_ref, sems.at[0])]
    for k in range(chunks):
        fetch.append(
            pltpu.make_async_copy(p_hbm.at[:, :, columns(k)], p_ref.at[k], sems.at[1 + k])
        )
    fetch_x = pltpu.make_async_copy(x_hbm, x_ref, sems.at[1 + chunks])
    fetch_g = pltpu.make_async_copy(g_hbm, g_ref, sems.at[2 + chunks])
    for copy in fetch + [fetch_x, fetch_g]:
        copy.start()
    fetch[0].wait()
    row = lax.broadcasted_iota(jnp.int32, (chans, wide), 0)
    for chunk in range(chunks):
        fetch[1 + chunk].wait()
        for level in range(3):
            cols = slice((3 * chunk + level) * wide, (3 * chunk + level + 1) * wide)
            high, low = split(p_ref[chunk, level])
            w_ref[:chans, cols] = high
            w_ref[chans:, cols] = low
            high, low = split(p_ref[chunk, level] * inv)
            phase = ph_ref[level : level + 1, columns(chunk)] * inv
            phase0 = phase.astype(bf16).astype(f32)
            phase1 = (phase - phase0).astype(bf16).astype(f32)
            phase2 = phase - phase0 - phase1
            extra = jnp.where(row == 0, phase0, jnp.where(row == 1, phase1, phase2))
            extra = jnp.where(row < 3, extra, 0.0).astype(bf16)
            for k, part in enumerate((high, high, low, extra)):
                r_ref[chans * k : chans * (k + 1), cols] = part
    fetch_g.wait()
    row = lax.broadcasted_iota(jnp.int32, weight_ref.shape, 0)
    weight = jnp.zeros(weight_ref.shape, f32)
    for b in range(batch):
        value = jnp.where(g_ref[b] == 1, 2.0 / batch, -2.0 / batch)
        weight = jnp.where(row == b, value, weight)
    weight_ref[...] = weight
    fetch_x.wait()


def turn_kernel(flat_ref, xt_ref):
    chans = flat_ref.shape[1]
    high, low = split(flat_ref[...].T)
    xt_ref[:chans, :] = high
    xt_ref[chans:, :] = low


def waves_kernel(amplitude, wide, x_ref, y_ref, r_ref, *rest):
    c_ref, s_ref, loc_ref, snd_ref, flat_ref, xs_ref, ang_ref = rest
    rows, chans = flat_ref.shape
    chunks = c_ref.shape[0]
    core = lax.axis_index("tm") & 1
    root = math.sqrt(2.0 * amplitude)
    sin_coefs = [root * coef for coef in SIN]
    cos_coefs = [-root * coef for coef in COS]
    lane = lax.broadcasted_iota(jnp.int32, (2 * SUB, chans), 1)
    ones = jnp.where(lane < 3, 1.0, 0.0).astype(bf16)

    def pairs(even_ref, odd_ref):
        def one(k, _):
            both = tall(*pair_rows(even_ref[tile(k), :], odd_ref[tile(k), :]))
            flat_ref[tile(k, 2), :] = both
            high, low = split(both)
            xs_ref[tile(k, 2), :] = jnp.concatenate([high, low, high, ones], axis=1)
            return 0

        lax.fori_loop(0, rows // (2 * SUB), one, 0, unroll=8)

    @pl.when(core == 0)
    def _():
        pairs(x_ref, y_ref)

    @pl.when(core == 1)
    def _():
        pairs(y_ref, x_ref)

    ang_ref[...] = jnp.dot(xs_ref[...], r_ref[...], preferred_element_type=f32)
    zero = jnp.zeros((SUB, wide), f32)
    for chunk in range(chunks):
        here = slice(chunk * wide, (chunk + 1) * wide)

        def step(i, carry):
            s0, s1, s2, s01, s12, s012 = carry
            cosines = []
            for level in range(3):
                at = (3 * chunk + level) * wide
                turn = ang_ref[tile(i), at : at + wide]
                r = turn - ((turn + MAGIC) - MAGIC)
                z = r * r
                sine = r * horner(z, sin_coefs)
                cosine = horner(z, cos_coefs)
                wave = amplitude - sine * sine
                c_ref[chunk, level, tile(i), :] = wave
                s_ref[chunk, level, tile(i), :] = sine * cosine
                cosines.append(wave)
            c0, c1, c2 = cosines
            s012 = s012 + s01 * c2
            s12 = s12 + s1 * c2
            s01 = s01 + s0 * c1
            return (s0 + c0, s1 + c1, s2 + c2, s01, s12, s012)

        sums = lax.fori_loop(0, rows // SUB, step, (zero,) * 6, unroll=16)
        for k in range(6):
            loc_ref[SUB * k : SUB * (k + 1), here] = sums[k]
        a0, a1, a2, a01, a12, a012 = [v[:HALF] for v in sums]
        b0, b1, b2, b01, b12, b012 = [v[HALF:] for v in sums]
        both = (
            a0 + b0,
            a1 + b1,
            a2 + b2,
            a01 + b01 + a0 * b1,
            a12 + b12 + a1 * b2,
            a012 + b012 + a0 * b12 + a01 * b2,
        )
        for k in range(6):
            snd_ref[HALF * k : HALF * (k + 1), here] = both[k]


def grads_kernel(sizes, c_ref, s_ref, loc_ref, xt_ref, w_ref, weight_ref, *refs):
    n_tm, n_freq, wide = sizes
    chips = n_tm // 2
    got, refs = refs[:chips], refs[chips:]
    gp_ref, gk_ref, gs_ref, sh_ref, sl_ref, all_ref, u1_ref, acc_ref, flat_ref = refs
    rows, chans = acc_ref.shape
    chunks = c_ref.shape[0]
    me = lax.axis_index("tm")
    core, chip, z = me & 1, me >> 1, lax.axis_index("freq")

    for d in range(chips):
        all_ref[jnp.bitwise_xor(chip, d)] = got[d][...]

    weight = weight_ref[:HALF]
    zero = jnp.zeros(weight.shape, f32)

    def sums_of(j):
        return [all_ref[j, HALF * k : HALF * (k + 1), :] for k in range(6)]

    def forward(j, carry):
        p0, p01, p012 = carry
        b0, b1, b2, b01, b12, b012 = sums_of(j)
        p012 = p012 + b012 + p0 * b12 + p01 * b2
        p01 = p01 + b01 + p0 * b1
        return (p0 + b0, p01, p012)

    def backward(step, carry):
        t1, t2, t12 = carry
        b0, b1, b2, b01, b12, b012 = sums_of(chips - 1 - step)
        t12 = t12 + b12 + b1 * t2
        return (t1 + b1, t2 + b2, t12)

    entry = lax.fori_loop(0, chip, forward, (zero,) * 3)
    e1, e2 = entry[:2]
    totals = lax.fori_loop(chip, chips, forward, entry)
    t1, t2, t12 = lax.fori_loop(0, chips - 1 - chip, backward, (zero,) * 3)
    seeds = [2.0 * weight * jnp.sum(weight * total, axis=0, keepdims=True) for total in totals]

    def local(k):
        value = loc_ref[SUB * k : SUB * (k + 1), :]
        return value[:HALF], value[HALF:]

    a0, _ = local(0)
    a1, b1 = local(1)
    _, b2 = local(2)
    a01, _ = local(3)
    _, b12 = local(4)
    d0, d1, d2 = [tall(seed, seed) for seed in seeds]
    tail2 = tall(t2 + b2, t2)
    tail1 = tall(t1 + b1, t1)
    tail12 = tall(t12 + b12 + b1 * t2, t12)
    starts = (
        d2,
        tall(e1, e1 + a0),
        tall(e2, e2 + a01 + e1 * a1),
        d1 + d2 * tail2,
        d0 + d1 * tail1 + d2 * tail12,
    )

    for chunk in range(chunks):
        scale, front1, front2, adjoint1, adjoint0 = [
            v[:, chunk * wide : (chunk + 1) * wide] for v in starts
        ]

        def keep(pair, level, slopes):
            high, low = split(tall(*slopes))
            at = (3 * chunk + level) * wide
            sh_ref[tile(pair, 2), at : at + wide] = high
            sl_ref[tile(pair, 2), at : at + wide] = low

        def fwd(pair, carry):
            f1, f2 = carry
            slopes = []
            for which in range(2):
                at = tile(2 * pair + which)
                u1_ref[at, :] = s_ref[chunk, 1, at, :] * f1
                slopes.append(s_ref[chunk, 2, at, :] * (scale * f2))
                f2 = f2 + f1 * c_ref[chunk, 1, at, :]
                f1 = f1 + c_ref[chunk, 0, at, :]
            keep(pair, 2, slopes)
            return f1, f2

        lax.fori_loop(0, rows // (2 * SUB), fwd, (front1, front2), unroll=8)

        def bwd(step, carry):
            g1, g0 = carry
            pair = rows // (2 * SUB) - 1 - step
            slope0, slope1 = [], []
            for which in (1, 0):
                at = tile(2 * pair + which)
                slope1.append(u1_ref[at, :] * g1)
                slope0.append(s_ref[chunk, 0, at, :] * g0)
                g0 = g0 + g1 * c_ref[chunk, 1, at, :]
                g1 = g1 + scale * c_ref[chunk, 2, at, :]
            keep(pair, 0, slope0[::-1])
            keep(pair, 1, slope1[::-1])
            return g1, g0

        lax.fori_loop(0, rows // (2 * SUB), bwd, (adjoint1, adjoint0), unroll=8)

    main = jnp.dot(xt_ref[...], sh_ref[...], preferred_element_type=f32)
    rest = jnp.dot(xt_ref[:chans, :], sl_ref[...], preferred_element_type=f32)
    grad = main[:chans] + main[chans:] + rest
    each = chans // n_tm
    for chunk in range(chunks):
        for level in range(3):
            at = (3 * chunk + level) * wide
            for d in range(n_tm):
                gp_ref[d, level, :, chunk * wide : (chunk + 1) * wide] = grad[
                    each * d : each * (d + 1), at : at + wide
                ]

    main = lax.dot_general(sh_ref[...], w_ref[...], NT, preferred_element_type=f32)
    rest = lax.dot_general(sl_ref[...], w_ref[:chans, :], NT, preferred_element_type=f32)
    acc_ref[...] = main[:, :chans] + main[:, chans:] + rest

    def one(k, _):
        even, odd = pair_rows(acc_ref[tile(2 * k), :], acc_ref[tile(2 * k + 1), :])
        flat_ref[0, tile(k), :] = even
        flat_ref[1, tile(k), :] = odd
        return 0

    lax.fori_loop(0, rows // (2 * SUB), one, 0, unroll=8)
    piece = rows // 2 // n_freq
    for j in range(n_freq):
        at = pl.ds(pl.multiple_of(jnp.bitwise_xor(z, j) * piece, piece), piece)
        gk_ref[j] = flat_ref[core, at, :]
        gs_ref[j] = flat_ref[1 - core, at, :]


def swap(value, axis, distance):
    count = lax.axis_size(axis)
    return lax.ppermute(value, axis, [(i, i ^ distance) for i in range(count)])


def resident(value):
    return pltpu.with_memory_space_constraint(value, pltpu.HBM)


def on_device(increments, projections, phases, groups):
    steps, batch, chans = increments.shape
    freqs = phases.shape[1]
    n_tm, n_freq = lax.axis_size("tm"), lax.axis_size("freq")
    amplitude = math.sqrt(2.0 / (steps * n_tm))
    rows = 2 * steps * batch
    mine = freqs // 2
    wide = min(WIDE, mine)
    chunks = mine // wide
    each = chans // n_tm
    chips = n_tm // 2
    x = increments.reshape(rows // 2, chans)
    p = jnp.transpose(projections, (1, 0, 2))
    y = swap(x, "tm", 1)
    x, weights, turns, weight = call(
        prepare_kernel,
        "prepare",
        1.9,
        [STAY] * 4,
        [
            pltpu.VMEM((rows // 2, chans), f32),
            pltpu.VMEM((2 * chans, 3 * mine), bf16),
            pltpu.VMEM((4 * chans, 3 * mine), bf16),
            pltpu.VMEM((SUB, mine), f32),
        ],
        [
            pltpu.VMEM((chunks, 3, chans, wide), f32),
            pltpu.VMEM((3, freqs), f32),
            pltpu.SMEM((batch,), jnp.int32),
            pltpu.SemaphoreType.DMA((3 + chunks,)),
        ],
        resident(x),
        resident(p),
        resident(phases),
        resident(groups),
    )

    def waves_body(*refs):
        waves_kernel(amplitude, wide, *refs)

    cosines, sines, local, own, flat = call(
        waves_body,
        "waves",
        8.0,
        [VECTORS] * 3,
        [
            pltpu.VMEM((chunks, 3, rows, wide), f32),
            pltpu.VMEM((chunks, 3, rows, wide), f32),
            pltpu.VMEM((6 * SUB, mine), f32),
            jax.ShapeDtypeStruct((3 * SUB, mine), f32),
            pltpu.VMEM((rows, chans), f32),
        ],
        [pltpu.VMEM((rows, 4 * chans), bf16), pltpu.VMEM((rows, 3 * mine), f32)],
        x,
        y,
        turns,
    )
    got = [own] + [swap(own, "tm", 2 * d) for d in range(1, chips)]
    (xt,) = call(
        turn_kernel, "turn", 0.8, [VECTORS], [pltpu.VMEM((2 * chans, rows), bf16)], [], flat
    )

    def grads_body(*refs):
        grads_kernel((n_tm, n_freq, wide), *refs)

    gshape = jax.ShapeDtypeStruct((n_freq, rows // 2 // n_freq, chans), f32)
    parts, kept, sent = call(
        grads_body,
        "grads",
        7.0,
        [VECTORS] * (6 + chips),
        [jax.ShapeDtypeStruct((n_tm, 3, each, mine), f32), gshape, gshape],
        [
            pltpu.VMEM((rows, 3 * mine), bf16),
            pltpu.VMEM((rows, 3 * mine), bf16),
            pltpu.VMEM((chips, 3 * SUB, mine), f32),
            pltpu.VMEM((rows, wide), f32),
            pltpu.VMEM((rows, chans), f32),
            pltpu.VMEM((2, rows // 2, chans), f32),
        ],
        cosines,
        sines,
        local,
        xt,
        weights,
        weight,
        *got,
    )

    pieces = kept + swap(sent, "tm", 1)
    result = pieces[0]
    for j in range(1, n_freq):
        result = result + swap(pieces[j], "freq", j)
    grad_increments = result.reshape(steps // n_freq, batch, chans)
    parts = lax.all_to_all(parts, "tm", 0, 0, tiled=True)
    total = jnp.sum(parts.reshape(chips, 2, 3, each, mine), axis=0)
    grad_projections = jnp.transpose(total, (2, 1, 0, 3)).reshape(each, 3, freqs)
    return (grad_increments, grad_projections)


def solution(mesh):
    placed = (P("tm", None, None), P(None, None, "freq"), P(None, "freq"), P())
    return jax.shard_map(
        on_device,
        mesh=mesh,
        in_specs=placed,
        out_specs=(P(("tm", "freq"), None, None), P("tm", None, "freq")),
        check_vma=False,
    )
```

```python
import math

import jax
import jax.numpy as jnp
from jax import lax
from jax.experimental import pallas as pl
from jax.experimental.pallas import tpu as pltpu
from jax.sharding import PartitionSpec as P

f32, bf16 = jnp.float32, jnp.bfloat16
SUB = 8
HALF = SUB // 2
WIDE = 256
MAGIC = 12582912.0
SIN = (3.141582022150658, -5.167142796368909, 2.541899027590427, -0.5546361970970186)
COS = (
    0.9999999534666683,
    -4.934792858675264,
    4.058411914167107,
    -1.3318801612488937,
    0.2196967986036905,
)
NT = (((1,), (1,)), ((), ()))
PARAMS = pltpu.CompilerParams(vmem_limit_bytes=24 * 1024 * 1024)
VECTORS = pl.BlockSpec(memory_space=pltpu.VMEM)
STAY = pl.BlockSpec(memory_space=pltpu.HBM)


def horner(z, coefs):
    acc = z * coefs[-1] + coefs[-2]
    for coef in coefs[-3::-1]:
        acc = acc * z + coef
    return acc


def split(value):
    high = value.astype(bf16)
    return high, (value - high.astype(f32)).astype(bf16)


def pair_rows(low, high):
    top = lax.broadcasted_iota(jnp.int32, low.shape, 0) < HALF
    first = jnp.where(top, low, pltpu.roll(high, HALF, 0))
    second = jnp.where(top, pltpu.roll(low, HALF, 0), high)
    return first, second


def tile(i, count=1):
    return pl.ds(pl.multiple_of(i * (count * SUB), count * SUB), count * SUB)


def tall(first, second):
    return jnp.concatenate([first, second], axis=0)


def call(body, name, micros, ins, outs, scratch, *operands):
    return pl.pallas_call(
        body,
        in_specs=ins,
        out_specs=[VECTORS] * len(outs),
        out_shape=outs,
        scratch_shapes=scratch,
        compiler_params=PARAMS,
        cost_estimate=pl.CostEstimate(
            flops=int(micros * 1.1e9), bytes_accessed=int(micros * 3e6), transcendentals=0
        ),
        name=name,
    )(*operands)


def prepare_kernel(x_hbm, p_hbm, ph_hbm, g_hbm, x_ref, w_ref, r_ref, weight_ref, *rest):
    p_ref, ph_ref, g_ref, sems = rest
    chunks, _, chans, wide = p_ref.shape
    batch = g_ref.shape[0]
    core = lax.axis_index("tm") & 1
    inv = 1.0 / (2.0 * math.pi)

    def columns(chunk):
        return pl.ds(pl.multiple_of((core * chunks + chunk) * wide, wide), wide)

    fetch = [pltpu.make_async_copy(ph_hbm, ph_ref, sems.at[0])]
    for k in range(chunks):
        fetch.append(
            pltpu.make_async_copy(p_hbm.at[:, :, columns(k)], p_ref.at[k], sems.at[1 + k])
        )
    fetch_x = pltpu.make_async_copy(x_hbm, x_ref, sems.at[1 + chunks])
    fetch_g = pltpu.make_async_copy(g_hbm, g_ref, sems.at[2 + chunks])
    for copy in fetch + [fetch_x, fetch_g]:
        copy.start()
    fetch[0].wait()
    row = lax.broadcasted_iota(jnp.int32, (chans, wide), 0)
    for chunk in range(chunks):
        fetch[1 + chunk].wait()
        for level in range(3):
            cols = slice((3 * chunk + level) * wide, (3 * chunk + level + 1) * wide)
            high, low = split(p_ref[chunk, level])
            w_ref[:chans, cols] = high
            w_ref[chans:, cols] = low
            high, low = split(p_ref[chunk, level] * inv)
            phase = ph_ref[level : level + 1, columns(chunk)] * inv
            phase0 = phase.astype(bf16).astype(f32)
            phase1 = (phase - phase0).astype(bf16).astype(f32)
            phase2 = phase - phase0 - phase1
            extra = jnp.where(row == 0, phase0, jnp.where(row == 1, phase1, phase2))
            extra = jnp.where(row < 3, extra, 0.0).astype(bf16)
            for k, part in enumerate((high, high, low, extra)):
                r_ref[chans * k : chans * (k + 1), cols] = part
    fetch_g.wait()
    row = lax.broadcasted_iota(jnp.int32, weight_ref.shape, 0)
    weight = jnp.zeros(weight_ref.shape, f32)
    for b in range(batch):
        value = jnp.where(g_ref[b] == 1, 2.0 / batch, -2.0 / batch)
        weight = jnp.where(row == b, value, weight)
    weight_ref[...] = weight
    fetch_x.wait()


def turn_kernel(flat_ref, xt_ref):
    chans = flat_ref.shape[1]
    high, low = split(flat_ref[...].T)
    xt_ref[:chans, :] = high
    xt_ref[chans:, :] = low


def waves_kernel(amplitude, wide, x_ref, y_ref, r_ref, *rest):
    c_ref, s_ref, loc_ref, snd_ref, flat_ref, xs_ref, ang_ref = rest
    rows, chans = flat_ref.shape
    chunks = c_ref.shape[0]
    core = lax.axis_index("tm") & 1
    root = math.sqrt(2.0 * amplitude)
    sin_coefs = [root * coef for coef in SIN]
    cos_coefs = [-root * coef for coef in COS]
    lane = lax.broadcasted_iota(jnp.int32, (2 * SUB, chans), 1)
    ones = jnp.where(lane < 3, 1.0, 0.0).astype(bf16)

    def pairs(even_ref, odd_ref):
        def one(k, _):
            both = tall(*pair_rows(even_ref[tile(k), :], odd_ref[tile(k), :]))
            flat_ref[tile(k, 2), :] = both
            high, low = split(both)
            xs_ref[tile(k, 2), :] = jnp.concatenate([high, low, high, ones], axis=1)
            return 0

        lax.fori_loop(0, rows // (2 * SUB), one, 0, unroll=8)

    @pl.when(core == 0)
    def _():
        pairs(x_ref, y_ref)

    @pl.when(core == 1)
    def _():
        pairs(y_ref, x_ref)

    ang_ref[...] = jnp.dot(xs_ref[...], r_ref[...], preferred_element_type=f32)
    zero = jnp.zeros((SUB, wide), f32)
    for chunk in range(chunks):
        here = slice(chunk * wide, (chunk + 1) * wide)

        def step(i, carry):
            s0, s1, s2, s01, s12, s012 = carry
            cosines = []
            for level in range(3):
                at = (3 * chunk + level) * wide
                turn = ang_ref[tile(i), at : at + wide]
                r = turn - ((turn + MAGIC) - MAGIC)
                z = r * r
                sine = r * horner(z, sin_coefs)
                cosine = horner(z, cos_coefs)
                wave = amplitude - sine * sine
                c_ref[chunk, level, tile(i), :] = wave
                s_ref[chunk, level, tile(i), :] = sine * cosine
                cosines.append(wave)
            c0, c1, c2 = cosines
            s012 = s012 + s01 * c2
            s12 = s12 + s1 * c2
            s01 = s01 + s0 * c1
            return (s0 + c0, s1 + c1, s2 + c2, s01, s12, s012)

        sums = lax.fori_loop(0, rows // SUB, step, (zero,) * 6, unroll=16)
        for k in range(6):
            loc_ref[SUB * k : SUB * (k + 1), here] = sums[k]
        a0, a1, a2, a01, a12, a012 = [v[:HALF] for v in sums]
        b0, b1, b2, b01, b12, b012 = [v[HALF:] for v in sums]
        both = (
            a0 + b0,
            a1 + b1,
            a2 + b2,
            a01 + b01 + a0 * b1,
            a12 + b12 + a1 * b2,
            a012 + b012 + a0 * b12 + a01 * b2,
        )
        for k in range(6):
            snd_ref[HALF * k : HALF * (k + 1), here] = both[k]


def compose(chips, loc_ref, weight_ref, got, all_ref):
    chip = lax.axis_index("tm") >> 1
    for d in range(chips):
        all_ref[jnp.bitwise_xor(chip, d)] = got[d][...]

    weight = weight_ref[:HALF]
    zero = jnp.zeros(weight.shape, f32)

    def sums_of(j):
        return [all_ref[j, HALF * k : HALF * (k + 1), :] for k in range(6)]

    def forward(j, carry):
        p0, p01, p012 = carry
        b0, b1, b2, b01, b12, b012 = sums_of(j)
        p012 = p012 + b012 + p0 * b12 + p01 * b2
        p01 = p01 + b01 + p0 * b1
        return (p0 + b0, p01, p012)

    def backward(step, carry):
        t1, t2, t12 = carry
        b0, b1, b2, b01, b12, b012 = sums_of(chips - 1 - step)
        t12 = t12 + b12 + b1 * t2
        return (t1 + b1, t2 + b2, t12)

    entry = lax.fori_loop(0, chip, forward, (zero,) * 3)
    e1, e2 = entry[:2]
    totals = lax.fori_loop(chip, chips, forward, entry)
    t1, t2, t12 = lax.fori_loop(0, chips - 1 - chip, backward, (zero,) * 3)
    seeds = [2.0 * weight * jnp.sum(weight * total, axis=0, keepdims=True) for total in totals]

    def local(k):
        value = loc_ref[SUB * k : SUB * (k + 1), :]
        return value[:HALF], value[HALF:]

    a0, _ = local(0)
    a1, b1 = local(1)
    _, b2 = local(2)
    a01, _ = local(3)
    _, b12 = local(4)
    d0, d1, d2 = [tall(seed, seed) for seed in seeds]
    tail2 = tall(t2 + b2, t2)
    tail1 = tall(t1 + b1, t1)
    tail12 = tall(t12 + b12 + b1 * t2, t12)
    return (
        d2,
        tall(e1, e1 + a0),
        tall(e2, e2 + a01 + e1 * a1),
        d1 + d2 * tail2,
        d0 + d1 * tail1 + d2 * tail12,
    )


def slopes(chunk, wide, starts_ref, c_ref, s_ref, u1_ref, sh_ref, sl_ref):
    rows = u1_ref.shape[0]
    scale, front1, front2, adjoint1, adjoint0 = [
        starts_ref[SUB * k : SUB * (k + 1), chunk * wide : (chunk + 1) * wide] for k in range(5)
    ]

    def keep(pair, level, values):
        high, low = split(tall(*values))
        sh_ref[tile(pair, 2), level * wide : (level + 1) * wide] = high
        sl_ref[tile(pair, 2), level * wide : (level + 1) * wide] = low

    def fwd(pair, carry):
        f1, f2 = carry
        slope2 = []
        for which in range(2):
            at = tile(2 * pair + which)
            u1_ref[at, :] = s_ref[chunk, 1, at, :] * f1
            slope2.append(s_ref[chunk, 2, at, :] * (scale * f2))
            f2 = f2 + f1 * c_ref[chunk, 1, at, :]
            f1 = f1 + c_ref[chunk, 0, at, :]
        keep(pair, 2, slope2)
        return f1, f2

    lax.fori_loop(0, rows // (2 * SUB), fwd, (front1, front2), unroll=8)

    def bwd(step, carry):
        g1, g0 = carry
        pair = rows // (2 * SUB) - 1 - step
        slope0, slope1 = [], []
        for which in (1, 0):
            at = tile(2 * pair + which)
            slope1.append(u1_ref[at, :] * g1)
            slope0.append(s_ref[chunk, 0, at, :] * g0)
            g0 = g0 + g1 * c_ref[chunk, 1, at, :]
            g1 = g1 + scale * c_ref[chunk, 2, at, :]
        keep(pair, 0, slope0[::-1])
        keep(pair, 1, slope1[::-1])
        return g1, g0

    lax.fori_loop(0, rows // (2 * SUB), bwd, (adjoint1, adjoint0), unroll=8)


def frequency_grads(bit, wide, xt_ref, sh_ref, sl_ref, gp_ref, keep_ref, send_ref):
    n_tm, _, each, _ = gp_ref.shape
    chans = n_tm * each
    main = jnp.dot(xt_ref[...], sh_ref[...], preferred_element_type=f32)
    rest = jnp.dot(xt_ref[:chans, :], sl_ref[...], preferred_element_type=f32)
    grad = main[:chans] + main[chans:] + rest
    for level in range(3):
        for d in range(n_tm):
            gp_ref[d, level] = grad[each * d : each * (d + 1), level * wide : (level + 1) * wide]
    me = lax.axis_index("tm")
    near = [j for j in range(n_tm // 2) if not j & bit]
    for k, j in enumerate(near):
        for core in range(2):
            keep_ref[k, core] = gp_ref[jnp.bitwise_xor(me, 2 * j + core)]
            send_ref[k, core] = gp_ref[jnp.bitwise_xor(me, 2 * (j | bit) + core)]


def increment_grads(w_ref, at, sh_ref, sl_ref):
    chans = w_ref.shape[0] // 2
    cols = slice(at, at + sh_ref.shape[1])
    main = lax.dot_general(sh_ref[...], w_ref[:, cols], NT, preferred_element_type=f32)
    rest = lax.dot_general(sl_ref[...], w_ref[:chans, cols], NT, preferred_element_type=f32)
    return main[:, :chans] + main[:, chans:] + rest


def grads_kernel(sizes, chunk, bit, c_ref, s_ref, xt_ref, w_ref, *refs):
    n_freq, chips, chunks, wide = sizes
    first, last = chunk == 0, chunk == chunks - 1
    if first:
        loc_ref, weight_ref, *refs = refs
        got, refs = refs[:chips], refs[chips:]
    else:
        starts_ref, before_ref, *refs = refs
    keep_ref, send_ref, *refs = refs
    if last:
        gk_ref, gs_ref, *refs = refs
    else:
        acc_ref, *refs = refs
    if first:
        starts_ref, all_ref, *refs = refs
    u1_ref, sh_ref, sl_ref, gp_ref, *refs = refs
    if last:
        acc_ref, flat_ref = refs
    if first:
        for k, value in enumerate(compose(chips, loc_ref, weight_ref, got, all_ref)):
            starts_ref[SUB * k : SUB * (k + 1), :] = value

    slopes(chunk, wide, starts_ref, c_ref, s_ref, u1_ref, sh_ref, sl_ref)
    frequency_grads(bit, wide, xt_ref, sh_ref, sl_ref, gp_ref, keep_ref, send_ref)
    total = increment_grads(w_ref, 3 * wide * chunk, sh_ref, sl_ref)
    if not first:
        total = total + before_ref[...]
    acc_ref[...] = total
    if not last:
        return

    rows, chans = acc_ref.shape
    core, z = lax.axis_index("tm") & 1, lax.axis_index("freq")

    def one(k, _):
        even, odd = pair_rows(acc_ref[tile(2 * k), :], acc_ref[tile(2 * k + 1), :])
        flat_ref[0, tile(k), :] = even
        flat_ref[1, tile(k), :] = odd
        return 0

    lax.fori_loop(0, rows // (2 * SUB), one, 0, unroll=8)
    piece = rows // 2 // n_freq
    for j in range(n_freq):
        at = pl.ds(pl.multiple_of(jnp.bitwise_xor(z, j) * piece, piece), piece)
        gk_ref[j] = flat_ref[core, at, :]
        gs_ref[j] = flat_ref[1 - core, at, :]


def swap(value, axis, distance):
    count = lax.axis_size(axis)
    return lax.ppermute(value, axis, [(i, i ^ distance) for i in range(count)])


def resident(value):
    return pltpu.with_memory_space_constraint(value, pltpu.HBM)


def on_device(increments, projections, phases, groups):
    steps, batch, chans = increments.shape
    freqs = phases.shape[1]
    n_tm, n_freq = lax.axis_size("tm"), lax.axis_size("freq")
    amplitude = math.sqrt(2.0 / (steps * n_tm))
    rows = 2 * steps * batch
    mine = freqs // 2
    wide = min(WIDE, mine)
    chunks = mine // wide
    each = chans // n_tm
    chips = n_tm // 2
    x = increments.reshape(rows // 2, chans)
    p = jnp.transpose(projections, (1, 0, 2))
    y = swap(x, "tm", 1)
    x, weights, turns, weight = call(
        prepare_kernel,
        "prepare",
        1.9,
        [STAY] * 4,
        [
            pltpu.VMEM((rows // 2, chans), f32),
            pltpu.VMEM((2 * chans, 3 * mine), bf16),
            pltpu.VMEM((4 * chans, 3 * mine), bf16),
            pltpu.VMEM((SUB, mine), f32),
        ],
        [
            pltpu.VMEM((chunks, 3, chans, wide), f32),
            pltpu.VMEM((3, freqs), f32),
            pltpu.SMEM((batch,), jnp.int32),
            pltpu.SemaphoreType.DMA((3 + chunks,)),
        ],
        resident(x),
        resident(p),
        resident(phases),
        resident(groups),
    )

    def waves_body(*refs):
        waves_kernel(amplitude, wide, *refs)

    cosines, sines, local, own, flat = call(
        waves_body,
        "waves",
        8.0,
        [VECTORS] * 3,
        [
            pltpu.VMEM((chunks, 3, rows, wide), f32),
            pltpu.VMEM((chunks, 3, rows, wide), f32),
            pltpu.VMEM((6 * SUB, mine), f32),
            jax.ShapeDtypeStruct((3 * SUB, mine), f32),
            pltpu.VMEM((rows, chans), f32),
        ],
        [pltpu.VMEM((rows, 4 * chans), bf16), pltpu.VMEM((rows, 3 * mine), f32)],
        x,
        y,
        turns,
    )
    got = [own] + [swap(own, "tm", 2 * d) for d in range(1, chips)]
    (xt,) = call(
        turn_kernel, "turn", 0.8, [VECTORS], [pltpu.VMEM((2 * chans, rows), bf16)], [], flat
    )

    bits = [1 << k for k in range(chips.bit_length() - 1)]
    bshape = jax.ShapeDtypeStruct((chips // 2, 2, 3, each, wide), f32)
    gshape = jax.ShapeDtypeStruct((n_freq, rows // 2 // n_freq, chans), f32)
    total = pltpu.VMEM((rows, chans), f32)
    starts = pltpu.VMEM((5 * SUB, mine), f32)
    sums = []
    for chunk in range(chunks):
        order = bits if chunk % 2 == 0 else bits[::-1]
        first, last = chunk == 0, chunk == chunks - 1

        def grads_body(*refs, chunk=chunk, bit=order[0]):
            grads_kernel((n_freq, chips, chunks, wide), chunk, bit, *refs)

        operands = [cosines, sines, xt, weights]
        operands += [local, weight, *got] if first else [entries, before]
        scratch = [pltpu.VMEM((chips, 3 * SUB, mine), f32)] if first else []
        scratch += [
            pltpu.VMEM((rows, wide), f32),
            pltpu.VMEM((rows, 3 * wide), bf16),
            pltpu.VMEM((rows, 3 * wide), bf16),
            pltpu.VMEM((n_tm, 3, each, wide), f32),
        ]
        scratch += [total, pltpu.VMEM((2, rows // 2, chans), f32)] if last else []
        outs = call(
            grads_body,
            f"grads{chunk}",
            3.5,
            [VECTORS] * len(operands),
            [bshape] * 2 + ([gshape] * 2 if last else [total]) + ([starts] if first else []),
            scratch,
            *operands,
        )
        kept, sent = outs[:2]
        if last:
            mine_kept, mine_sent = outs[2:4]
        else:
            before = outs[2]
        if first:
            entries = outs[-1]
        sums.append((kept, sent, order))

    pieces = mine_kept + swap(mine_sent, "tm", 1)
    done = []
    for kept, sent, order in sums:
        blocks = kept + swap(sent, "tm", 2 * order[0])
        for k, bit in enumerate(order[1:]):
            left = order[k + 1 :]
            place = sum(1 for b in left if b < bit)
            halves = blocks.reshape((-1, 2, 1 << place) + blocks.shape[1:])
            shape = (-1,) + blocks.shape[1:]
            mate = swap(halves[:, 1].reshape(shape), "tm", 2 * bit)
            blocks = halves[:, 0].reshape(shape) + mate
        done.append(blocks[0])
    for bit in [1 << k for k in range(n_freq.bit_length() - 1)]:
        halves = pieces.reshape((-1, 2) + pieces.shape[1:])
        pieces = halves[:, 0] + swap(halves[:, 1], "freq", bit)
    grad_increments = pieces.reshape(steps // n_freq, batch, chans)

    here = jnp.concatenate([blocks[0] for blocks in done], axis=-1)
    away = swap(jnp.concatenate([blocks[1] for blocks in done], axis=-1), "tm", 1)
    even = lax.axis_index("tm") & 1 == 0
    low, high = jnp.where(even, here, away), jnp.where(even, away, here)
    grad_projections = jnp.transpose(jnp.concatenate([low, high], axis=-1), (1, 0, 2))
    return (grad_increments, grad_projections)


def solution(mesh):
    placed = (P("tm", None, None), P(None, None, "freq"), P(None, "freq"), P())
    return jax.shard_map(
        on_device,
        mesh=mesh,
        in_specs=placed,
        out_specs=(P(("tm", "freq"), None, None), P("tm", None, "freq")),
        check_vma=False,
    )
```

```python
import math

import jax
import jax.numpy as jnp
from jax import lax
from jax.experimental import pallas as pl
from jax.experimental.pallas import tpu as pltpu
from jax.sharding import PartitionSpec as P

f32, bf16 = jnp.float32, jnp.bfloat16
SUB = 8
HALF = SUB // 2
WIDE = 256
MAGIC = 12582912.0
SIN = (3.141582022150658, -5.167142796368909, 2.541899027590427, -0.5546361970970186)
COS = (
    0.9999999534666683,
    -4.934792858675264,
    4.058411914167107,
    -1.3318801612488937,
    0.2196967986036905,
)
NT = (((1,), (1,)), ((), ()))
PARAMS = pltpu.CompilerParams(vmem_limit_bytes=24 * 1024 * 1024)
VECTORS = pl.BlockSpec(memory_space=pltpu.VMEM)
STAY = pl.BlockSpec(memory_space=pltpu.HBM)


def horner(z, coefs):
    acc = z * coefs[-1] + coefs[-2]
    for coef in coefs[-3::-1]:
        acc = acc * z + coef
    return acc


def split(value):
    high = value.astype(bf16)
    return high, (value - high.astype(f32)).astype(bf16)


def pair_rows(low, high):
    top = lax.broadcasted_iota(jnp.int32, low.shape, 0) < HALF
    first = jnp.where(top, low, pltpu.roll(high, HALF, 0))
    second = jnp.where(top, pltpu.roll(low, HALF, 0), high)
    return first, second


def tile(i, count=1):
    return pl.ds(pl.multiple_of(i * (count * SUB), count * SUB), count * SUB)


def tall(first, second):
    return jnp.concatenate([first, second], axis=0)


def call(body, name, micros, ins, outs, scratch, *operands):
    return pl.pallas_call(
        body,
        in_specs=ins,
        out_specs=[VECTORS] * len(outs),
        out_shape=outs,
        scratch_shapes=scratch,
        compiler_params=PARAMS,
        cost_estimate=pl.CostEstimate(
            flops=int(micros * 1.1e9), bytes_accessed=int(micros * 3e6), transcendentals=0
        ),
        name=name,
    )(*operands)


def prepare_kernel(x_hbm, p_hbm, ph_hbm, g_hbm, x_ref, w_ref, r_ref, weight_ref, *rest):
    p_ref, ph_ref, g_ref, sems = rest
    chunks, _, chans, wide = p_ref.shape
    batch = g_ref.shape[0]
    core = lax.axis_index("tm") & 1
    inv = 1.0 / (2.0 * math.pi)

    def columns(chunk):
        return pl.ds(pl.multiple_of((core * chunks + chunk) * wide, wide), wide)

    fetch = [pltpu.make_async_copy(ph_hbm, ph_ref, sems.at[0])]
    for k in range(chunks):
        fetch.append(
            pltpu.make_async_copy(p_hbm.at[:, :, columns(k)], p_ref.at[k], sems.at[1 + k])
        )
    fetch_x = pltpu.make_async_copy(x_hbm, x_ref, sems.at[1 + chunks])
    fetch_g = pltpu.make_async_copy(g_hbm, g_ref, sems.at[2 + chunks])
    for copy in fetch + [fetch_x, fetch_g]:
        copy.start()
    fetch[0].wait()
    row = lax.broadcasted_iota(jnp.int32, (chans, wide), 0)
    for chunk in range(chunks):
        fetch[1 + chunk].wait()
        for level in range(3):
            cols = slice((3 * chunk + level) * wide, (3 * chunk + level + 1) * wide)
            high, low = split(p_ref[chunk, level])
            w_ref[:chans, cols] = high
            w_ref[chans:, cols] = low
            high, low = split(p_ref[chunk, level] * inv)
            phase = ph_ref[level : level + 1, columns(chunk)] * inv
            phase0 = phase.astype(bf16).astype(f32)
            phase1 = (phase - phase0).astype(bf16).astype(f32)
            phase2 = phase - phase0 - phase1
            extra = jnp.where(row == 0, phase0, jnp.where(row == 1, phase1, phase2))
            extra = jnp.where(row < 3, extra, 0.0).astype(bf16)
            for k, part in enumerate((high, high, low, extra)):
                r_ref[chans * k : chans * (k + 1), cols] = part
    fetch_g.wait()
    row = lax.broadcasted_iota(jnp.int32, weight_ref.shape, 0)
    weight = jnp.zeros(weight_ref.shape, f32)
    for b in range(batch):
        value = jnp.where(g_ref[b] == 1, 2.0 / batch, -2.0 / batch)
        weight = jnp.where(row == b, value, weight)
    weight_ref[...] = weight
    fetch_x.wait()


def turn_kernel(flat_ref, xt_ref):
    chans = flat_ref.shape[1]
    high, low = split(flat_ref[...].T)
    xt_ref[:chans, :] = high
    xt_ref[chans:, :] = low


def waves_kernel(amplitude, wide, x_ref, y_ref, r_ref, *rest):
    c_ref, s_ref, loc_ref, snd_ref, flat_ref, xs_ref, ang0_ref, ang1_ref = rest
    rows, chans = flat_ref.shape
    chunks = c_ref.shape[0]
    core = lax.axis_index("tm") & 1
    root = math.sqrt(2.0 * amplitude)
    sin_coefs = [root * coef for coef in SIN]
    cos_coefs = [-root * coef for coef in COS]
    lane = lax.broadcasted_iota(jnp.int32, (2 * SUB, chans), 1)
    ones = jnp.where(lane < 3, 1.0, 0.0).astype(bf16)

    def pairs(even_ref, odd_ref):
        def one(k, _):
            both = tall(*pair_rows(even_ref[tile(k), :], odd_ref[tile(k), :]))
            flat_ref[tile(k, 2), :] = both
            high, low = split(both)
            xs_ref[tile(k, 2), :] = jnp.concatenate([high, low, high, ones], axis=1)
            return 0

        lax.fori_loop(0, rows // (2 * SUB), one, 0, unroll=8)

    @pl.when(core == 0)
    def _():
        pairs(x_ref, y_ref)

    @pl.when(core == 1)
    def _():
        pairs(y_ref, x_ref)

    block = ang0_ref.shape[0]
    blocks = rows // block

    def turns(item, ang_ref):
        at = pl.ds(pl.multiple_of(lax.rem(item, blocks) * block, block), block)
        cols = pl.ds(pl.multiple_of(lax.div(item, blocks) * (3 * wide), 3 * wide), 3 * wide)
        ang_ref[...] = jnp.dot(xs_ref[at, :], r_ref[:, cols], preferred_element_type=f32)

    def sums_over(chunk, base, ang_ref, carry):
        for k in range(block // SUB):
            s0, s1, s2, s01, s12, s012 = carry
            at = pl.ds(pl.multiple_of(base + k * SUB, SUB), SUB)
            cosines = []
            for level in range(3):
                turn = ang_ref[k * SUB : (k + 1) * SUB, level * wide : (level + 1) * wide]
                r = turn - ((turn + MAGIC) - MAGIC)
                z = r * r
                sine = r * horner(z, sin_coefs)
                cosine = horner(z, cos_coefs)
                wave = amplitude - sine * sine
                c_ref[chunk, level, at, :] = wave
                s_ref[chunk, level, at, :] = sine * cosine
                cosines.append(wave)
            c0, c1, c2 = cosines
            s012 = s012 + s01 * c2
            s12 = s12 + s1 * c2
            s01 = s01 + s0 * c1
            carry = (s0 + c0, s1 + c1, s2 + c2, s01, s12, s012)
        return carry

    zero = jnp.zeros((SUB, wide), f32)
    turns(jnp.int32(0), ang0_ref)
    for chunk in range(chunks):
        here = slice(chunk * wide, (chunk + 1) * wide)

        def step(i, carry):
            item = chunk * blocks + 2 * i
            turns(item + 1, ang1_ref)
            carry = sums_over(chunk, 2 * i * block, ang0_ref, carry)
            turns(jnp.minimum(item + 2, chunks * blocks - 1), ang0_ref)
            return sums_over(chunk, (2 * i + 1) * block, ang1_ref, carry)

        sums = lax.fori_loop(0, blocks // 2, step, (zero,) * 6)
        for k in range(6):
            loc_ref[SUB * k : SUB * (k + 1), here] = sums[k]
        a0, a1, a2, a01, a12, a012 = [v[:HALF] for v in sums]
        b0, b1, b2, b01, b12, b012 = [v[HALF:] for v in sums]
        both = (
            a0 + b0,
            a1 + b1,
            a2 + b2,
            a01 + b01 + a0 * b1,
            a12 + b12 + a1 * b2,
            a012 + b012 + a0 * b12 + a01 * b2,
        )
        for k in range(6):
            snd_ref[HALF * k : HALF * (k + 1), here] = both[k]


def compose(chips, loc_ref, weight_ref, got, all_ref):
    chip = lax.axis_index("tm") >> 1
    for d in range(chips):
        all_ref[jnp.bitwise_xor(chip, d)] = got[d][...]

    weight = weight_ref[:HALF]
    zero = jnp.zeros(weight.shape, f32)

    def sums_of(j):
        return [all_ref[j, HALF * k : HALF * (k + 1), :] for k in range(6)]

    def forward(j, carry):
        p0, p01, p012 = carry
        b0, b1, b2, b01, b12, b012 = sums_of(j)
        p012 = p012 + b012 + p0 * b12 + p01 * b2
        p01 = p01 + b01 + p0 * b1
        return (p0 + b0, p01, p012)

    def backward(step, carry):
        t1, t2, t12 = carry
        b0, b1, b2, b01, b12, b012 = sums_of(chips - 1 - step)
        t12 = t12 + b12 + b1 * t2
        return (t1 + b1, t2 + b2, t12)

    entry = lax.fori_loop(0, chip, forward, (zero,) * 3)
    e1, e2 = entry[:2]
    totals = lax.fori_loop(chip, chips, forward, entry)
    t1, t2, t12 = lax.fori_loop(0, chips - 1 - chip, backward, (zero,) * 3)
    seeds = [2.0 * weight * jnp.sum(weight * total, axis=0, keepdims=True) for total in totals]

    def local(k):
        value = loc_ref[SUB * k : SUB * (k + 1), :]
        return value[:HALF], value[HALF:]

    a0, _ = local(0)
    a1, b1 = local(1)
    _, b2 = local(2)
    a01, _ = local(3)
    _, b12 = local(4)
    d0, d1, d2 = [tall(seed, seed) for seed in seeds]
    tail2 = tall(t2 + b2, t2)
    tail1 = tall(t1 + b1, t1)
    tail12 = tall(t12 + b12 + b1 * t2, t12)
    return (
        d2,
        tall(e1, e1 + a0),
        tall(e2, e2 + a01 + e1 * a1),
        d1 + d2 * tail2,
        d0 + d1 * tail1 + d2 * tail12,
    )


def slopes(chunk, wide, starts_ref, c_ref, s_ref, u1_ref, sh_ref, sl_ref):
    rows = u1_ref.shape[0]
    scale, front1, front2, adjoint1, adjoint0 = [
        starts_ref[SUB * k : SUB * (k + 1), chunk * wide : (chunk + 1) * wide] for k in range(5)
    ]

    def keep(pair, level, values):
        high, low = split(tall(*values))
        sh_ref[tile(pair, 2), level * wide : (level + 1) * wide] = high
        sl_ref[tile(pair, 2), level * wide : (level + 1) * wide] = low

    def fwd(pair, carry):
        f1, f2 = carry
        slope2 = []
        for which in range(2):
            at = tile(2 * pair + which)
            u1_ref[at, :] = s_ref[chunk, 1, at, :] * f1
            slope2.append(s_ref[chunk, 2, at, :] * (scale * f2))
            f2 = f2 + f1 * c_ref[chunk, 1, at, :]
            f1 = f1 + c_ref[chunk, 0, at, :]
        keep(pair, 2, slope2)
        return f1, f2

    lax.fori_loop(0, rows // (2 * SUB), fwd, (front1, front2), unroll=8)

    def bwd(step, carry):
        g1, g0 = carry
        pair = rows // (2 * SUB) - 1 - step
        slope0, slope1 = [], []
        for which in (1, 0):
            at = tile(2 * pair + which)
            slope1.append(u1_ref[at, :] * g1)
            slope0.append(s_ref[chunk, 0, at, :] * g0)
            g0 = g0 + g1 * c_ref[chunk, 1, at, :]
            g1 = g1 + scale * c_ref[chunk, 2, at, :]
        keep(pair, 0, slope0[::-1])
        keep(pair, 1, slope1[::-1])
        return g1, g0

    lax.fori_loop(0, rows // (2 * SUB), bwd, (adjoint1, adjoint0), unroll=8)


def frequency_grads(bit, wide, xt_ref, sh_ref, sl_ref, gp_ref, keep_ref, send_ref):
    n_tm, _, each, _ = gp_ref.shape
    chans = n_tm * each
    main = jnp.dot(xt_ref[...], sh_ref[...], preferred_element_type=f32)
    rest = jnp.dot(xt_ref[:chans, :], sl_ref[...], preferred_element_type=f32)
    grad = main[:chans] + main[chans:] + rest
    for level in range(3):
        for d in range(n_tm):
            gp_ref[d, level] = grad[each * d : each * (d + 1), level * wide : (level + 1) * wide]
    me = lax.axis_index("tm")
    near = [j for j in range(n_tm // 2) if not j & bit]
    for k, j in enumerate(near):
        for core in range(2):
            keep_ref[k, core] = gp_ref[jnp.bitwise_xor(me, 2 * j + core)]
            send_ref[k, core] = gp_ref[jnp.bitwise_xor(me, 2 * (j | bit) + core)]


def increment_grads(w_ref, at, sh_ref, sl_ref):
    chans = w_ref.shape[0] // 2
    cols = slice(at, at + sh_ref.shape[1])
    main = lax.dot_general(sh_ref[...], w_ref[:, cols], NT, preferred_element_type=f32)
    rest = lax.dot_general(sl_ref[...], w_ref[:chans, cols], NT, preferred_element_type=f32)
    return main[:, :chans] + main[:, chans:] + rest


def grads_kernel(sizes, chunk, bit, c_ref, s_ref, *refs):
    n_freq, chips, chunks, wide = sizes
    first, last = chunk == 0, chunk == chunks - 1
    if first:
        loc_ref, weight_ref, *refs = refs
        got, refs = refs[:chips], refs[chips:]
    else:
        starts_ref, *refs = refs
    if last:
        w_ref, *refs = refs
        before, refs = refs[: 2 * chunk], refs[2 * chunk :]
    else:
        xt_ref, keep_ref, send_ref, *refs = refs
    sh_ref, sl_ref, *refs = refs
    if last:
        gk_ref, gs_ref, *refs = refs
    if first:
        starts_ref, all_ref, *refs = refs
    u1_ref, *refs = refs
    if first:
        for k, value in enumerate(compose(chips, loc_ref, weight_ref, got, all_ref)):
            starts_ref[SUB * k : SUB * (k + 1), :] = value

    slopes(chunk, wide, starts_ref, c_ref, s_ref, u1_ref, sh_ref, sl_ref)
    if not last:
        (gp_ref,) = refs
        frequency_grads(bit, wide, xt_ref, sh_ref, sl_ref, gp_ref, keep_ref, send_ref)
        return

    acc_ref, flat_ref = refs
    total = increment_grads(w_ref, 3 * wide * chunk, sh_ref, sl_ref)
    for k in range(chunk):
        total = total + increment_grads(w_ref, 3 * wide * k, before[2 * k], before[2 * k + 1])
    acc_ref[...] = total

    rows, chans = acc_ref.shape
    core, z = lax.axis_index("tm") & 1, lax.axis_index("freq")

    def one(k, _):
        even, odd = pair_rows(acc_ref[tile(2 * k), :], acc_ref[tile(2 * k + 1), :])
        flat_ref[0, tile(k), :] = even
        flat_ref[1, tile(k), :] = odd
        return 0

    lax.fori_loop(0, rows // (2 * SUB), one, 0, unroll=8)
    piece = rows // 2 // n_freq
    for j in range(n_freq):
        at = pl.ds(pl.multiple_of(jnp.bitwise_xor(z, j) * piece, piece), piece)
        gk_ref[j] = flat_ref[core, at, :]
        gs_ref[j] = flat_ref[1 - core, at, :]


def join_kernel(n_freq, early, places, kept_ref, other_ref, *refs):
    blocks, refs = refs[: 2 * early], refs[2 * early :]
    for j in range(n_freq):
        refs[j][...] = kept_ref[j] + other_ref[j]
    for k in range(early):
        near_ref, far_ref = refs[n_freq + 2 * k : n_freq + 2 * k + 2]
        size, bit = near_ref.shape[0], 1 << places[k]
        for j in range(size):
            at = (j // bit) * (2 * bit) + j % bit
            near_ref[j] = blocks[2 * k][at] + blocks[2 * k + 1][at]
            far_ref[j] = blocks[2 * k][at + bit] + blocks[2 * k + 1][at + bit]


def swap(value, axis, distance):
    count = lax.axis_size(axis)
    return lax.ppermute(value, axis, [(i, i ^ distance) for i in range(count)])


def resident(value):
    return pltpu.with_memory_space_constraint(value, pltpu.HBM)


def on_device(increments, projections, phases, groups):
    steps, batch, chans = increments.shape
    freqs = phases.shape[1]
    n_tm, n_freq = lax.axis_size("tm"), lax.axis_size("freq")
    amplitude = math.sqrt(2.0 / (steps * n_tm))
    rows = 2 * steps * batch
    mine = freqs // 2
    wide = min(WIDE, mine)
    chunks = mine // wide
    each = chans // n_tm
    chips = n_tm // 2
    x = increments.reshape(rows // 2, chans)
    p = jnp.transpose(projections, (1, 0, 2))
    y = swap(x, "tm", 1)
    x, weights, turns, weight = call(
        prepare_kernel,
        "prepare",
        1.9,
        [STAY] * 4,
        [
            pltpu.VMEM((rows // 2, chans), f32),
            pltpu.VMEM((2 * chans, 3 * mine), bf16),
            pltpu.VMEM((4 * chans, 3 * mine), bf16),
            pltpu.VMEM((SUB, mine), f32),
        ],
        [
            pltpu.VMEM((chunks, 3, chans, wide), f32),
            pltpu.VMEM((3, freqs), f32),
            pltpu.SMEM((batch,), jnp.int32),
            pltpu.SemaphoreType.DMA((3 + chunks,)),
        ],
        resident(x),
        resident(p),
        resident(phases),
        resident(groups),
    )

    def waves_body(*refs):
        waves_kernel(amplitude, wide, *refs)

    cosines, sines, local, own, flat = call(
        waves_body,
        "waves",
        8.0,
        [VECTORS] * 3,
        [
            pltpu.VMEM((chunks, 3, rows, wide), f32),
            pltpu.VMEM((chunks, 3, rows, wide), f32),
            pltpu.VMEM((6 * SUB, mine), f32),
            jax.ShapeDtypeStruct((3 * SUB, mine), f32),
            pltpu.VMEM((rows, chans), f32),
        ],
        [pltpu.VMEM((rows, 4 * chans), bf16)] + [pltpu.VMEM((rows // 4, 3 * wide), f32)] * 2,
        x,
        y,
        turns,
    )
    got = [own] + [swap(own, "tm", 2 * d) for d in range(1, chips)]
    (xt,) = call(
        turn_kernel, "turn", 0.8, [VECTORS], [pltpu.VMEM((2 * chans, rows), bf16)], [], flat
    )

    bits = [1 << k for k in range(chips.bit_length() - 1)]
    orders = [bits if chunk % 2 == 0 else bits[::-1] for chunk in range(chunks)]
    bshape = jax.ShapeDtypeStruct((chips // 2, 2, 3, each, wide), f32)
    gshape = jax.ShapeDtypeStruct((n_freq, rows // 2 // n_freq, chans), f32)
    gp = pltpu.VMEM((n_tm, 3, each, wide), f32)
    early, parts = [], []
    for chunk in range(chunks):
        first, last = chunk == 0, chunk == chunks - 1

        def grads_body(*refs, chunk=chunk):
            grads_kernel((n_freq, chips, chunks, wide), chunk, orders[chunk][0], *refs)

        operands = [cosines, sines] + ([local, weight, *got] if first else [entries])
        operands += [weights, *parts] if last else [xt]
        outs = [] if last else [bshape] * 2
        outs += [pltpu.VMEM((rows, 3 * wide), bf16)] * 2
        outs += [gshape] * 2 if last else []
        outs += [pltpu.VMEM((5 * SUB, mine), f32)] if first else []
        scratch = [pltpu.VMEM((chips, 3 * SUB, mine), f32)] if first else []
        scratch += [pltpu.VMEM((rows, wide), f32)]
        if last:
            scratch += [pltpu.VMEM((rows, chans), f32), pltpu.VMEM((2, rows // 2, chans), f32)]
        else:
            scratch += [gp]
        outs = call(
            grads_body, f"grads{chunk}", 2.5, [VECTORS] * len(operands), outs, scratch, *operands
        )
        if first:
            entries = outs[-1]
        if last:
            high, low, kept, sent = outs[:4]
        else:
            early += [outs[0], swap(outs[1], "tm", 2 * orders[chunk][0])]
            parts += outs[2:4]

    other = swap(sent, "tm", 1)

    def last_body(*refs):
        frequency_grads(orders[-1][0], wide, *refs[:3], refs[5], *refs[3:5])

    near, far = call(
        last_body, "last", 0.8, [VECTORS] * 3, [bshape] * 2, [gp], xt, high, low
    )
    near_sum = near + swap(far, "tm", 2 * orders[-1][0])

    def place(order, step):
        return sum(1 for b in order[step:] if b < order[step])

    def join_body(*refs):
        join_kernel(n_freq, chunks - 1, [place(order, 1) for order in orders[:-1]], *refs)

    half = jax.ShapeDtypeStruct((chips // 4,) + bshape.shape[1:], f32)
    joined = call(
        join_body,
        "join",
        0.2,
        [VECTORS] * (2 + len(early)),
        [jax.ShapeDtypeStruct(gshape.shape[1:], f32)] * n_freq + [half] * len(early),
        [],
        kept,
        other,
        *early,
    )
    result = joined[0]
    for j in range(1, n_freq):
        result = result + swap(joined[j], "freq", j)
    grad_increments = result.reshape(steps // n_freq, batch, chans)

    done = []
    for chunk, order in enumerate(orders):
        if chunk < chunks - 1:
            kept, sent = joined[n_freq + 2 * chunk : n_freq + 2 * chunk + 2]
            blocks, step = kept + swap(sent, "tm", 2 * order[1]), 2
        else:
            blocks, step = near_sum, 1
        for k in range(step, len(order)):
            halves = blocks.reshape((-1, 2, 1 << place(order, k)) + blocks.shape[1:])
            shape = (-1,) + blocks.shape[1:]
            mate = swap(halves[:, 1].reshape(shape), "tm", 2 * order[k])
            blocks = halves[:, 0].reshape(shape) + mate
        done.append(blocks[0])

    here = jnp.concatenate([blocks[0] for blocks in done], axis=-1)
    away = swap(jnp.concatenate([blocks[1] for blocks in done], axis=-1), "tm", 1)
    even = lax.axis_index("tm") & 1 == 0
    low, high = jnp.where(even, here, away), jnp.where(even, away, here)
    grad_projections = jnp.transpose(jnp.concatenate([low, high], axis=-1), (1, 0, 2))
    return (grad_increments, grad_projections)


def solution(mesh):
    placed = (P("tm", None, None), P(None, None, "freq"), P(None, "freq"), P())
    return jax.shard_map(
        on_device,
        mesh=mesh,
        in_specs=placed,
        out_specs=(P(("tm", "freq"), None, None), P("tm", None, "freq")),
        check_vma=False,
    )
```

```python
import math

import jax
import jax.numpy as jnp
from jax import lax
from jax.experimental import pallas as pl
from jax.experimental.pallas import tpu as pltpu
from jax.sharding import PartitionSpec as P

f32, bf16 = jnp.float32, jnp.bfloat16
SUB = 8
HALF = SUB // 2
WIDE = 256
MAGIC = 12582912.0
SIN = (3.141582022150658, -5.167142796368909, 2.541899027590427, -0.5546361970970186)
COS = (
    0.9999999534666683,
    -4.934792858675264,
    4.058411914167107,
    -1.3318801612488937,
    0.2196967986036905,
)
NT = (((1,), (1,)), ((), ()))
PARAMS = pltpu.CompilerParams(vmem_limit_bytes=20 * 1024 * 1024)
VECTORS = pl.BlockSpec(memory_space=pltpu.VMEM)
STAY = pl.BlockSpec(memory_space=pltpu.HBM)


def horner(z, coefs):
    acc = z * coefs[-1] + coefs[-2]
    for coef in coefs[-3::-1]:
        acc = acc * z + coef
    return acc


def split(value):
    high = value.astype(bf16)
    return high, (value - high.astype(f32)).astype(bf16)


def pair_rows(low, high):
    top = lax.broadcasted_iota(jnp.int32, low.shape, 0) < HALF
    first = jnp.where(top, low, pltpu.roll(high, HALF, 0))
    second = jnp.where(top, pltpu.roll(low, HALF, 0), high)
    return first, second


def tile(i, count=1):
    return pl.ds(pl.multiple_of(i * (count * SUB), count * SUB), count * SUB)


def tall(first, second):
    return jnp.concatenate([first, second], axis=0)


def call(body, name, micros, ins, outs, scratch, *operands):
    return pl.pallas_call(
        body,
        in_specs=ins,
        out_specs=[VECTORS] * len(outs),
        out_shape=outs,
        scratch_shapes=scratch,
        compiler_params=PARAMS,
        cost_estimate=pl.CostEstimate(
            flops=int(micros * 1.1e9), bytes_accessed=int(micros * 3e6), transcendentals=0
        ),
        name=name,
    )(*operands)


def prepare_kernel(x_hbm, p_hbm, ph_hbm, g_hbm, x_ref, w_ref, r_ref, weight_ref, *rest):
    p_ref, ph_ref, g_ref, sems = rest
    chunks, _, chans, wide = p_ref.shape
    batch = g_ref.shape[0]
    core = lax.axis_index("tm") & 1
    inv = 1.0 / (2.0 * math.pi)

    def columns(chunk):
        return pl.ds(pl.multiple_of((core * chunks + chunk) * wide, wide), wide)

    fetch = [pltpu.make_async_copy(ph_hbm, ph_ref, sems.at[0])]
    for k in range(chunks):
        fetch.append(
            pltpu.make_async_copy(p_hbm.at[:, :, columns(k)], p_ref.at[k], sems.at[1 + k])
        )
    fetch_x = pltpu.make_async_copy(x_hbm, x_ref, sems.at[1 + chunks])
    fetch_g = pltpu.make_async_copy(g_hbm, g_ref, sems.at[2 + chunks])
    for copy in fetch + [fetch_x, fetch_g]:
        copy.start()
    fetch[0].wait()
    row = lax.broadcasted_iota(jnp.int32, (chans, wide), 0)
    for chunk in range(chunks):
        fetch[1 + chunk].wait()
        for level in range(3):
            cols = slice((3 * chunk + level) * wide, (3 * chunk + level + 1) * wide)
            high, low = split(p_ref[chunk, level])
            w_ref[:chans, cols] = high
            w_ref[chans:, cols] = low
            high, low = split(p_ref[chunk, level] * inv)
            phase = ph_ref[level : level + 1, columns(chunk)] * inv
            phase0 = phase.astype(bf16).astype(f32)
            phase1 = (phase - phase0).astype(bf16).astype(f32)
            phase2 = phase - phase0 - phase1
            extra = jnp.where(row == 0, phase0, jnp.where(row == 1, phase1, phase2))
            extra = jnp.where(row < 3, extra, 0.0).astype(bf16)
            for k, part in enumerate((high, high, low, extra)):
                r_ref[chans * k : chans * (k + 1), cols] = part
    fetch_g.wait()
    row = lax.broadcasted_iota(jnp.int32, weight_ref.shape, 0)
    weight = jnp.zeros(weight_ref.shape, f32)
    for b in range(batch):
        value = jnp.where(g_ref[b] == 1, 2.0 / batch, -2.0 / batch)
        weight = jnp.where(row == b, value, weight)
    weight_ref[...] = weight
    fetch_x.wait()


def turn_kernel(flat_ref, xt_ref):
    chans = flat_ref.shape[1]
    high, low = split(flat_ref[...].T)
    xt_ref[:chans, :] = high
    xt_ref[chans:, :] = low


def waves_kernel(amplitude, wide, x_ref, y_ref, r_ref, *rest):
    c_ref, half_ref, z_ref, loc_ref, snd_ref, flat_ref, xs_ref, ang0_ref, ang1_ref = rest
    rows, chans = flat_ref.shape
    chunks = c_ref.shape[0]
    core = lax.axis_index("tm") & 1
    root = math.sqrt(2.0 * amplitude)
    sin_coefs = [root * coef for coef in SIN]
    lane = lax.broadcasted_iota(jnp.int32, (2 * SUB, chans), 1)
    ones = jnp.where(lane < 3, 1.0, 0.0).astype(bf16)

    def pairs(even_ref, odd_ref):
        def one(k, _):
            both = tall(*pair_rows(even_ref[tile(k), :], odd_ref[tile(k), :]))
            flat_ref[tile(k, 2), :] = both
            high, low = split(both)
            xs_ref[tile(k, 2), :] = jnp.concatenate([high, low, high, ones], axis=1)
            return 0

        lax.fori_loop(0, rows // (2 * SUB), one, 0, unroll=8)

    @pl.when(core == 0)
    def _():
        pairs(x_ref, y_ref)

    @pl.when(core == 1)
    def _():
        pairs(y_ref, x_ref)

    block = ang0_ref.shape[0]
    blocks = rows // block

    def turns(item, ang_ref):
        at = pl.ds(pl.multiple_of(lax.rem(item, blocks) * block, block), block)
        cols = pl.ds(pl.multiple_of(lax.div(item, blocks) * (3 * wide), 3 * wide), 3 * wide)
        ang_ref[...] = jnp.dot(xs_ref[at, :], r_ref[:, cols], preferred_element_type=f32)

    def sums_over(chunk, base, ang_ref, carry):
        for k in range(block // SUB):
            s0, s1, s2, s01, s12, s012 = carry
            at = pl.ds(pl.multiple_of(base + k * SUB, SUB), SUB)
            cosines = []
            for level in range(3):
                turn = ang_ref[k * SUB : (k + 1) * SUB, level * wide : (level + 1) * wide]
                r = turn - ((turn + MAGIC) - MAGIC)
                z = r * r
                sine = r * horner(z, sin_coefs)
                wave = amplitude - sine * sine
                c_ref[chunk, level, at, :] = wave
                half_ref[chunk, level, at, :] = sine
                z_ref[chunk, level, at, :] = z
                cosines.append(wave)
            c0, c1, c2 = cosines
            s012 = s012 + s01 * c2
            s12 = s12 + s1 * c2
            s01 = s01 + s0 * c1
            carry = (s0 + c0, s1 + c1, s2 + c2, s01, s12, s012)
        return carry

    zero = jnp.zeros((SUB, wide), f32)
    turns(jnp.int32(0), ang0_ref)
    for chunk in range(chunks):
        here = slice(chunk * wide, (chunk + 1) * wide)

        def step(i, carry):
            item = chunk * blocks + 2 * i
            turns(item + 1, ang1_ref)
            carry = sums_over(chunk, 2 * i * block, ang0_ref, carry)
            turns(jnp.minimum(item + 2, chunks * blocks - 1), ang0_ref)
            return sums_over(chunk, (2 * i + 1) * block, ang1_ref, carry)

        sums = lax.fori_loop(0, blocks // 2, step, (zero,) * 6)
        for k in range(6):
            loc_ref[SUB * k : SUB * (k + 1), here] = sums[k]
        a0, a1, a2, a01, a12, a012 = [v[:HALF] for v in sums]
        b0, b1, b2, b01, b12, b012 = [v[HALF:] for v in sums]
        both = (
            a0 + b0,
            a1 + b1,
            a2 + b2,
            a01 + b01 + a0 * b1,
            a12 + b12 + a1 * b2,
            a012 + b012 + a0 * b12 + a01 * b2,
        )
        for k in range(6):
            snd_ref[HALF * k : HALF * (k + 1), here] = both[k]


def sines_kernel(amplitude, half_ref, z_ref, s_ref):
    chunks, levels, rows, _ = s_ref.shape
    coefs = [-math.sqrt(2.0 * amplitude) * coef for coef in COS]
    for chunk in range(chunks):
        for level in range(levels):

            def step(i, _):
                value = horner(z_ref[chunk, level, tile(i), :], coefs)
                s_ref[chunk, level, tile(i), :] = half_ref[chunk, level, tile(i), :] * value
                return 0

            lax.fori_loop(0, rows // SUB, step, 0, unroll=16)


def compose(chips, loc_ref, weight_ref, got, all_ref):
    chip = lax.axis_index("tm") >> 1
    for d in range(chips):
        all_ref[jnp.bitwise_xor(chip, d)] = got[d][...]

    weight = weight_ref[:HALF]
    zero = jnp.zeros(weight.shape, f32)

    def sums_of(j):
        return [all_ref[j, HALF * k : HALF * (k + 1), :] for k in range(6)]

    def forward(j, carry):
        p0, p01, p012 = carry
        b0, b1, b2, b01, b12, b012 = sums_of(j)
        p012 = p012 + b012 + p0 * b12 + p01 * b2
        p01 = p01 + b01 + p0 * b1
        return (p0 + b0, p01, p012)

    def backward(step, carry):
        t1, t2, t12 = carry
        b0, b1, b2, b01, b12, b012 = sums_of(chips - 1 - step)
        t12 = t12 + b12 + b1 * t2
        return (t1 + b1, t2 + b2, t12)

    entry = lax.fori_loop(0, chip, forward, (zero,) * 3)
    e1, e2 = entry[:2]
    totals = lax.fori_loop(chip, chips, forward, entry)
    t1, t2, t12 = lax.fori_loop(0, chips - 1 - chip, backward, (zero,) * 3)
    seeds = [2.0 * weight * jnp.sum(weight * total, axis=0, keepdims=True) for total in totals]

    def local(k):
        value = loc_ref[SUB * k : SUB * (k + 1), :]
        return value[:HALF], value[HALF:]

    a0, _ = local(0)
    a1, b1 = local(1)
    _, b2 = local(2)
    a01, _ = local(3)
    _, b12 = local(4)
    d0, d1, d2 = [tall(seed, seed) for seed in seeds]
    tail2 = tall(t2 + b2, t2)
    tail1 = tall(t1 + b1, t1)
    tail12 = tall(t12 + b12 + b1 * t2, t12)
    return (
        d2,
        tall(e1, e1 + a0),
        tall(e2, e2 + a01 + e1 * a1),
        d1 + d2 * tail2,
        d0 + d1 * tail1 + d2 * tail12,
    )


def slopes(chunk, wide, starts, c_ref, s_ref, u1_ref, sh_ref, sl_ref):
    rows = u1_ref.shape[0]
    scale, front1, front2, adjoint1, adjoint0 = [
        v[:, chunk * wide : (chunk + 1) * wide] for v in starts
    ]

    def keep(pair, level, values):
        high, low = split(tall(*values))
        at = (3 * chunk + level) * wide
        sh_ref[tile(pair, 2), at : at + wide] = high
        sl_ref[tile(pair, 2), at : at + wide] = low

    def fwd(pair, carry):
        f1, f2 = carry
        slope2 = []
        for which in range(2):
            at = tile(2 * pair + which)
            u1_ref[at, :] = s_ref[chunk, 1, at, :] * f1
            slope2.append(s_ref[chunk, 2, at, :] * (scale * f2))
            f2 = f2 + f1 * c_ref[chunk, 1, at, :]
            f1 = f1 + c_ref[chunk, 0, at, :]
        keep(pair, 2, slope2)
        return f1, f2

    lax.fori_loop(0, rows // (2 * SUB), fwd, (front1, front2), unroll=8)

    def bwd(step, carry):
        g1, g0 = carry
        pair = rows // (2 * SUB) - 1 - step
        slope0, slope1 = [], []
        for which in (1, 0):
            at = tile(2 * pair + which)
            slope1.append(u1_ref[at, :] * g1)
            slope0.append(s_ref[chunk, 0, at, :] * g0)
            g0 = g0 + g1 * c_ref[chunk, 1, at, :]
            g1 = g1 + scale * c_ref[chunk, 2, at, :]
        keep(pair, 0, slope0[::-1])
        keep(pair, 1, slope1[::-1])
        return g1, g0

    lax.fori_loop(0, rows // (2 * SUB), bwd, (adjoint1, adjoint0), unroll=8)


def grads_kernel(sizes, c_ref, s_ref, loc_ref, xt_ref, w_ref, weight_ref, *refs):
    n_tm, n_freq, wide = sizes
    chips = n_tm // 2
    got, refs = refs[:chips], refs[chips:]
    blocks, refs = refs[:chips], refs[chips:]
    gk_ref, gs_ref, sh_ref, sl_ref, gp_ref, all_ref, u1_ref, acc_ref, flat_ref = refs
    rows, chans = acc_ref.shape
    each = chans // n_tm
    me = lax.axis_index("tm")
    core, z = me & 1, lax.axis_index("freq")

    starts = compose(chips, loc_ref, weight_ref, got, all_ref)
    for chunk in range(c_ref.shape[0]):
        slopes(chunk, wide, starts, c_ref, s_ref, u1_ref, sh_ref, sl_ref)

    main = jnp.dot(xt_ref[...], sh_ref[...], preferred_element_type=f32)
    rest = jnp.dot(xt_ref[:chans, :], sl_ref[...], preferred_element_type=f32)
    grad = main[:chans] + main[chans:] + rest
    for chunk in range(c_ref.shape[0]):
        for level in range(3):
            at = (3 * chunk + level) * wide
            for d in range(n_tm):
                gp_ref[d, level, :, chunk * wide : (chunk + 1) * wide] = grad[
                    each * d : each * (d + 1), at : at + wide
                ]
    for d in range(n_tm):
        blocks[d // 2][d % 2] = gp_ref[jnp.bitwise_xor(me, d)]

    main = lax.dot_general(sh_ref[...], w_ref[...], NT, preferred_element_type=f32)
    rest = lax.dot_general(sl_ref[...], w_ref[:chans, :], NT, preferred_element_type=f32)
    acc_ref[...] = main[:, :chans] + main[:, chans:] + rest

    def one(k, _):
        even, odd = pair_rows(acc_ref[tile(2 * k), :], acc_ref[tile(2 * k + 1), :])
        flat_ref[0, tile(k), :] = even
        flat_ref[1, tile(k), :] = odd
        return 0

    lax.fori_loop(0, rows // (2 * SUB), one, 0, unroll=8)
    piece = rows // 2 // n_freq
    for j in range(n_freq):
        at = pl.ds(pl.multiple_of(jnp.bitwise_xor(z, j) * piece, piece), piece)
        gk_ref[j] = flat_ref[core, at, :]
        gs_ref[j] = flat_ref[1 - core, at, :]


def swap(value, axis, distance):
    count = lax.axis_size(axis)
    return lax.ppermute(value, axis, [(i, i ^ distance) for i in range(count)])


def resident(value):
    return pltpu.with_memory_space_constraint(value, pltpu.HBM)


def on_device(increments, projections, phases, groups):
    steps, batch, chans = increments.shape
    freqs = phases.shape[1]
    n_tm, n_freq = lax.axis_size("tm"), lax.axis_size("freq")
    amplitude = math.sqrt(2.0 / (steps * n_tm))
    rows = 2 * steps * batch
    mine = freqs // 2
    wide = min(WIDE, mine)
    chunks = mine // wide
    each = chans // n_tm
    chips = n_tm // 2
    x = increments.reshape(rows // 2, chans)
    p = jnp.transpose(projections, (1, 0, 2))
    y = swap(x, "tm", 1)
    x, weights, turns, weight = call(
        prepare_kernel,
        "prepare",
        1.9,
        [STAY] * 4,
        [
            pltpu.VMEM((rows // 2, chans), f32),
            pltpu.VMEM((2 * chans, 3 * mine), bf16),
            pltpu.VMEM((4 * chans, 3 * mine), bf16),
            pltpu.VMEM((SUB, mine), f32),
        ],
        [
            pltpu.VMEM((chunks, 3, chans, wide), f32),
            pltpu.VMEM((3, freqs), f32),
            pltpu.SMEM((batch,), jnp.int32),
            pltpu.SemaphoreType.DMA((3 + chunks,)),
        ],
        resident(x),
        resident(p),
        resident(phases),
        resident(groups),
    )

    def waves_body(*refs):
        waves_kernel(amplitude, wide, *refs)

    def sines_body(*refs):
        sines_kernel(amplitude, *refs)

    big = pltpu.VMEM((chunks, 3, rows, wide), f32)
    cosines, halves, squares, local, own, flat = call(
        waves_body,
        "waves",
        8.0,
        [VECTORS] * 3,
        [
            big,
            big,
            big,
            pltpu.VMEM((6 * SUB, mine), f32),
            jax.ShapeDtypeStruct((3 * SUB, mine), f32),
            pltpu.VMEM((rows, chans), f32),
        ],
        [pltpu.VMEM((rows, 4 * chans), bf16)] + [pltpu.VMEM((rows // 4, 3 * wide), f32)] * 2,
        x,
        y,
        turns,
    )
    got = [own] + [swap(own, "tm", 2 * d) for d in range(1, chips)]
    (xt,) = call(
        turn_kernel, "turn", 0.8, [VECTORS], [pltpu.VMEM((2 * chans, rows), bf16)], [], flat
    )

    (sines,) = call(sines_body, "sines", 2.4, [VECTORS] * 2, [big], [], halves, squares)

    def grads_body(*refs):
        grads_kernel((n_tm, n_freq, wide), *refs)

    bshape = jax.ShapeDtypeStruct((2, 3, each, mine), f32)
    gshape = jax.ShapeDtypeStruct((n_freq, rows // 2 // n_freq, chans), f32)
    *blocks, kept, sent = call(
        grads_body,
        "grads",
        6.0,
        [VECTORS] * (6 + chips),
        [bshape] * chips + [gshape] * 2,
        [
            pltpu.VMEM((rows, 3 * mine), bf16),
            pltpu.VMEM((rows, 3 * mine), bf16),
            pltpu.VMEM((n_tm, 3, each, mine), f32),
            pltpu.VMEM((chips, 3 * SUB, mine), f32),
            pltpu.VMEM((rows, wide), f32),
            pltpu.VMEM((rows, chans), f32),
            pltpu.VMEM((2, rows // 2, chans), f32),
        ],
        cosines,
        sines,
        local,
        xt,
        weights,
        weight,
        *got,
    )

    pieces = kept + swap(sent, "tm", 1)
    others = [swap(pieces[j], "freq", j) for j in range(1, n_freq)]
    others[0], blocks[0] = lax.optimization_barrier((others[0], blocks[0]))
    total = blocks[0]
    for d in range(chips - 1, 0, -1):
        total = total + swap(blocks[d], "tm", 2 * d)
    result = pieces[0]
    for other in others:
        result = result + other
    grad_increments = result.reshape(steps // n_freq, batch, chans)

    here, away = total[0], swap(total[1], "tm", 1)
    even = lax.axis_index("tm") & 1 == 0
    low, high = jnp.where(even, here, away), jnp.where(even, away, here)
    grad_projections = jnp.transpose(jnp.concatenate([low, high], axis=-1), (1, 0, 2))
    return (grad_increments, grad_projections)


def solution(mesh):
    placed = (P("tm", None, None), P(None, None, "freq"), P(None, "freq"), P())
    return jax.shard_map(
        on_device,
        mesh=mesh,
        in_specs=placed,
        out_specs=(P(("tm", "freq"), None, None), P("tm", None, "freq")),
        check_vma=False,
    )
```

```python
import math

import jax
import jax.numpy as jnp
from jax import lax
from jax.experimental import pallas as pl
from jax.experimental.pallas import tpu as pltpu
from jax.sharding import PartitionSpec as P

f32, bf16 = jnp.float32, jnp.bfloat16
SUB = 8
HALF = SUB // 2
WIDE = 256
MAGIC = 12582912.0
SIN = (3.141582022150658, -5.167142796368909, 2.541899027590427, -0.5546361970970186)
COS = (
    0.9999999534666683,
    -4.934792858675264,
    4.058411914167107,
    -1.3318801612488937,
    0.2196967986036905,
)
NT = (((1,), (1,)), ((), ()))
PARAMS = pltpu.CompilerParams(vmem_limit_bytes=20 * 1024 * 1024)
VECTORS = pl.BlockSpec(memory_space=pltpu.VMEM)
STAY = pl.BlockSpec(memory_space=pltpu.HBM)


def horner(z, coefs):
    acc = z * coefs[-1] + coefs[-2]
    for coef in coefs[-3::-1]:
        acc = acc * z + coef
    return acc


def split(value):
    high = value.astype(bf16)
    return high, (value - high.astype(f32)).astype(bf16)


def pair_rows(low, high):
    top = lax.broadcasted_iota(jnp.int32, low.shape, 0) < HALF
    first = jnp.where(top, low, pltpu.roll(high, HALF, 0))
    second = jnp.where(top, pltpu.roll(low, HALF, 0), high)
    return first, second


def tile(i, count=1):
    return pl.ds(pl.multiple_of(i * (count * SUB), count * SUB), count * SUB)


def tall(first, second):
    return jnp.concatenate([first, second], axis=0)


def call(body, name, micros, ins, outs, scratch, *operands):
    return pl.pallas_call(
        body,
        in_specs=ins,
        out_specs=[VECTORS] * len(outs),
        out_shape=outs,
        scratch_shapes=scratch,
        compiler_params=PARAMS,
        cost_estimate=pl.CostEstimate(
            flops=int(micros * 1.1e9), bytes_accessed=int(micros * 3e6), transcendentals=0
        ),
        name=name,
    )(*operands)


def prepare_kernel(x_hbm, p_hbm, ph_hbm, g_hbm, x_ref, w_ref, r_ref, weight_ref, *rest):
    p_ref, ph_ref, g_ref, sems = rest
    chunks, _, chans, wide = p_ref.shape
    batch = g_ref.shape[0]
    core = lax.axis_index("tm") & 1
    inv = 1.0 / (2.0 * math.pi)

    def columns(chunk):
        return pl.ds(pl.multiple_of((core * chunks + chunk) * wide, wide), wide)

    fetch = [pltpu.make_async_copy(ph_hbm, ph_ref, sems.at[0])]
    for k in range(chunks):
        fetch.append(
            pltpu.make_async_copy(p_hbm.at[:, :, columns(k)], p_ref.at[k], sems.at[1 + k])
        )
    fetch_x = pltpu.make_async_copy(x_hbm, x_ref, sems.at[1 + chunks])
    fetch_g = pltpu.make_async_copy(g_hbm, g_ref, sems.at[2 + chunks])
    for copy in fetch + [fetch_x, fetch_g]:
        copy.start()
    fetch[0].wait()
    row = lax.broadcasted_iota(jnp.int32, (chans, wide), 0)
    for chunk in range(chunks):
        fetch[1 + chunk].wait()
        for level in range(3):
            cols = slice((3 * chunk + level) * wide, (3 * chunk + level + 1) * wide)
            high, low = split(p_ref[chunk, level])
            w_ref[:chans, cols] = high
            w_ref[chans:, cols] = low
            high, low = split(p_ref[chunk, level] * inv)
            phase = ph_ref[level : level + 1, columns(chunk)] * inv
            phase0 = phase.astype(bf16).astype(f32)
            phase1 = (phase - phase0).astype(bf16).astype(f32)
            phase2 = phase - phase0 - phase1
            extra = jnp.where(row == 0, phase0, jnp.where(row == 1, phase1, phase2))
            extra = jnp.where(row < 3, extra, 0.0).astype(bf16)
            for k, part in enumerate((high, high, low, extra)):
                r_ref[chans * k : chans * (k + 1), cols] = part
    fetch_g.wait()
    row = lax.broadcasted_iota(jnp.int32, weight_ref.shape, 0)
    weight = jnp.zeros(weight_ref.shape, f32)
    for b in range(batch):
        value = jnp.where(g_ref[b] == 1, 2.0 / batch, -2.0 / batch)
        weight = jnp.where(row == b, value, weight)
    weight_ref[...] = weight
    fetch_x.wait()


def turn_kernel(flat_ref, xt_ref):
    chans = flat_ref.shape[1]
    high, low = split(flat_ref[...].T)
    xt_ref[:chans, :] = high
    xt_ref[chans:, :] = low


def waves_kernel(amplitude, wide, x_ref, y_ref, r_ref, *rest):
    c_ref, half_ref, z_ref, loc_ref, snd_ref, flat_ref, xs_ref, ang0_ref, ang1_ref = rest
    rows, chans = flat_ref.shape
    chunks = c_ref.shape[0]
    core = lax.axis_index("tm") & 1
    root = math.sqrt(2.0 * amplitude)
    sin_coefs = [root * coef for coef in SIN]
    lane = lax.broadcasted_iota(jnp.int32, (2 * SUB, chans), 1)
    ones = jnp.where(lane < 3, 1.0, 0.0).astype(bf16)

    def pairs(even_ref, odd_ref):
        def one(k, _):
            both = tall(*pair_rows(even_ref[tile(k), :], odd_ref[tile(k), :]))
            flat_ref[tile(k, 2), :] = both
            high, low = split(both)
            xs_ref[tile(k, 2), :] = jnp.concatenate([high, low, high, ones], axis=1)
            return 0

        lax.fori_loop(0, rows // (2 * SUB), one, 0, unroll=8)

    @pl.when(core == 0)
    def _():
        pairs(x_ref, y_ref)

    @pl.when(core == 1)
    def _():
        pairs(y_ref, x_ref)

    block = ang0_ref.shape[0]
    blocks = rows // block

    def turns(item, ang_ref):
        at = pl.ds(pl.multiple_of(lax.rem(item, blocks) * block, block), block)
        cols = pl.ds(pl.multiple_of(lax.div(item, blocks) * (3 * wide), 3 * wide), 3 * wide)
        ang_ref[...] = jnp.dot(xs_ref[at, :], r_ref[:, cols], preferred_element_type=f32)

    def sums_over(chunk, base, ang_ref, carry):
        for k in range(block // SUB):
            s0, s1, s2, s01, s12, s012 = carry
            at = pl.ds(pl.multiple_of(base + k * SUB, SUB), SUB)
            cosines = []
            for level in range(3):
                turn = ang_ref[k * SUB : (k + 1) * SUB, level * wide : (level + 1) * wide]
                r = turn - ((turn + MAGIC) - MAGIC)
                z = r * r
                sine = r * horner(z, sin_coefs)
                wave = amplitude - sine * sine
                c_ref[chunk, level, at, :] = wave
                half_ref[chunk, level, at, :] = sine
                z_ref[chunk, level, at, :] = z
                cosines.append(wave)
            c0, c1, c2 = cosines
            s012 = s012 + s01 * c2
            s12 = s12 + s1 * c2
            s01 = s01 + s0 * c1
            carry = (s0 + c0, s1 + c1, s2 + c2, s01, s12, s012)
        return carry

    zero = jnp.zeros((SUB, wide), f32)
    turns(jnp.int32(0), ang0_ref)
    for chunk in range(chunks):
        here = slice(chunk * wide, (chunk + 1) * wide)

        def step(i, carry):
            item = chunk * blocks + 2 * i
            turns(item + 1, ang1_ref)
            carry = sums_over(chunk, 2 * i * block, ang0_ref, carry)
            turns(jnp.minimum(item + 2, chunks * blocks - 1), ang0_ref)
            return sums_over(chunk, (2 * i + 1) * block, ang1_ref, carry)

        sums = lax.fori_loop(0, blocks // 2, step, (zero,) * 6)
        for k in range(6):
            loc_ref[SUB * k : SUB * (k + 1), here] = sums[k]
        a0, a1, a2, a01, a12, a012 = [v[:HALF] for v in sums]
        b0, b1, b2, b01, b12, b012 = [v[HALF:] for v in sums]
        both = (
            a0 + b0,
            a1 + b1,
            a2 + b2,
            a01 + b01 + a0 * b1,
            a12 + b12 + a1 * b2,
            a012 + b012 + a0 * b12 + a01 * b2,
        )
        for k in range(6):
            snd_ref[HALF * k : HALF * (k + 1), here] = both[k]


def sines_kernel(amplitude, chunk, half_ref, z_ref, s_ref):
    levels, rows, _ = s_ref.shape
    coefs = [-math.sqrt(2.0 * amplitude) * coef for coef in COS]
    for level in range(levels):

        def step(i, _):
            value = horner(z_ref[chunk, level, tile(i), :], coefs)
            s_ref[level, tile(i), :] = half_ref[chunk, level, tile(i), :] * value
            return 0

        lax.fori_loop(0, rows // SUB, step, 0, unroll=16)


def parts_of(ref):
    return [ref[HALF * k : HALF * (k + 1), :] for k in range(6)]


def chain(early, late):
    a0, a1, a2, a01, a12, a012 = early
    b0, b1, b2, b01, b12, b012 = late
    return (
        a0 + b0,
        a1 + b1,
        a2 + b2,
        a01 + b01 + a0 * b1,
        a12 + b12 + a1 * b2,
        a012 + b012 + a0 * b12 + a01 * b2,
    )


def ordered(flag, mine, other):
    early = [jnp.where(flag, b, a) for a, b in zip(mine, other)]
    late = [jnp.where(flag, a, b) for a, b in zip(mine, other)]
    return early, late


def chain_kernel(bit, own_ref, other_ref, out_ref):
    flag = (lax.axis_index("tm") >> 1) & bit != 0
    both = chain(*ordered(flag, parts_of(own_ref), parts_of(other_ref)))
    for k in range(6):
        out_ref[HALF * k : HALF * (k + 1), :] = both[k]


def compose(loc_ref, weight_ref, own_ref, got):
    chip = lax.axis_index("tm") >> 1
    weight = weight_ref[:HALF]
    zero = jnp.zeros(weight.shape, f32)
    own = parts_of(own_ref)
    before, after = [zero] * 6, [zero] * 6
    for k, ref in enumerate(got):
        other = parts_of(ref)
        flag = chip & (1 << k) != 0
        first = [jnp.where(flag, v, 0.0) for v in other]
        second = [jnp.where(flag, 0.0, v) for v in other]
        before = chain(first, before)
        after = chain(after, second)
    p0, p1, p2, p01, p12, p012 = before
    e1, e2 = p0, p01
    _, t1, t2, _, t12, _ = after
    whole = chain(chain(before, own), after)
    totals = (whole[0], whole[3], whole[5])
    seeds = [2.0 * weight * jnp.sum(weight * total, axis=0, keepdims=True) for total in totals]

    def local(k):
        value = loc_ref[SUB * k : SUB * (k + 1), :]
        return value[:HALF], value[HALF:]

    a0, _ = local(0)
    a1, b1 = local(1)
    _, b2 = local(2)
    a01, _ = local(3)
    _, b12 = local(4)
    d0, d1, d2 = [tall(seed, seed) for seed in seeds]
    tail2 = tall(t2 + b2, t2)
    tail1 = tall(t1 + b1, t1)
    tail12 = tall(t12 + b12 + b1 * t2, t12)
    return (
        d2,
        tall(e1, e1 + a0),
        tall(e2, e2 + a01 + e1 * a1),
        d1 + d2 * tail2,
        d0 + d1 * tail1 + d2 * tail12,
    )


def slopes(chunk, wide, starts, c_ref, s_ref, u1_ref, sh_ref, sl_ref):
    rows = u1_ref.shape[0]
    scale, front1, front2, adjoint1, adjoint0 = [
        v[:, chunk * wide : (chunk + 1) * wide] for v in starts
    ]

    def keep(pair, level, values):
        high, low = split(tall(*values))
        at = (3 * chunk + level) * wide
        sh_ref[tile(pair, 2), at : at + wide] = high
        sl_ref[tile(pair, 2), at : at + wide] = low

    def fwd(pair, carry):
        f1, f2 = carry
        slope2 = []
        for which in range(2):
            at = tile(2 * pair + which)
            u1_ref[at, :] = s_ref[1, at, :] * f1
            slope2.append(s_ref[2, at, :] * (scale * f2))
            f2 = f2 + f1 * c_ref[chunk, 1, at, :]
            f1 = f1 + c_ref[chunk, 0, at, :]
        keep(pair, 2, slope2)
        return f1, f2

    lax.fori_loop(0, rows // (2 * SUB), fwd, (front1, front2), unroll=8)

    def bwd(step, carry):
        g1, g0 = carry
        pair = rows // (2 * SUB) - 1 - step
        slope0, slope1 = [], []
        for which in (1, 0):
            at = tile(2 * pair + which)
            slope1.append(u1_ref[at, :] * g1)
            slope0.append(s_ref[0, at, :] * g0)
            g0 = g0 + g1 * c_ref[chunk, 1, at, :]
            g1 = g1 + scale * c_ref[chunk, 2, at, :]
        keep(pair, 0, slope0[::-1])
        keep(pair, 1, slope1[::-1])
        return g1, g0

    lax.fori_loop(0, rows // (2 * SUB), bwd, (adjoint1, adjoint0), unroll=8)


def grads_kernel(sizes, c_ref, loc_ref, xt_ref, w_ref, weight_ref, *refs):
    n_tm, n_freq, wide, levels = sizes
    chunks = c_ref.shape[0]
    sines, refs = refs[:chunks], refs[chunks:]
    own_ref, got, refs = refs[0], refs[1 : 1 + levels], refs[1 + levels :]
    blocks, refs = refs[: n_tm // 2], refs[n_tm // 2 :]
    gk_ref, gs_ref, sh_ref, sl_ref, gp_ref, u1_ref, acc_ref, flat_ref = refs
    rows, chans = acc_ref.shape
    each = chans // n_tm
    me = lax.axis_index("tm")
    core, z = me & 1, lax.axis_index("freq")

    starts = compose(loc_ref, weight_ref, own_ref, got)
    for chunk, s_ref in enumerate(sines):
        slopes(chunk, wide, starts, c_ref, s_ref, u1_ref, sh_ref, sl_ref)

    main = jnp.dot(xt_ref[...], sh_ref[...], preferred_element_type=f32)
    rest = jnp.dot(xt_ref[:chans, :], sl_ref[...], preferred_element_type=f32)
    grad = main[:chans] + main[chans:] + rest
    for chunk in range(c_ref.shape[0]):
        for level in range(3):
            at = (3 * chunk + level) * wide
            for d in range(n_tm):
                gp_ref[d, level, :, chunk * wide : (chunk + 1) * wide] = grad[
                    each * d : each * (d + 1), at : at + wide
                ]
    for d in range(n_tm):
        blocks[d // 2][d % 2] = gp_ref[jnp.bitwise_xor(me, d)]

    main = lax.dot_general(sh_ref[...], w_ref[...], NT, preferred_element_type=f32)
    rest = lax.dot_general(sl_ref[...], w_ref[:chans, :], NT, preferred_element_type=f32)
    acc_ref[...] = main[:, :chans] + main[:, chans:] + rest

    def one(k, _):
        even, odd = pair_rows(acc_ref[tile(2 * k), :], acc_ref[tile(2 * k + 1), :])
        flat_ref[0, tile(k), :] = even
        flat_ref[1, tile(k), :] = odd
        return 0

    lax.fori_loop(0, rows // (2 * SUB), one, 0, unroll=8)
    piece = rows // 2 // n_freq
    for j in range(n_freq):
        at = pl.ds(pl.multiple_of(jnp.bitwise_xor(z, j) * piece, piece), piece)
        gk_ref[j] = flat_ref[core, at, :]
        gs_ref[j] = flat_ref[1 - core, at, :]


def swap(value, axis, distance):
    count = lax.axis_size(axis)
    return lax.ppermute(value, axis, [(i, i ^ distance) for i in range(count)])


def resident(value):
    return pltpu.with_memory_space_constraint(value, pltpu.HBM)


def on_device(increments, projections, phases, groups):
    steps, batch, chans = increments.shape
    freqs = phases.shape[1]
    n_tm, n_freq = lax.axis_size("tm"), lax.axis_size("freq")
    amplitude = math.sqrt(2.0 / (steps * n_tm))
    rows = 2 * steps * batch
    mine = freqs // 2
    wide = min(WIDE, mine)
    chunks = mine // wide
    each = chans // n_tm
    chips = n_tm // 2
    x = increments.reshape(rows // 2, chans)
    p = jnp.transpose(projections, (1, 0, 2))
    y = swap(x, "tm", 1)
    x, weights, turns, weight = call(
        prepare_kernel,
        "prepare",
        1.9,
        [STAY] * 4,
        [
            pltpu.VMEM((rows // 2, chans), f32),
            pltpu.VMEM((2 * chans, 3 * mine), bf16),
            pltpu.VMEM((4 * chans, 3 * mine), bf16),
            pltpu.VMEM((SUB, mine), f32),
        ],
        [
            pltpu.VMEM((chunks, 3, chans, wide), f32),
            pltpu.VMEM((3, freqs), f32),
            pltpu.SMEM((batch,), jnp.int32),
            pltpu.SemaphoreType.DMA((3 + chunks,)),
        ],
        resident(x),
        resident(p),
        resident(phases),
        resident(groups),
    )

    def waves_body(*refs):
        waves_kernel(amplitude, wide, *refs)

    big = pltpu.VMEM((chunks, 3, rows, wide), f32)
    cosines, halves, squares, local, own, flat = call(
        waves_body,
        "waves",
        8.0,
        [VECTORS] * 3,
        [
            big,
            big,
            big,
            pltpu.VMEM((6 * SUB, mine), f32),
            jax.ShapeDtypeStruct((3 * SUB, mine), f32),
            pltpu.VMEM((rows, chans), f32),
        ],
        [pltpu.VMEM((rows, 4 * chans), bf16)] + [pltpu.VMEM((rows // 4, 3 * wide), f32)] * 2,
        x,
        y,
        turns,
    )
    (xt,) = call(
        turn_kernel, "turn", 0.8, [VECTORS], [pltpu.VMEM((2 * chans, rows), bf16)], [], flat
    )

    def sines_of(chunk):
        def sines_body(*refs):
            sines_kernel(amplitude, chunk, *refs)

        return call(
            sines_body,
            f"sines{chunk}",
            1.2,
            [VECTORS] * 2,
            [pltpu.VMEM((3, rows, wide), f32)],
            [],
            halves,
            squares,
        )[0]

    levels = chips.bit_length() - 1
    got, sines, current = [], [], own
    for k in range(levels):
        other = swap(current, "tm", 2 << k)
        if k < levels - 1:

            def chain_body(*refs, bit=1 << k):
                chain_kernel(bit, *refs)

            if len(sines) < chunks:
                sines.append(sines_of(len(sines)))
                other, sines[-1] = lax.optimization_barrier((other, sines[-1]))
            (current,) = call(
                chain_body,
                "chain",
                0.1,
                [VECTORS] * 2,
                [jax.ShapeDtypeStruct(own.shape, f32)],
                [],
                current,
                other,
            )
            halves, current = lax.optimization_barrier((halves, current))
        got.append(other)
    sines += [sines_of(k) for k in range(len(sines), chunks)]

    def grads_body(*refs):
        grads_kernel((n_tm, n_freq, wide, levels), *refs)

    bshape = jax.ShapeDtypeStruct((2, 3, each, mine), f32)
    gshape = jax.ShapeDtypeStruct((n_freq, rows // 2 // n_freq, chans), f32)
    *blocks, kept, sent = call(
        grads_body,
        "grads",
        6.0,
        [VECTORS] * (6 + chunks + levels),
        [bshape] * chips + [gshape] * 2,
        [
            pltpu.VMEM((rows, 3 * mine), bf16),
            pltpu.VMEM((rows, 3 * mine), bf16),
            pltpu.VMEM((n_tm, 3, each, mine), f32),
            pltpu.VMEM((rows, wide), f32),
            pltpu.VMEM((rows, chans), f32),
            pltpu.VMEM((2, rows // 2, chans), f32),
        ],
        cosines,
        local,
        xt,
        weights,
        weight,
        *sines,
        own,
        *got,
    )

    pieces = kept + swap(sent, "tm", 1)
    others = [swap(pieces[j], "freq", j) for j in range(1, n_freq)]
    others[0], blocks[0] = lax.optimization_barrier((others[0], blocks[0]))
    total = blocks[0]
    for d in range(chips - 1, 0, -1):
        total = total + swap(blocks[d], "tm", 2 * d)
    result = pieces[0]
    for other in others:
        result = result + other
    grad_increments = result.reshape(steps // n_freq, batch, chans)

    here, away = total[0], swap(total[1], "tm", 1)
    even = lax.axis_index("tm") & 1 == 0
    low, high = jnp.where(even, here, away), jnp.where(even, away, here)
    grad_projections = jnp.transpose(jnp.concatenate([low, high], axis=-1), (1, 0, 2))
    return (grad_increments, grad_projections)


def solution(mesh):
    placed = (P("tm", None, None), P(None, None, "freq"), P(None, "freq"), P())
    return jax.shard_map(
        on_device,
        mesh=mesh,
        in_specs=placed,
        out_specs=(P(("tm", "freq"), None, None), P("tm", None, "freq")),
        check_vma=False,
    )
```

```python
import math

import jax
import jax.numpy as jnp
from jax import lax
from jax.experimental import pallas as pl
from jax.experimental.pallas import tpu as pltpu
from jax.sharding import PartitionSpec as P

f32, bf16 = jnp.float32, jnp.bfloat16
SUB = 8
HALF = SUB // 2
WIDE = 256
MAGIC = 12582912.0
SIN = (3.141582022150658, -5.167142796368909, 2.541899027590427, -0.5546361970970186)
COS = (
    0.9999999534666683,
    -4.934792858675264,
    4.058411914167107,
    -1.3318801612488937,
    0.2196967986036905,
)
NT = (((1,), (1,)), ((), ()))
PARAMS = pltpu.CompilerParams(vmem_limit_bytes=20 * 1024 * 1024)
VECTORS = pl.BlockSpec(memory_space=pltpu.VMEM)
STAY = pl.BlockSpec(memory_space=pltpu.HBM)


def horner(z, coefs):
    acc = z * coefs[-1] + coefs[-2]
    for coef in coefs[-3::-1]:
        acc = acc * z + coef
    return acc


def split(value):
    high = value.astype(bf16)
    return high, (value - high.astype(f32)).astype(bf16)


def pair_rows(low, high):
    top = lax.broadcasted_iota(jnp.int32, low.shape, 0) < HALF
    first = jnp.where(top, low, pltpu.roll(high, HALF, 0))
    second = jnp.where(top, pltpu.roll(low, HALF, 0), high)
    return first, second


def tile(i, count=1):
    return pl.ds(pl.multiple_of(i * (count * SUB), count * SUB), count * SUB)


def tall(first, second):
    return jnp.concatenate([first, second], axis=0)


def call(body, name, micros, ins, outs, scratch, *operands):
    return pl.pallas_call(
        body,
        in_specs=ins,
        out_specs=[VECTORS] * len(outs),
        out_shape=outs,
        scratch_shapes=scratch,
        compiler_params=PARAMS,
        cost_estimate=pl.CostEstimate(
            flops=int(micros * 1.1e9), bytes_accessed=int(micros * 3e6), transcendentals=0
        ),
        name=name,
    )(*operands)


def prepare_kernel(x_hbm, p_hbm, ph_hbm, g_hbm, x_ref, w_ref, r_ref, weight_ref, *rest):
    p_ref, ph_ref, g_ref, sems = rest
    chunks, _, chans, wide = p_ref.shape
    batch = g_ref.shape[0]
    core = lax.axis_index("tm") & 1
    inv = 1.0 / (2.0 * math.pi)

    def columns(chunk):
        return pl.ds(pl.multiple_of((core * chunks + chunk) * wide, wide), wide)

    fetch = [pltpu.make_async_copy(ph_hbm, ph_ref, sems.at[0])]
    for k in range(chunks):
        fetch.append(
            pltpu.make_async_copy(p_hbm.at[:, :, columns(k)], p_ref.at[k], sems.at[1 + k])
        )
    fetch_x = pltpu.make_async_copy(x_hbm, x_ref, sems.at[1 + chunks])
    fetch_g = pltpu.make_async_copy(g_hbm, g_ref, sems.at[2 + chunks])
    for copy in fetch + [fetch_x, fetch_g]:
        copy.start()
    fetch[0].wait()
    row = lax.broadcasted_iota(jnp.int32, (chans, wide), 0)
    for chunk in range(chunks):
        fetch[1 + chunk].wait()
        for level in range(3):
            cols = slice((3 * chunk + level) * wide, (3 * chunk + level + 1) * wide)
            high, low = split(p_ref[chunk, level])
            w_ref[:chans, cols] = high
            w_ref[chans:, cols] = low
            high, low = split(p_ref[chunk, level] * inv)
            phase = ph_ref[level : level + 1, columns(chunk)] * inv
            phase0 = phase.astype(bf16).astype(f32)
            phase1 = (phase - phase0).astype(bf16).astype(f32)
            phase2 = phase - phase0 - phase1
            extra = jnp.where(row == 0, phase0, jnp.where(row == 1, phase1, phase2))
            extra = jnp.where(row < 3, extra, 0.0).astype(bf16)
            for k, part in enumerate((high, high, low, extra)):
                r_ref[chans * k : chans * (k + 1), cols] = part
    fetch_g.wait()
    row = lax.broadcasted_iota(jnp.int32, weight_ref.shape, 0)
    weight = jnp.zeros(weight_ref.shape, f32)
    for b in range(batch):
        value = jnp.where(g_ref[b] == 1, 2.0 / batch, -2.0 / batch)
        weight = jnp.where(row == b, value, weight)
    weight_ref[...] = weight
    fetch_x.wait()


def turn_kernel(flat_ref, xt_ref):
    chans = flat_ref.shape[1]
    high, low = split(flat_ref[...].T)
    xt_ref[:chans, :] = high
    xt_ref[chans:, :] = low


def waves_kernel(amplitude, wide, x_ref, y_ref, r_ref, *rest):
    c_ref, half_ref, z_ref, loc_ref, snd_ref, flat_ref, xs_ref, ang0_ref, ang1_ref = rest
    rows, chans = flat_ref.shape
    chunks = c_ref.shape[0]
    core = lax.axis_index("tm") & 1
    root = math.sqrt(2.0 * amplitude)
    sin_coefs = [root * coef for coef in SIN]
    lane = lax.broadcasted_iota(jnp.int32, (2 * SUB, chans), 1)
    ones = jnp.where(lane < 3, 1.0, 0.0).astype(bf16)

    def pairs(even_ref, odd_ref):
        def one(k, _):
            both = tall(*pair_rows(even_ref[tile(k), :], odd_ref[tile(k), :]))
            flat_ref[tile(k, 2), :] = both
            high, low = split(both)
            xs_ref[tile(k, 2), :] = jnp.concatenate([high, low, high, ones], axis=1)
            return 0

        lax.fori_loop(0, rows // (2 * SUB), one, 0, unroll=8)

    @pl.when(core == 0)
    def _():
        pairs(x_ref, y_ref)

    @pl.when(core == 1)
    def _():
        pairs(y_ref, x_ref)

    block = ang0_ref.shape[0]
    blocks = rows // block

    def turns(item, ang_ref):
        at = pl.ds(pl.multiple_of(lax.rem(item, blocks) * block, block), block)
        cols = pl.ds(pl.multiple_of(lax.div(item, blocks) * (3 * wide), 3 * wide), 3 * wide)
        ang_ref[...] = jnp.dot(xs_ref[at, :], r_ref[:, cols], preferred_element_type=f32)

    def sums_over(chunk, base, ang_ref, carry):
        for k in range(block // SUB):
            s0, s1, s2, s01, s12, s012 = carry
            at = pl.ds(pl.multiple_of(base + k * SUB, SUB), SUB)
            cosines = []
            for level in range(3):
                turn = ang_ref[k * SUB : (k + 1) * SUB, level * wide : (level + 1) * wide]
                r = turn - ((turn + MAGIC) - MAGIC)
                z = r * r
                sine = r * horner(z, sin_coefs)
                wave = amplitude - sine * sine
                c_ref[chunk, level, at, :] = wave
                half_ref[chunk, level, at, :] = sine
                z_ref[chunk, level, at, :] = z
                cosines.append(wave)
            c0, c1, c2 = cosines
            s012 = s012 + s01 * c2
            s12 = s12 + s1 * c2
            s01 = s01 + s0 * c1
            carry = (s0 + c0, s1 + c1, s2 + c2, s01, s12, s012)
        return carry

    zero = jnp.zeros((SUB, wide), f32)
    turns(jnp.int32(0), ang0_ref)
    for chunk in range(chunks):
        here = slice(chunk * wide, (chunk + 1) * wide)

        def step(i, carry):
            item = chunk * blocks + 2 * i
            turns(item + 1, ang1_ref)
            carry = sums_over(chunk, 2 * i * block, ang0_ref, carry)
            turns(jnp.minimum(item + 2, chunks * blocks - 1), ang0_ref)
            return sums_over(chunk, (2 * i + 1) * block, ang1_ref, carry)

        sums = lax.fori_loop(0, blocks // 2, step, (zero,) * 6)
        for k in range(6):
            loc_ref[SUB * k : SUB * (k + 1), here] = sums[k]
        a0, a1, a2, a01, a12, a012 = [v[:HALF] for v in sums]
        b0, b1, b2, b01, b12, b012 = [v[HALF:] for v in sums]
        both = (
            a0 + b0,
            a1 + b1,
            a2 + b2,
            a01 + b01 + a0 * b1,
            a12 + b12 + a1 * b2,
            a012 + b012 + a0 * b12 + a01 * b2,
        )
        for k in range(6):
            snd_ref[HALF * k : HALF * (k + 1), here] = both[k]


def sines_kernel(amplitude, half_ref, z_ref, s_ref):
    chunks, levels, rows, _ = s_ref.shape
    coefs = [-math.sqrt(2.0 * amplitude) * coef for coef in COS]
    for chunk in range(chunks):
        for level in range(levels):

            def step(i, _):
                value = horner(z_ref[chunk, level, tile(i), :], coefs)
                s_ref[chunk, level, tile(i), :] = half_ref[chunk, level, tile(i), :] * value
                return 0

            lax.fori_loop(0, rows // SUB, step, 0, unroll=16)


def parts_of(ref):
    return [ref[HALF * k : HALF * (k + 1), :] for k in range(6)]


def chain(early, late):
    a0, a1, a2, a01, a12, a012 = early
    b0, b1, b2, b01, b12, b012 = late
    return (
        a0 + b0,
        a1 + b1,
        a2 + b2,
        a01 + b01 + a0 * b1,
        a12 + b12 + a1 * b2,
        a012 + b012 + a0 * b12 + a01 * b2,
    )


def ordered(flag, mine, other):
    early = [jnp.where(flag, b, a) for a, b in zip(mine, other)]
    late = [jnp.where(flag, a, b) for a, b in zip(mine, other)]
    return early, late


def compose(loc_ref, weight_ref, own_ref, got):
    chip = lax.axis_index("tm") >> 1
    weight = weight_ref[:HALF]
    zero = jnp.zeros(weight.shape, f32)
    blocks = [parts_of(ref) for ref in (own_ref, *got)]
    before, after = [zero] * 6, [zero] * 6
    for k in range(len(got).bit_length()):
        other = blocks[1]
        flag = chip & (1 << k) != 0
        first = [jnp.where(flag, v, 0.0) for v in other]
        second = [jnp.where(flag, 0.0, v) for v in other]
        before = chain(first, before)
        after = chain(after, second)
        blocks = [chain(*ordered(flag, a, b)) for a, b in zip(blocks[::2], blocks[1::2])]
    p0, p1, p2, p01, p12, p012 = before
    e1, e2 = p0, p01
    _, t1, t2, _, t12, _ = after
    whole = blocks[0]
    totals = (whole[0], whole[3], whole[5])
    seeds = [2.0 * weight * jnp.sum(weight * total, axis=0, keepdims=True) for total in totals]

    def local(k):
        value = loc_ref[SUB * k : SUB * (k + 1), :]
        return value[:HALF], value[HALF:]

    a0, _ = local(0)
    a1, b1 = local(1)
    _, b2 = local(2)
    a01, _ = local(3)
    _, b12 = local(4)
    d0, d1, d2 = [tall(seed, seed) for seed in seeds]
    tail2 = tall(t2 + b2, t2)
    tail1 = tall(t1 + b1, t1)
    tail12 = tall(t12 + b12 + b1 * t2, t12)
    return (
        d2,
        tall(e1, e1 + a0),
        tall(e2, e2 + a01 + e1 * a1),
        d1 + d2 * tail2,
        d0 + d1 * tail1 + d2 * tail12,
    )


def slopes(chunk, wide, starts, c_ref, s_ref, u1_ref, sh_ref, sl_ref):
    rows = u1_ref.shape[0]
    scale, front1, front2, adjoint1, adjoint0 = [
        v[:, chunk * wide : (chunk + 1) * wide] for v in starts
    ]

    def keep(pair, level, values):
        high, low = split(tall(*values))
        at = (3 * chunk + level) * wide
        sh_ref[tile(pair, 2), at : at + wide] = high
        sl_ref[tile(pair, 2), at : at + wide] = low

    def fwd(pair, carry):
        f1, f2 = carry
        slope2 = []
        for which in range(2):
            at = tile(2 * pair + which)
            u1_ref[at, :] = s_ref[chunk, 1, at, :] * f1
            slope2.append(s_ref[chunk, 2, at, :] * (scale * f2))
            f2 = f2 + f1 * c_ref[chunk, 1, at, :]
            f1 = f1 + c_ref[chunk, 0, at, :]
        keep(pair, 2, slope2)
        return f1, f2

    lax.fori_loop(0, rows // (2 * SUB), fwd, (front1, front2), unroll=8)

    def bwd(step, carry):
        g1, g0 = carry
        pair = rows // (2 * SUB) - 1 - step
        slope0, slope1 = [], []
        for which in (1, 0):
            at = tile(2 * pair + which)
            slope1.append(u1_ref[at, :] * g1)
            slope0.append(s_ref[chunk, 0, at, :] * g0)
            g0 = g0 + g1 * c_ref[chunk, 1, at, :]
            g1 = g1 + scale * c_ref[chunk, 2, at, :]
        keep(pair, 0, slope0[::-1])
        keep(pair, 1, slope1[::-1])
        return g1, g0

    lax.fori_loop(0, rows // (2 * SUB), bwd, (adjoint1, adjoint0), unroll=8)


def increments_kernel(sizes, c_ref, s_ref, loc_ref, w_ref, weight_ref, own_ref, *refs):
    chips, n_freq, wide = sizes
    got, refs = refs[: chips - 1], refs[chips - 1 :]
    gk_ref, gs_ref, sh_ref, sl_ref, u1_ref, acc_ref, flat_ref = refs
    rows, chans = acc_ref.shape
    core, z = lax.axis_index("tm") & 1, lax.axis_index("freq")
    starts = compose(loc_ref, weight_ref, own_ref, got)
    for chunk in range(c_ref.shape[0]):
        slopes(chunk, wide, starts, c_ref, s_ref, u1_ref, sh_ref, sl_ref)

    main = lax.dot_general(sh_ref[...], w_ref[...], NT, preferred_element_type=f32)
    rest = lax.dot_general(sl_ref[...], w_ref[:chans, :], NT, preferred_element_type=f32)
    acc_ref[...] = main[:, :chans] + main[:, chans:] + rest

    def one(k, _):
        even, odd = pair_rows(acc_ref[tile(2 * k), :], acc_ref[tile(2 * k + 1), :])
        flat_ref[0, tile(k), :] = even
        flat_ref[1, tile(k), :] = odd
        return 0

    lax.fori_loop(0, rows // (2 * SUB), one, 0, unroll=8)
    piece = rows // 2 // n_freq
    for j in range(n_freq):
        at = pl.ds(pl.multiple_of(jnp.bitwise_xor(z, j) * piece, piece), piece)
        gk_ref[j] = flat_ref[core, at, :]
        gs_ref[j] = flat_ref[1 - core, at, :]


def frequencies_kernel(sizes, bits, xt_ref, sh_ref, sl_ref, *refs):
    n_tm, wide = sizes
    chips, chunks = n_tm // 2, len(bits)
    blocks, gp_ref = refs[: 2 * chunks], refs[2 * chunks]
    chans = xt_ref.shape[0] // 2
    each = chans // n_tm
    me = lax.axis_index("tm")
    main = jnp.dot(xt_ref[...], sh_ref[...], preferred_element_type=f32)
    rest = jnp.dot(xt_ref[:chans, :], sl_ref[...], preferred_element_type=f32)
    grad = main[:chans] + main[chans:] + rest
    for chunk in range(chunks):
        for level in range(3):
            at = (3 * chunk + level) * wide
            for d in range(n_tm):
                gp_ref[chunk, d, level] = grad[each * d : each * (d + 1), at : at + wide]
        keep_ref, send_ref = blocks[2 * chunk : 2 * chunk + 2]
        bit = bits[chunk]
        for k, j in enumerate([j for j in range(chips) if not j & bit]):
            for side in range(2):
                keep_ref[k, side] = gp_ref[chunk, jnp.bitwise_xor(me, 2 * j + side)]
                send_ref[k, side] = gp_ref[chunk, jnp.bitwise_xor(me, 2 * (j | bit) + side)]


def swap(value, axis, distance):
    count = lax.axis_size(axis)
    return lax.ppermute(value, axis, [(i, i ^ distance) for i in range(count)])


def resident(value):
    return pltpu.with_memory_space_constraint(value, pltpu.HBM)


def on_device(increments, projections, phases, groups):
    steps, batch, chans = increments.shape
    freqs = phases.shape[1]
    n_tm, n_freq = lax.axis_size("tm"), lax.axis_size("freq")
    amplitude = math.sqrt(2.0 / (steps * n_tm))
    rows = 2 * steps * batch
    mine = freqs // 2
    wide = min(WIDE, mine)
    chunks = mine // wide
    each = chans // n_tm
    chips = n_tm // 2
    x = increments.reshape(rows // 2, chans)
    p = jnp.transpose(projections, (1, 0, 2))
    y = swap(x, "tm", 1)
    x, weights, turns, weight = call(
        prepare_kernel,
        "prepare",
        1.9,
        [STAY] * 4,
        [
            pltpu.VMEM((rows // 2, chans), f32),
            pltpu.VMEM((2 * chans, 3 * mine), bf16),
            pltpu.VMEM((4 * chans, 3 * mine), bf16),
            pltpu.VMEM((SUB, mine), f32),
        ],
        [
            pltpu.VMEM((chunks, 3, chans, wide), f32),
            pltpu.VMEM((3, freqs), f32),
            pltpu.SMEM((batch,), jnp.int32),
            pltpu.SemaphoreType.DMA((3 + chunks,)),
        ],
        resident(x),
        resident(p),
        resident(phases),
        resident(groups),
    )

    def waves_body(*refs):
        waves_kernel(amplitude, wide, *refs)

    big = pltpu.VMEM((chunks, 3, rows, wide), f32)
    cosines, halves, squares, local, own, flat = call(
        waves_body,
        "waves",
        8.0,
        [VECTORS] * 3,
        [
            big,
            big,
            big,
            pltpu.VMEM((6 * SUB, mine), f32),
            jax.ShapeDtypeStruct((3 * SUB, mine), f32),
            pltpu.VMEM((rows, chans), f32),
        ],
        [pltpu.VMEM((rows, 4 * chans), bf16)] + [pltpu.VMEM((rows // 4, 3 * wide), f32)] * 2,
        x,
        y,
        turns,
    )
    (xt,) = call(
        turn_kernel, "turn", 0.8, [VECTORS], [pltpu.VMEM((2 * chans, rows), bf16)], [], flat
    )

    def sines_body(*refs):
        sines_kernel(amplitude, *refs)

    got = [swap(own, "tm", 2 * d) for d in range(1, chips)]
    (sines,) = call(sines_body, "sines", 2.4, [VECTORS] * 2, [big], [], halves, squares)

    def increments_body(*refs):
        increments_kernel((chips, n_freq, wide), *refs)

    gshape = jax.ShapeDtypeStruct((n_freq, rows // 2 // n_freq, chans), f32)
    kept, sent, high, low = call(
        increments_body,
        "increments",
        3.8,
        [VECTORS] * (5 + chips),
        [gshape] * 2 + [pltpu.VMEM((rows, 3 * mine), bf16)] * 2,
        [
            pltpu.VMEM((rows, wide), f32),
            pltpu.VMEM((rows, chans), f32),
            pltpu.VMEM((2, rows // 2, chans), f32),
        ],
        cosines,
        sines,
        local,
        weights,
        weight,
        own,
        *got,
    )

    bits = [1 << k for k in range(chips.bit_length() - 1)]
    orders = [bits if chunk % 2 == 0 else bits[::-1] for chunk in range(chunks)]

    def frequencies_body(*refs):
        frequencies_kernel((n_tm, wide), [order[0] for order in orders], *refs)

    bshape = jax.ShapeDtypeStruct((chips // 2, 2, 3, each, wide), f32)
    blocks = call(
        frequencies_body,
        "frequencies",
        1.5,
        [VECTORS] * 3,
        [bshape] * (2 * chunks),
        [pltpu.VMEM((chunks, n_tm, 3, each, wide), f32)],
        xt,
        high,
        low,
    )
    pieces = kept + swap(sent, "tm", 1)
    pieces, *blocks = lax.optimization_barrier((pieces, *blocks))
    others = [swap(pieces[j], "freq", j) for j in range(1, n_freq)]
    result = pieces[0]
    for other in others:
        result = result + other
    grad_increments = result.reshape(steps // n_freq, batch, chans)

    sums = [
        blocks[2 * k] + swap(blocks[2 * k + 1], "tm", 2 * order[0]) for k, order in enumerate(orders)
    ]
    for step in range(1, len(bits)):
        for k, order in enumerate(orders):
            place = sum(1 for bit in order[step:] if bit < order[step])
            halves = sums[k].reshape((-1, 2, 1 << place) + bshape.shape[1:])
            shape = (-1,) + bshape.shape[1:]
            mate = swap(halves[:, 1].reshape(shape), "tm", 2 * order[step])
            sums[k] = halves[:, 0].reshape(shape) + mate
    total = jnp.concatenate([value[0] for value in sums], axis=-1)
    here, away = total[0], swap(total[1], "tm", 1)
    even = lax.axis_index("tm") & 1 == 0
    low, high = jnp.where(even, here, away), jnp.where(even, away, here)
    grad_projections = jnp.transpose(jnp.concatenate([low, high], axis=-1), (1, 0, 2))
    return (grad_increments, grad_projections)


def solution(mesh):
    placed = (P("tm", None, None), P(None, None, "freq"), P(None, "freq"), P())
    return jax.shard_map(
        on_device,
        mesh=mesh,
        in_specs=placed,
        out_specs=(P(("tm", "freq"), None, None), P("tm", None, "freq")),
        check_vma=False,
    )
```

```python
import math

import jax
import jax.numpy as jnp
from jax import lax
from jax.experimental import pallas as pl
from jax.experimental.pallas import tpu as pltpu
from jax.sharding import PartitionSpec as P

f32, bf16 = jnp.float32, jnp.bfloat16
SUB = 8
HALF = SUB // 2
WIDE = 256
MAGIC = 12582912.0
SIN = (3.141582022150658, -5.167142796368909, 2.541899027590427, -0.5546361970970186)
COS = (
    0.9999999534666683,
    -4.934792858675264,
    4.058411914167107,
    -1.3318801612488937,
    0.2196967986036905,
)
NT = (((1,), (1,)), ((), ()))
PARAMS = pltpu.CompilerParams(vmem_limit_bytes=16 * 1024 * 1024)
VECTORS = pl.BlockSpec(memory_space=pltpu.VMEM)
STAY = pl.BlockSpec(memory_space=pltpu.HBM)


def horner(z, coefs):
    acc = z * coefs[-1] + coefs[-2]
    for coef in coefs[-3::-1]:
        acc = acc * z + coef
    return acc


def split(value):
    high = value.astype(bf16)
    return high, (value - high.astype(f32)).astype(bf16)


def pair_rows(low, high):
    top = lax.broadcasted_iota(jnp.int32, low.shape, 0) < HALF
    first = jnp.where(top, low, pltpu.roll(high, HALF, 0))
    second = jnp.where(top, pltpu.roll(low, HALF, 0), high)
    return first, second


def tile(i, count=1):
    return pl.ds(pl.multiple_of(i * (count * SUB), count * SUB), count * SUB)


def tall(first, second):
    return jnp.concatenate([first, second], axis=0)


def call(body, name, micros, ins, outs, scratch, *operands):
    return pl.pallas_call(
        body,
        in_specs=ins,
        out_specs=[VECTORS] * len(outs),
        out_shape=outs,
        scratch_shapes=scratch,
        compiler_params=PARAMS,
        cost_estimate=pl.CostEstimate(
            flops=int(micros * 1.1e9), bytes_accessed=int(micros * 3e6), transcendentals=0
        ),
        name=name,
    )(*operands)


def prepare_kernel(x_hbm, p_hbm, ph_hbm, g_hbm, x_ref, w_ref, r_ref, weight_ref, *rest):
    p_ref, ph_ref, g_ref, sems = rest
    chunks, _, chans, wide = p_ref.shape
    batch = g_ref.shape[0]
    core = lax.axis_index("tm") & 1
    inv = 1.0 / (2.0 * math.pi)

    def columns(chunk):
        return pl.ds(pl.multiple_of((core * chunks + chunk) * wide, wide), wide)

    fetch = [pltpu.make_async_copy(ph_hbm, ph_ref, sems.at[0])]
    for k in range(chunks):
        fetch.append(
            pltpu.make_async_copy(p_hbm.at[:, :, columns(k)], p_ref.at[k], sems.at[1 + k])
        )
    fetch_x = pltpu.make_async_copy(x_hbm, x_ref, sems.at[1 + chunks])
    fetch_g = pltpu.make_async_copy(g_hbm, g_ref, sems.at[2 + chunks])
    for copy in fetch + [fetch_x, fetch_g]:
        copy.start()
    fetch[0].wait()
    row = lax.broadcasted_iota(jnp.int32, (chans, wide), 0)
    for chunk in range(chunks):
        fetch[1 + chunk].wait()
        for level in range(3):
            cols = slice((3 * chunk + level) * wide, (3 * chunk + level + 1) * wide)
            high, low = split(p_ref[chunk, level])
            w_ref[:chans, cols] = high
            w_ref[chans:, cols] = low
            high, low = split(p_ref[chunk, level] * inv)
            phase = ph_ref[level : level + 1, columns(chunk)] * inv
            phase0 = phase.astype(bf16).astype(f32)
            phase1 = (phase - phase0).astype(bf16).astype(f32)
            phase2 = phase - phase0 - phase1
            extra = jnp.where(row == 0, phase0, jnp.where(row == 1, phase1, phase2))
            extra = jnp.where(row < 3, extra, 0.0).astype(bf16)
            for k, part in enumerate((high, high, low, extra)):
                r_ref[chans * k : chans * (k + 1), cols] = part
    fetch_g.wait()
    row = lax.broadcasted_iota(jnp.int32, weight_ref.shape, 0)
    weight = jnp.zeros(weight_ref.shape, f32)
    for b in range(batch):
        value = jnp.where(g_ref[b] == 1, 2.0 / batch, -2.0 / batch)
        weight = jnp.where(row == b, value, weight)
    weight_ref[...] = weight
    fetch_x.wait()


def turn_kernel(flat_ref, xt_ref):
    chans = flat_ref.shape[1]
    high, low = split(flat_ref[...].T)
    xt_ref[:chans, :] = high
    xt_ref[chans:, :] = low


def waves_kernel(amplitude, wide, x_ref, y_ref, r_ref, *rest):
    c_ref, half_ref, z_ref, loc_ref, snd_ref, flat_ref, xs_ref, ang0_ref, ang1_ref = rest
    rows, chans = flat_ref.shape
    chunks = c_ref.shape[0]
    core = lax.axis_index("tm") & 1
    root = math.sqrt(2.0 * amplitude)
    sin_coefs = [root * coef for coef in SIN]
    lane = lax.broadcasted_iota(jnp.int32, (2 * SUB, chans), 1)
    ones = jnp.where(lane < 3, 1.0, 0.0).astype(bf16)

    def pairs(even_ref, odd_ref):
        def one(k, _):
            both = tall(*pair_rows(even_ref[tile(k), :], odd_ref[tile(k), :]))
            flat_ref[tile(k, 2), :] = both
            high, low = split(both)
            xs_ref[tile(k, 2), :] = jnp.concatenate([high, low, high, ones], axis=1)
            return 0

        lax.fori_loop(0, rows // (2 * SUB), one, 0, unroll=8)

    @pl.when(core == 0)
    def _():
        pairs(x_ref, y_ref)

    @pl.when(core == 1)
    def _():
        pairs(y_ref, x_ref)

    block = ang0_ref.shape[0]
    blocks = rows // block

    def turns(item, ang_ref):
        at = pl.ds(pl.multiple_of(lax.rem(item, blocks) * block, block), block)
        cols = pl.ds(pl.multiple_of(lax.div(item, blocks) * (3 * wide), 3 * wide), 3 * wide)
        ang_ref[...] = jnp.dot(xs_ref[at, :], r_ref[:, cols], preferred_element_type=f32)

    def sums_over(chunk, base, ang_ref, carry):
        for k in range(block // SUB):
            s0, s1, s2, s01, s12, s012 = carry
            at = pl.ds(pl.multiple_of(base + k * SUB, SUB), SUB)
            cosines = []
            for level in range(3):
                turn = ang_ref[k * SUB : (k + 1) * SUB, level * wide : (level + 1) * wide]
                r = turn - ((turn + MAGIC) - MAGIC)
                z = r * r
                sine = r * horner(z, sin_coefs)
                wave = amplitude - sine * sine
                c_ref[chunk, level, at, :] = wave
                half_ref[chunk, level, at, :] = sine
                z_ref[chunk, level, at, :] = z
                cosines.append(wave)
            c0, c1, c2 = cosines
            s012 = s012 + s01 * c2
            s12 = s12 + s1 * c2
            s01 = s01 + s0 * c1
            carry = (s0 + c0, s1 + c1, s2 + c2, s01, s12, s012)
        return carry

    zero = jnp.zeros((SUB, wide), f32)
    turns(jnp.int32(0), ang0_ref)
    for chunk in range(chunks):
        here = slice(chunk * wide, (chunk + 1) * wide)

        def step(i, carry):
            item = chunk * blocks + 2 * i
            turns(item + 1, ang1_ref)
            carry = sums_over(chunk, 2 * i * block, ang0_ref, carry)
            turns(jnp.minimum(item + 2, chunks * blocks - 1), ang0_ref)
            return sums_over(chunk, (2 * i + 1) * block, ang1_ref, carry)

        sums = lax.fori_loop(0, blocks // 2, step, (zero,) * 6)
        for k in range(6):
            loc_ref[SUB * k : SUB * (k + 1), here] = sums[k]
        a0, a1, a2, a01, a12, a012 = [v[:HALF] for v in sums]
        b0, b1, b2, b01, b12, b012 = [v[HALF:] for v in sums]
        both = (
            a0 + b0,
            a1 + b1,
            a2 + b2,
            a01 + b01 + a0 * b1,
            a12 + b12 + a1 * b2,
            a012 + b012 + a0 * b12 + a01 * b2,
        )
        for k in range(6):
            snd_ref[HALF * k : HALF * (k + 1), here] = both[k]


def sines_kernel(amplitude, half_ref, z_ref, s_ref):
    chunks, levels, rows, _ = s_ref.shape
    coefs = [-math.sqrt(2.0 * amplitude) * coef for coef in COS]
    for chunk in range(chunks):
        for level in range(levels):

            def step(i, _):
                value = horner(z_ref[chunk, level, tile(i), :], coefs)
                s_ref[chunk, level, tile(i), :] = half_ref[chunk, level, tile(i), :] * value
                return 0

            lax.fori_loop(0, rows // SUB, step, 0, unroll=16)


def parts_of(ref):
    return [ref[HALF * k : HALF * (k + 1), :] for k in range(6)]


def chain(early, late):
    a0, a1, a2, a01, a12, a012 = early
    b0, b1, b2, b01, b12, b012 = late
    return (
        a0 + b0,
        a1 + b1,
        a2 + b2,
        a01 + b01 + a0 * b1,
        a12 + b12 + a1 * b2,
        a012 + b012 + a0 * b12 + a01 * b2,
    )


def ordered(flag, mine, other):
    early = [jnp.where(flag, b, a) for a, b in zip(mine, other)]
    late = [jnp.where(flag, a, b) for a, b in zip(mine, other)]
    return early, late


def compose(loc_ref, weight_ref, own_ref, got):
    chip = lax.axis_index("tm") >> 1
    weight = weight_ref[:HALF]
    zero = jnp.zeros(weight.shape, f32)
    blocks = [parts_of(ref) for ref in (own_ref, *got)]
    before, after = [zero] * 6, [zero] * 6
    for k in range(len(got).bit_length()):
        other = blocks[1]
        flag = chip & (1 << k) != 0
        first = [jnp.where(flag, v, 0.0) for v in other]
        second = [jnp.where(flag, 0.0, v) for v in other]
        before = chain(first, before)
        after = chain(after, second)
        blocks = [chain(*ordered(flag, a, b)) for a, b in zip(blocks[::2], blocks[1::2])]
    p0, p1, p2, p01, p12, p012 = before
    e1, e2 = p0, p01
    _, t1, t2, _, t12, _ = after
    whole = blocks[0]
    totals = (whole[0], whole[3], whole[5])
    seeds = [2.0 * weight * jnp.sum(weight * total, axis=0, keepdims=True) for total in totals]

    def local(k):
        value = loc_ref[SUB * k : SUB * (k + 1), :]
        return value[:HALF], value[HALF:]

    a0, _ = local(0)
    a1, b1 = local(1)
    _, b2 = local(2)
    a01, _ = local(3)
    _, b12 = local(4)
    d0, d1, d2 = [tall(seed, seed) for seed in seeds]
    tail2 = tall(t2 + b2, t2)
    tail1 = tall(t1 + b1, t1)
    tail12 = tall(t12 + b12 + b1 * t2, t12)
    return (
        d2,
        tall(e1, e1 + a0),
        tall(e2, e2 + a01 + e1 * a1),
        d1 + d2 * tail2,
        d0 + d1 * tail1 + d2 * tail12,
    )


def slopes(chunk, wide, starts, c_ref, s_ref, u1_ref, sh_ref, sl_ref):
    rows = u1_ref.shape[0]
    scale, front1, front2, adjoint1, adjoint0 = [
        v[:, chunk * wide : (chunk + 1) * wide] for v in starts
    ]

    def keep(pair, level, values):
        high, low = split(tall(*values))
        at = (3 * chunk + level) * wide
        sh_ref[tile(pair, 2), at : at + wide] = high
        sl_ref[tile(pair, 2), at : at + wide] = low

    def fwd(pair, carry):
        f1, f2 = carry
        slope2 = []
        for which in range(2):
            at = tile(2 * pair + which)
            u1_ref[at, :] = s_ref[chunk, 1, at, :] * f1
            slope2.append(s_ref[chunk, 2, at, :] * (scale * f2))
            f2 = f2 + f1 * c_ref[chunk, 1, at, :]
            f1 = f1 + c_ref[chunk, 0, at, :]
        keep(pair, 2, slope2)
        return f1, f2

    lax.fori_loop(0, rows // (2 * SUB), fwd, (front1, front2), unroll=8)

    def bwd(step, carry):
        g1, g0 = carry
        pair = rows // (2 * SUB) - 1 - step
        slope0, slope1 = [], []
        for which in (1, 0):
            at = tile(2 * pair + which)
            slope1.append(u1_ref[at, :] * g1)
            slope0.append(s_ref[chunk, 0, at, :] * g0)
            g0 = g0 + g1 * c_ref[chunk, 1, at, :]
            g1 = g1 + scale * c_ref[chunk, 2, at, :]
        keep(pair, 0, slope0[::-1])
        keep(pair, 1, slope1[::-1])
        return g1, g0

    lax.fori_loop(0, rows // (2 * SUB), bwd, (adjoint1, adjoint0), unroll=8)


def grads_kernel(sizes, c_ref, s_ref, loc_ref, xt_ref, w_ref, weight_ref, own_ref, *refs):
    n_tm, n_freq, wide = sizes
    got, refs = refs[: n_tm // 2 - 1], refs[n_tm // 2 - 1 :]
    blocks, refs = refs[: n_tm // 2], refs[n_tm // 2 :]
    gk_ref, gs_ref, sh_ref, sl_ref, gp_ref, u1_ref, acc_ref, flat_ref = refs
    rows, chans = acc_ref.shape
    each = chans // n_tm
    me = lax.axis_index("tm")
    core, z = me & 1, lax.axis_index("freq")

    starts = compose(loc_ref, weight_ref, own_ref, got)
    for chunk in range(c_ref.shape[0]):
        slopes(chunk, wide, starts, c_ref, s_ref, u1_ref, sh_ref, sl_ref)

    main = jnp.dot(xt_ref[...], sh_ref[...], preferred_element_type=f32)
    rest = jnp.dot(xt_ref[:chans, :], sl_ref[...], preferred_element_type=f32)
    grad = main[:chans] + main[chans:] + rest
    for chunk in range(c_ref.shape[0]):
        for level in range(3):
            at = (3 * chunk + level) * wide
            for d in range(n_tm):
                gp_ref[d, level, :, chunk * wide : (chunk + 1) * wide] = grad[
                    each * d : each * (d + 1), at : at + wide
                ]
    for d in range(n_tm):
        blocks[d // 2][d % 2] = gp_ref[jnp.bitwise_xor(me, d)]

    main = lax.dot_general(sh_ref[...], w_ref[...], NT, preferred_element_type=f32)
    rest = lax.dot_general(sl_ref[...], w_ref[:chans, :], NT, preferred_element_type=f32)
    acc_ref[...] = main[:, :chans] + main[:, chans:] + rest

    def one(k, _):
        even, odd = pair_rows(acc_ref[tile(2 * k), :], acc_ref[tile(2 * k + 1), :])
        flat_ref[0, tile(k), :] = even
        flat_ref[1, tile(k), :] = odd
        return 0

    lax.fori_loop(0, rows // (2 * SUB), one, 0, unroll=8)
    piece = rows // 2 // n_freq
    for j in range(n_freq):
        at = pl.ds(pl.multiple_of(jnp.bitwise_xor(z, j) * piece, piece), piece)
        gk_ref[j] = flat_ref[core, at, :]
        gs_ref[j] = flat_ref[1 - core, at, :]


def swap(value, axis, distance):
    count = lax.axis_size(axis)
    return lax.ppermute(value, axis, [(i, i ^ distance) for i in range(count)])


def resident(value):
    return pltpu.with_memory_space_constraint(value, pltpu.HBM)


def on_device(increments, projections, phases, groups):
    steps, batch, chans = increments.shape
    freqs = phases.shape[1]
    n_tm, n_freq = lax.axis_size("tm"), lax.axis_size("freq")
    amplitude = math.sqrt(2.0 / (steps * n_tm))
    rows = 2 * steps * batch
    mine = freqs // 2
    wide = min(WIDE, mine)
    chunks = mine // wide
    each = chans // n_tm
    chips = n_tm // 2
    x = increments.reshape(rows // 2, chans)
    p = jnp.transpose(projections, (1, 0, 2))
    y = swap(x, "tm", 1)
    x, weights, turns, weight = call(
        prepare_kernel,
        "prepare",
        1.9,
        [STAY] * 4,
        [
            pltpu.VMEM((rows // 2, chans), f32),
            pltpu.VMEM((2 * chans, 3 * mine), bf16),
            pltpu.VMEM((4 * chans, 3 * mine), bf16),
            pltpu.VMEM((SUB, mine), f32),
        ],
        [
            pltpu.VMEM((chunks, 3, chans, wide), f32),
            pltpu.VMEM((3, freqs), f32),
            pltpu.SMEM((batch,), jnp.int32),
            pltpu.SemaphoreType.DMA((3 + chunks,)),
        ],
        resident(x),
        resident(p),
        resident(phases),
        resident(groups),
    )

    def waves_body(*refs):
        waves_kernel(amplitude, wide, *refs)

    big = pltpu.VMEM((chunks, 3, rows, wide), f32)
    cosines, halves, squares, local, own, flat = call(
        waves_body,
        "waves",
        8.0,
        [VECTORS] * 3,
        [
            big,
            big,
            big,
            pltpu.VMEM((6 * SUB, mine), f32),
            jax.ShapeDtypeStruct((3 * SUB, mine), f32),
            pltpu.VMEM((rows, chans), f32),
        ],
        [pltpu.VMEM((rows, 4 * chans), bf16)] + [pltpu.VMEM((rows // 4, 3 * wide), f32)] * 2,
        x,
        y,
        turns,
    )
    (xt,) = call(
        turn_kernel, "turn", 0.8, [VECTORS], [pltpu.VMEM((2 * chans, rows), bf16)], [], flat
    )

    def sines_body(*refs):
        sines_kernel(amplitude, *refs)

    got = [swap(own, "tm", 2 * d) for d in range(1, chips)]
    (sines,) = call(sines_body, "sines", 2.4, [VECTORS] * 2, [big], [], halves, squares)

    def grads_body(*refs):
        grads_kernel((n_tm, n_freq, wide), *refs)

    bshape = jax.ShapeDtypeStruct((2, 3, each, mine), f32)
    gshape = jax.ShapeDtypeStruct((n_freq, rows // 2 // n_freq, chans), f32)
    *blocks, kept, sent = call(
        grads_body,
        "grads",
        6.0,
        [VECTORS] * (6 + chips),
        [bshape] * chips + [gshape] * 2,
        [
            pltpu.VMEM((rows, 3 * mine), bf16),
            pltpu.VMEM((rows, 3 * mine), bf16),
            pltpu.VMEM((n_tm, 3, each, mine), f32),
            pltpu.VMEM((rows, wide), f32),
            pltpu.VMEM((rows, chans), f32),
            pltpu.VMEM((2, rows // 2, chans), f32),
        ],
        cosines,
        sines,
        local,
        xt,
        weights,
        weight,
        own,
        *got,
    )

    pieces = kept + swap(sent, "tm", 1)
    others = [swap(pieces[j], "freq", j) for j in range(1, n_freq)]
    others[0], blocks[0] = lax.optimization_barrier((others[0], blocks[0]))
    total = blocks[0]
    for d in range(chips - 1, 0, -1):
        total = total + swap(blocks[d], "tm", 2 * d)
    result = pieces[0]
    for other in others:
        result = result + other
    grad_increments = result.reshape(steps // n_freq, batch, chans)

    here, away = total[0], swap(total[1], "tm", 1)
    even = lax.axis_index("tm") & 1 == 0
    low, high = jnp.where(even, here, away), jnp.where(even, away, here)
    grad_projections = jnp.transpose(jnp.concatenate([low, high], axis=-1), (1, 0, 2))
    return (grad_increments, grad_projections)


def solution(mesh):
    placed = (P("tm", None, None), P(None, None, "freq"), P(None, "freq"), P())
    return jax.shard_map(
        on_device,
        mesh=mesh,
        in_specs=placed,
        out_specs=(P(("tm", "freq"), None, None), P("tm", None, "freq")),
        check_vma=False,
    )
```

```python
import math

import jax
import jax.numpy as jnp
from jax import lax
from jax.experimental import pallas as pl
from jax.experimental.pallas import tpu as pltpu
from jax.sharding import PartitionSpec as P

f32, bf16 = jnp.float32, jnp.bfloat16
SUB = 8
HALF = SUB // 2
WIDE = 256
MAGIC = 12582912.0
SIN = (3.141582022150658, -5.167142796368909, 2.541899027590427, -0.5546361970970186)
COS = (
    0.9999999534666683,
    -4.934792858675264,
    4.058411914167107,
    -1.3318801612488937,
    0.2196967986036905,
)
NT = (((1,), (1,)), ((), ()))
PARAMS = pltpu.CompilerParams(vmem_limit_bytes=16 * 1024 * 1024)
VECTORS = pl.BlockSpec(memory_space=pltpu.VMEM)
STAY = pl.BlockSpec(memory_space=pltpu.HBM)


def horner(z, coefs):
    acc = z * coefs[-1] + coefs[-2]
    for coef in coefs[-3::-1]:
        acc = acc * z + coef
    return acc


def split(value):
    high = value.astype(bf16)
    return high, (value - high.astype(f32)).astype(bf16)


def pair_rows(low, high):
    top = lax.broadcasted_iota(jnp.int32, low.shape, 0) < HALF
    first = jnp.where(top, low, pltpu.roll(high, HALF, 0))
    second = jnp.where(top, pltpu.roll(low, HALF, 0), high)
    return first, second


def tile(i, count=1):
    return pl.ds(pl.multiple_of(i * (count * SUB), count * SUB), count * SUB)


def tall(first, second):
    return jnp.concatenate([first, second], axis=0)


def call(body, name, micros, ins, outs, scratch, *operands):
    return pl.pallas_call(
        body,
        in_specs=ins,
        out_specs=[VECTORS] * len(outs),
        out_shape=outs,
        scratch_shapes=scratch,
        compiler_params=PARAMS,
        cost_estimate=pl.CostEstimate(
            flops=int(micros * 1.1e9), bytes_accessed=int(micros * 3e6), transcendentals=0
        ),
        name=name,
    )(*operands)


def prepare_kernel(x_hbm, p_hbm, ph_hbm, g_hbm, x_ref, w_ref, r_ref, weight_ref, *rest):
    p_ref, ph_ref, g_ref, sems = rest
    chunks, _, chans, wide = p_ref.shape
    batch = g_ref.shape[0]
    core = lax.axis_index("tm") & 1
    inv = 1.0 / (2.0 * math.pi)

    def columns(chunk):
        return pl.ds(pl.multiple_of((core * chunks + chunk) * wide, wide), wide)

    fetch = [pltpu.make_async_copy(ph_hbm, ph_ref, sems.at[0])]
    for k in range(chunks):
        fetch.append(
            pltpu.make_async_copy(p_hbm.at[:, :, columns(k)], p_ref.at[k], sems.at[1 + k])
        )
    fetch_x = pltpu.make_async_copy(x_hbm, x_ref, sems.at[1 + chunks])
    fetch_g = pltpu.make_async_copy(g_hbm, g_ref, sems.at[2 + chunks])
    for copy in fetch + [fetch_x, fetch_g]:
        copy.start()
    fetch[0].wait()
    row = lax.broadcasted_iota(jnp.int32, (chans, wide), 0)
    for chunk in range(chunks):
        fetch[1 + chunk].wait()
        for level in range(3):
            cols = slice((3 * chunk + level) * wide, (3 * chunk + level + 1) * wide)
            high, low = split(p_ref[chunk, level])
            w_ref[:chans, cols] = high
            w_ref[chans:, cols] = low
            high, low = split(p_ref[chunk, level] * inv)
            phase = ph_ref[level : level + 1, columns(chunk)] * inv
            phase0 = phase.astype(bf16).astype(f32)
            phase1 = (phase - phase0).astype(bf16).astype(f32)
            phase2 = phase - phase0 - phase1
            extra = jnp.where(row == 0, phase0, jnp.where(row == 1, phase1, phase2))
            extra = jnp.where(row < 3, extra, 0.0).astype(bf16)
            for k, part in enumerate((high, high, low, extra)):
                r_ref[chans * k : chans * (k + 1), cols] = part
    fetch_g.wait()
    row = lax.broadcasted_iota(jnp.int32, weight_ref.shape, 0)
    weight = jnp.zeros(weight_ref.shape, f32)
    for b in range(batch):
        value = jnp.where(g_ref[b] == 1, 2.0 / batch, -2.0 / batch)
        weight = jnp.where(row == b, value, weight)
    weight_ref[...] = weight
    fetch_x.wait()


def turn_kernel(flat_ref, xt_ref):
    chans = flat_ref.shape[1]
    high, low = split(flat_ref[...].T)
    xt_ref[:chans, :] = high
    xt_ref[chans:, :] = low


def waves_kernel(amplitude, wide, x_ref, y_ref, r_ref, *rest):
    c_ref, half_ref, z_ref, loc_ref, snd_ref, flat_ref, xs_ref, ang0_ref, ang1_ref = rest
    rows, chans = flat_ref.shape
    chunks = c_ref.shape[0]
    core = lax.axis_index("tm") & 1
    root = math.sqrt(2.0 * amplitude)
    sin_coefs = [root * coef for coef in SIN]
    lane = lax.broadcasted_iota(jnp.int32, (2 * SUB, chans), 1)
    ones = jnp.where(lane < 3, 1.0, 0.0).astype(bf16)

    def pairs(even_ref, odd_ref):
        def one(k, _):
            both = tall(*pair_rows(even_ref[tile(k), :], odd_ref[tile(k), :]))
            flat_ref[tile(k, 2), :] = both
            high, low = split(both)
            xs_ref[tile(k, 2), :] = jnp.concatenate([high, low, high, ones], axis=1)
            return 0

        lax.fori_loop(0, rows // (2 * SUB), one, 0, unroll=8)

    @pl.when(core == 0)
    def _():
        pairs(x_ref, y_ref)

    @pl.when(core == 1)
    def _():
        pairs(y_ref, x_ref)

    block = ang0_ref.shape[0]
    blocks = rows // block

    def turns(item, ang_ref):
        at = pl.ds(pl.multiple_of(lax.rem(item, blocks) * block, block), block)
        cols = pl.ds(pl.multiple_of(lax.div(item, blocks) * (3 * wide), 3 * wide), 3 * wide)
        ang_ref[...] = jnp.dot(xs_ref[at, :], r_ref[:, cols], preferred_element_type=f32)

    def sums_over(chunk, base, ang_ref, carry):
        for k in range(block // SUB):
            s0, s1, s2, s01, s12, s012 = carry
            at = pl.ds(pl.multiple_of(base + k * SUB, SUB), SUB)
            cosines = []
            for level in range(3):
                turn = ang_ref[k * SUB : (k + 1) * SUB, level * wide : (level + 1) * wide]
                r = turn - ((turn + MAGIC) - MAGIC)
                z = r * r
                sine = r * horner(z, sin_coefs)
                wave = amplitude - sine * sine
                c_ref[chunk, level, at, :] = wave
                half_ref[chunk, level, at, :] = sine
                z_ref[chunk, level, at, :] = z
                cosines.append(wave)
            c0, c1, c2 = cosines
            s012 = s012 + s01 * c2
            s12 = s12 + s1 * c2
            s01 = s01 + s0 * c1
            carry = (s0 + c0, s1 + c1, s2 + c2, s01, s12, s012)
        return carry

    zero = jnp.zeros((SUB, wide), f32)
    turns(jnp.int32(0), ang0_ref)
    for chunk in range(chunks):
        here = slice(chunk * wide, (chunk + 1) * wide)

        def step(i, carry):
            item = chunk * blocks + 2 * i
            turns(item + 1, ang1_ref)
            carry = sums_over(chunk, 2 * i * block, ang0_ref, carry)
            turns(jnp.minimum(item + 2, chunks * blocks - 1), ang0_ref)
            return sums_over(chunk, (2 * i + 1) * block, ang1_ref, carry)

        sums = lax.fori_loop(0, blocks // 2, step, (zero,) * 6)
        for k in range(6):
            loc_ref[SUB * k : SUB * (k + 1), here] = sums[k]
        a0, a1, a2, a01, a12, a012 = [v[:HALF] for v in sums]
        b0, b1, b2, b01, b12, b012 = [v[HALF:] for v in sums]
        both = (
            a0 + b0,
            a1 + b1,
            a2 + b2,
            a01 + b01 + a0 * b1,
            a12 + b12 + a1 * b2,
            a012 + b012 + a0 * b12 + a01 * b2,
        )
        for k in range(6):
            snd_ref[HALF * k : HALF * (k + 1), here] = both[k]


def sines_kernel(amplitude, half_ref, z_ref, s_ref):
    chunks, levels, rows, _ = s_ref.shape
    coefs = [-math.sqrt(2.0 * amplitude) * coef for coef in COS]
    for chunk in range(chunks):
        for level in range(levels):

            def step(i, _):
                value = horner(z_ref[chunk, level, tile(i), :], coefs)
                s_ref[chunk, level, tile(i), :] = half_ref[chunk, level, tile(i), :] * value
                return 0

            lax.fori_loop(0, rows // SUB, step, 0, unroll=16)


def parts_of(ref):
    return [ref[HALF * k : HALF * (k + 1), :] for k in range(6)]


def chain(early, late):
    a0, a1, a2, a01, a12, a012 = early
    b0, b1, b2, b01, b12, b012 = late
    return (
        a0 + b0,
        a1 + b1,
        a2 + b2,
        a01 + b01 + a0 * b1,
        a12 + b12 + a1 * b2,
        a012 + b012 + a0 * b12 + a01 * b2,
    )


def ordered(flag, mine, other):
    early = [jnp.where(flag, b, a) for a, b in zip(mine, other)]
    late = [jnp.where(flag, a, b) for a, b in zip(mine, other)]
    return early, late


def compose(loc_ref, weight_ref, own_ref, got):
    chip = lax.axis_index("tm") >> 1
    weight = weight_ref[:HALF]
    zero = jnp.zeros(weight.shape, f32)
    blocks = [parts_of(ref) for ref in (own_ref, *got)]
    before, after = [zero] * 6, [zero] * 6
    for k in range(len(got).bit_length()):
        other = blocks[1]
        flag = chip & (1 << k) != 0
        first = [jnp.where(flag, v, 0.0) for v in other]
        second = [jnp.where(flag, 0.0, v) for v in other]
        before = chain(first, before)
        after = chain(after, second)
        blocks = [chain(*ordered(flag, a, b)) for a, b in zip(blocks[::2], blocks[1::2])]
    p0, p1, p2, p01, p12, p012 = before
    e1, e2 = p0, p01
    _, t1, t2, _, t12, _ = after
    whole = blocks[0]
    totals = (whole[0], whole[3], whole[5])
    seeds = [2.0 * weight * jnp.sum(weight * total, axis=0, keepdims=True) for total in totals]

    def local(k):
        value = loc_ref[SUB * k : SUB * (k + 1), :]
        return value[:HALF], value[HALF:]

    a0, _ = local(0)
    a1, b1 = local(1)
    _, b2 = local(2)
    a01, _ = local(3)
    _, b12 = local(4)
    d0, d1, d2 = [tall(seed, seed) for seed in seeds]
    tail2 = tall(t2 + b2, t2)
    tail1 = tall(t1 + b1, t1)
    tail12 = tall(t12 + b12 + b1 * t2, t12)
    return (
        d2,
        tall(e1, e1 + a0),
        tall(e2, e2 + a01 + e1 * a1),
        d1 + d2 * tail2,
        d0 + d1 * tail1 + d2 * tail12,
    )


def slopes(chunk, wide, starts, c_ref, s_ref, u1_ref, sh_ref, sl_ref):
    rows = u1_ref.shape[0]
    scale, front1, front2, adjoint1, adjoint0 = [
        v[:, chunk * wide : (chunk + 1) * wide] for v in starts
    ]

    def keep(pair, level, values):
        high, low = split(tall(*values))
        at = (3 * chunk + level) * wide
        sh_ref[tile(pair, 2), at : at + wide] = high
        sl_ref[tile(pair, 2), at : at + wide] = low

    def fwd(pair, carry):
        f1, f2 = carry
        slope2 = []
        for which in range(2):
            at = tile(2 * pair + which)
            u1_ref[at, :] = s_ref[chunk, 1, at, :] * f1
            slope2.append(s_ref[chunk, 2, at, :] * (scale * f2))
            f2 = f2 + f1 * c_ref[chunk, 1, at, :]
            f1 = f1 + c_ref[chunk, 0, at, :]
        keep(pair, 2, slope2)
        return f1, f2

    lax.fori_loop(0, rows // (2 * SUB), fwd, (front1, front2), unroll=8)

    def bwd(step, carry):
        g1, g0 = carry
        pair = rows // (2 * SUB) - 1 - step
        slope0, slope1 = [], []
        for which in (1, 0):
            at = tile(2 * pair + which)
            slope1.append(u1_ref[at, :] * g1)
            slope0.append(s_ref[chunk, 0, at, :] * g0)
            g0 = g0 + g1 * c_ref[chunk, 1, at, :]
            g1 = g1 + scale * c_ref[chunk, 2, at, :]
        keep(pair, 0, slope0[::-1])
        keep(pair, 1, slope1[::-1])
        return g1, g0

    lax.fori_loop(0, rows // (2 * SUB), bwd, (adjoint1, adjoint0), unroll=8)


def grads_kernel(sizes, c_ref, s_ref, loc_ref, xt_ref, w_ref, weight_ref, own_ref, *refs):
    n_tm, n_freq, wide = sizes
    got, refs = refs[: n_tm // 2 - 1], refs[n_tm // 2 - 1 :]
    blocks, refs = refs[: n_tm // 2], refs[n_tm // 2 :]
    gk_ref, gs_ref, sh_ref, sl_ref, gp_ref, u1_ref, acc_ref, flat_ref = refs
    rows, chans = acc_ref.shape
    each = chans // n_tm
    me = lax.axis_index("tm")
    core, z = me & 1, lax.axis_index("freq")

    starts = compose(loc_ref, weight_ref, own_ref, got)
    for chunk in range(c_ref.shape[0]):
        slopes(chunk, wide, starts, c_ref, s_ref, u1_ref, sh_ref, sl_ref)

    main = jnp.dot(xt_ref[...], sh_ref[...], preferred_element_type=f32)
    rest = jnp.dot(xt_ref[:chans, :], sl_ref[...], preferred_element_type=f32)
    grad = main[:chans] + main[chans:] + rest
    for chunk in range(c_ref.shape[0]):
        for level in range(3):
            at = (3 * chunk + level) * wide
            for d in range(n_tm):
                gp_ref[d, level, :, chunk * wide : (chunk + 1) * wide] = grad[
                    each * d : each * (d + 1), at : at + wide
                ]
    for d in range(n_tm):
        blocks[d // 2][d % 2] = gp_ref[jnp.bitwise_xor(me, d)]

    main = lax.dot_general(sh_ref[...], w_ref[...], NT, preferred_element_type=f32)
    rest = lax.dot_general(sl_ref[...], w_ref[:chans, :], NT, preferred_element_type=f32)
    acc_ref[...] = main[:, :chans] + main[:, chans:] + rest

    def one(k, _):
        even, odd = pair_rows(acc_ref[tile(2 * k), :], acc_ref[tile(2 * k + 1), :])
        flat_ref[0, tile(k), :] = even
        flat_ref[1, tile(k), :] = odd
        return 0

    lax.fori_loop(0, rows // (2 * SUB), one, 0, unroll=8)
    piece = rows // 2 // n_freq
    for j in range(n_freq):
        at = pl.ds(pl.multiple_of(jnp.bitwise_xor(z, j) * piece, piece), piece)
        gk_ref[j] = flat_ref[core, at, :]
        gs_ref[j] = flat_ref[1 - core, at, :]


def swap(value, axis, distance):
    count = lax.axis_size(axis)
    return lax.ppermute(value, axis, [(i, i ^ distance) for i in range(count)])


def resident(value):
    return pltpu.with_memory_space_constraint(value, pltpu.HBM)


def on_device(increments, projections, phases, groups):
    steps, batch, chans = increments.shape
    freqs = phases.shape[1]
    n_tm, n_freq = lax.axis_size("tm"), lax.axis_size("freq")
    amplitude = math.sqrt(2.0 / (steps * n_tm))
    rows = 2 * steps * batch
    mine = freqs // 2
    wide = min(WIDE, mine)
    chunks = mine // wide
    each = chans // n_tm
    chips = n_tm // 2
    x = increments.reshape(rows // 2, chans)
    p = jnp.transpose(projections, (1, 0, 2))
    y = swap(x, "tm", 1)
    x, weights, turns, weight = call(
        prepare_kernel,
        "prepare",
        1.9,
        [STAY] * 4,
        [
            pltpu.VMEM((rows // 2, chans), f32),
            pltpu.VMEM((2 * chans, 3 * mine), bf16),
            pltpu.VMEM((4 * chans, 3 * mine), bf16),
            pltpu.VMEM((SUB, mine), f32),
        ],
        [
            pltpu.VMEM((chunks, 3, chans, wide), f32),
            pltpu.VMEM((3, freqs), f32),
            pltpu.SMEM((batch,), jnp.int32),
            pltpu.SemaphoreType.DMA((3 + chunks,)),
        ],
        resident(x),
        resident(p),
        resident(phases),
        resident(groups),
    )

    def waves_body(*refs):
        waves_kernel(amplitude, wide, *refs)

    big = pltpu.VMEM((chunks, 3, rows, wide), f32)
    cosines, halves, squares, local, own, flat = call(
        waves_body,
        "waves",
        8.0,
        [VECTORS] * 3,
        [
            big,
            big,
            big,
            pltpu.VMEM((6 * SUB, mine), f32),
            jax.ShapeDtypeStruct((3 * SUB, mine), f32),
            pltpu.VMEM((rows, chans), f32),
        ],
        [pltpu.VMEM((rows, 4 * chans), bf16)] + [pltpu.VMEM((rows // 4, 3 * wide), f32)] * 2,
        x,
        y,
        turns,
    )
    (xt,) = call(
        turn_kernel, "turn", 0.8, [VECTORS], [pltpu.VMEM((2 * chans, rows), bf16)], [], flat
    )

    def sines_body(*refs):
        sines_kernel(amplitude, *refs)

    got = [swap(own, "tm", 2 * d) for d in range(1, chips)]
    (sines,) = call(sines_body, "sines", 2.4, [VECTORS] * 2, [big], [], halves, squares)

    def grads_body(*refs):
        grads_kernel((n_tm, n_freq, wide), *refs)

    bshape = jax.ShapeDtypeStruct((2, 3, each, mine), f32)
    gshape = jax.ShapeDtypeStruct((n_freq, rows // 2 // n_freq, chans), f32)
    *blocks, kept, sent = call(
        grads_body,
        "grads",
        6.0,
        [VECTORS] * (6 + chips),
        [bshape] * chips + [gshape] * 2,
        [
            pltpu.VMEM((rows, 3 * mine), bf16),
            pltpu.VMEM((rows, 3 * mine), bf16),
            pltpu.VMEM((n_tm, 3, each, mine), f32),
            pltpu.VMEM((rows, wide), f32),
            pltpu.VMEM((rows, chans), f32),
            pltpu.VMEM((2, rows // 2, chans), f32),
        ],
        cosines,
        sines,
        local,
        xt,
        weights,
        weight,
        own,
        *got,
    )

    pieces = kept + swap(sent, "tm", 1)
    pieces, blocks[1] = lax.optimization_barrier((pieces, blocks[1]))
    others = [swap(pieces[j], "freq", j) for j in range(1, n_freq)]
    others[0], blocks[0] = lax.optimization_barrier((others[0], blocks[0]))
    total = blocks[0]
    for d in range(chips - 1, 0, -1):
        total = total + swap(blocks[d], "tm", 2 * d)
    result = pieces[0]
    for other in others:
        result = result + other
    grad_increments = result.reshape(steps // n_freq, batch, chans)

    here, away = total[0], swap(total[1], "tm", 1)
    even = lax.axis_index("tm") & 1 == 0
    low, high = jnp.where(even, here, away), jnp.where(even, away, here)
    grad_projections = jnp.transpose(jnp.concatenate([low, high], axis=-1), (1, 0, 2))
    return (grad_increments, grad_projections)


def solution(mesh):
    placed = (P("tm", None, None), P(None, None, "freq"), P(None, "freq"), P())
    return jax.shard_map(
        on_device,
        mesh=mesh,
        in_specs=placed,
        out_specs=(P(("tm", "freq"), None, None), P("tm", None, "freq")),
        check_vma=False,
    )
```

```python
import math

import jax
import jax.numpy as jnp
from jax import lax
from jax.experimental import pallas as pl
from jax.experimental.pallas import tpu as pltpu
from jax.sharding import PartitionSpec as P

f32, bf16 = jnp.float32, jnp.bfloat16
SUB = 8
HALF = SUB // 2
WIDE = 256
MAGIC = 12582912.0
SIN = (3.141582022150658, -5.167142796368909, 2.541899027590427, -0.5546361970970186)
COS = (
    0.9999999534666683,
    -4.934792858675264,
    4.058411914167107,
    -1.3318801612488937,
    0.2196967986036905,
)
NT = (((1,), (1,)), ((), ()))
PARAMS = pltpu.CompilerParams(vmem_limit_bytes=20 * 1024 * 1024)
VECTORS = pl.BlockSpec(memory_space=pltpu.VMEM)
STAY = pl.BlockSpec(memory_space=pltpu.HBM)


def horner(z, coefs):
    acc = z * coefs[-1] + coefs[-2]
    for coef in coefs[-3::-1]:
        acc = acc * z + coef
    return acc


def split(value):
    high = value.astype(bf16)
    return high, (value - high.astype(f32)).astype(bf16)


def pair_rows(low, high):
    top = lax.broadcasted_iota(jnp.int32, low.shape, 0) < HALF
    first = jnp.where(top, low, pltpu.roll(high, HALF, 0))
    second = jnp.where(top, pltpu.roll(low, HALF, 0), high)
    return first, second


def tile(i, count=1):
    return pl.ds(pl.multiple_of(i * (count * SUB), count * SUB), count * SUB)


def tall(first, second):
    return jnp.concatenate([first, second], axis=0)


def call(body, name, micros, ins, outs, scratch, *operands):
    return pl.pallas_call(
        body,
        in_specs=ins,
        out_specs=[VECTORS] * len(outs),
        out_shape=outs,
        scratch_shapes=scratch,
        compiler_params=PARAMS,
        cost_estimate=pl.CostEstimate(
            flops=int(micros * 1.1e9), bytes_accessed=int(micros * 3e6), transcendentals=0
        ),
        name=name,
    )(*operands)


def prepare_kernel(x_hbm, p_hbm, ph_hbm, g_hbm, x_ref, w_ref, r_ref, weight_ref, *rest):
    p_ref, ph_ref, g_ref, sems = rest
    chunks, _, chans, wide = p_ref.shape
    batch = g_ref.shape[0]
    core = lax.axis_index("tm") & 1
    inv = 1.0 / (2.0 * math.pi)

    def columns(chunk):
        return pl.ds(pl.multiple_of((core * chunks + chunk) * wide, wide), wide)

    fetch = [pltpu.make_async_copy(ph_hbm, ph_ref, sems.at[0])]
    for k in range(chunks):
        fetch.append(
            pltpu.make_async_copy(p_hbm.at[:, :, columns(k)], p_ref.at[k], sems.at[1 + k])
        )
    fetch_x = pltpu.make_async_copy(x_hbm, x_ref, sems.at[1 + chunks])
    fetch_g = pltpu.make_async_copy(g_hbm, g_ref, sems.at[2 + chunks])
    for copy in fetch + [fetch_x, fetch_g]:
        copy.start()
    fetch[0].wait()
    row = lax.broadcasted_iota(jnp.int32, (chans, wide), 0)
    for chunk in range(chunks):
        fetch[1 + chunk].wait()
        for level in range(3):
            cols = slice((3 * chunk + level) * wide, (3 * chunk + level + 1) * wide)
            high, low = split(p_ref[chunk, level])
            w_ref[:chans, cols] = high
            w_ref[chans:, cols] = low
            high, low = split(p_ref[chunk, level] * inv)
            phase = ph_ref[level : level + 1, columns(chunk)] * inv
            phase0 = phase.astype(bf16).astype(f32)
            phase1 = (phase - phase0).astype(bf16).astype(f32)
            phase2 = phase - phase0 - phase1
            extra = jnp.where(row == 0, phase0, jnp.where(row == 1, phase1, phase2))
            extra = jnp.where(row < 3, extra, 0.0).astype(bf16)
            for k, part in enumerate((high, high, low, extra)):
                r_ref[chans * k : chans * (k + 1), cols] = part
    fetch_g.wait()
    row = lax.broadcasted_iota(jnp.int32, weight_ref.shape, 0)
    weight = jnp.zeros(weight_ref.shape, f32)
    for b in range(batch):
        value = jnp.where(g_ref[b] == 1, 2.0 / batch, -2.0 / batch)
        weight = jnp.where(row == b, value, weight)
    weight_ref[...] = weight
    fetch_x.wait()


def turn_kernel(flat_ref, xt_ref):
    chans = flat_ref.shape[1]
    high, low = split(flat_ref[...].T)
    xt_ref[:chans, :] = high
    xt_ref[chans:, :] = low


def waves_kernel(amplitude, wide, x_ref, y_ref, r_ref, *rest):
    c_ref, half_ref, z_ref, loc_ref, snd_ref, flat_ref, xs_ref, ang0_ref, ang1_ref = rest
    rows, chans = flat_ref.shape
    chunks = c_ref.shape[0]
    core = lax.axis_index("tm") & 1
    root = math.sqrt(2.0 * amplitude)
    sin_coefs = [root * coef for coef in SIN]
    lane = lax.broadcasted_iota(jnp.int32, (2 * SUB, chans), 1)
    ones = jnp.where(lane < 3, 1.0, 0.0).astype(bf16)

    def pairs(even_ref, odd_ref):
        def one(k, _):
            both = tall(*pair_rows(even_ref[tile(k), :], odd_ref[tile(k), :]))
            flat_ref[tile(k, 2), :] = both
            high, low = split(both)
            xs_ref[tile(k, 2), :] = jnp.concatenate([high, low, high, ones], axis=1)
            return 0

        lax.fori_loop(0, rows // (2 * SUB), one, 0, unroll=16)

    @pl.when(core == 0)
    def _():
        pairs(x_ref, y_ref)

    @pl.when(core == 1)
    def _():
        pairs(y_ref, x_ref)

    block = ang0_ref.shape[0]
    blocks = rows // block

    def turns(item, ang_ref):
        at = pl.ds(pl.multiple_of(lax.rem(item, blocks) * block, block), block)
        cols = pl.ds(pl.multiple_of(lax.div(item, blocks) * (3 * wide), 3 * wide), 3 * wide)
        ang_ref[...] = jnp.dot(xs_ref[at, :], r_ref[:, cols], preferred_element_type=f32)

    def sums_over(chunk, base, ang_ref, carry):
        for k in range(block // SUB):
            s0, s1, s2, s01, s12, s012 = carry
            at = pl.ds(pl.multiple_of(base + k * SUB, SUB), SUB)
            cosines = []
            for level in range(3):
                turn = ang_ref[k * SUB : (k + 1) * SUB, level * wide : (level + 1) * wide]
                r = turn - ((turn + MAGIC) - MAGIC)
                z = r * r
                sine = r * horner(z, sin_coefs)
                wave = amplitude - sine * sine
                c_ref[chunk, level, at, :] = wave
                half_ref[chunk, level, at, :] = sine
                z_ref[chunk, level, at, :] = z
                cosines.append(wave)
            c0, c1, c2 = cosines
            s012 = s012 + s01 * c2
            s12 = s12 + s1 * c2
            s01 = s01 + s0 * c1
            carry = (s0 + c0, s1 + c1, s2 + c2, s01, s12, s012)
        return carry

    zero = jnp.zeros((SUB, wide), f32)
    turns(jnp.int32(0), ang0_ref)
    for chunk in range(chunks):
        here = slice(chunk * wide, (chunk + 1) * wide)

        def step(i, carry):
            item = chunk * blocks + 2 * i
            turns(item + 1, ang1_ref)
            carry = sums_over(chunk, 2 * i * block, ang0_ref, carry)
            turns(jnp.minimum(item + 2, chunks * blocks - 1), ang0_ref)
            return sums_over(chunk, (2 * i + 1) * block, ang1_ref, carry)

        sums = lax.fori_loop(0, blocks // 2, step, (zero,) * 6)
        for k in range(6):
            loc_ref[SUB * k : SUB * (k + 1), here] = sums[k]
        a0, a1, a2, a01, a12, a012 = [v[:HALF] for v in sums]
        b0, b1, b2, b01, b12, b012 = [v[HALF:] for v in sums]
        both = (
            a0 + b0,
            a1 + b1,
            a2 + b2,
            a01 + b01 + a0 * b1,
            a12 + b12 + a1 * b2,
            a012 + b012 + a0 * b12 + a01 * b2,
        )
        for k in range(6):
            snd_ref[HALF * k : HALF * (k + 1), here] = both[k]


def sines_kernel(amplitude, chunk, half_ref, z_ref, s_ref):
    levels, rows, _ = s_ref.shape
    coefs = [-math.sqrt(2.0 * amplitude) * coef for coef in COS]
    for level in range(levels):

        def step(i, _):
            value = horner(z_ref[chunk, level, tile(i), :], coefs)
            s_ref[level, tile(i), :] = half_ref[chunk, level, tile(i), :] * value
            return 0

        lax.fori_loop(0, rows // SUB, step, 0, unroll=16)


def parts_of(ref):
    return [ref[HALF * k : HALF * (k + 1), :] for k in range(6)]


def chain(early, late):
    a0, a1, a2, a01, a12, a012 = early
    b0, b1, b2, b01, b12, b012 = late
    return (
        a0 + b0,
        a1 + b1,
        a2 + b2,
        a01 + b01 + a0 * b1,
        a12 + b12 + a1 * b2,
        a012 + b012 + a0 * b12 + a01 * b2,
    )


def ordered(flag, mine, other):
    early = [jnp.where(flag, b, a) for a, b in zip(mine, other)]
    late = [jnp.where(flag, a, b) for a, b in zip(mine, other)]
    return early, late


def chain_kernel(bit, own_ref, other_ref, out_ref):
    flag = (lax.axis_index("tm") >> 1) & bit != 0
    both = chain(*ordered(flag, parts_of(own_ref), parts_of(other_ref)))
    for k in range(6):
        out_ref[HALF * k : HALF * (k + 1), :] = both[k]


def compose(loc_ref, weight_ref, own_ref, got):
    chip = lax.axis_index("tm") >> 1
    weight = weight_ref[:HALF]
    zero = jnp.zeros(weight.shape, f32)
    own = parts_of(own_ref)
    before, after = [zero] * 6, [zero] * 6
    for k, ref in enumerate(got):
        other = parts_of(ref)
        flag = chip & (1 << k) != 0
        first = [jnp.where(flag, v, 0.0) for v in other]
        second = [jnp.where(flag, 0.0, v) for v in other]
        before = chain(first, before)
        after = chain(after, second)
    p0, p1, p2, p01, p12, p012 = before
    e1, e2 = p0, p01
    _, t1, t2, _, t12, _ = after
    whole = chain(chain(before, own), after)
    totals = (whole[0], whole[3], whole[5])
    seeds = [2.0 * weight * jnp.sum(weight * total, axis=0, keepdims=True) for total in totals]

    def local(k):
        value = loc_ref[SUB * k : SUB * (k + 1), :]
        return value[:HALF], value[HALF:]

    a0, _ = local(0)
    a1, b1 = local(1)
    _, b2 = local(2)
    a01, _ = local(3)
    _, b12 = local(4)
    d0, d1, d2 = [tall(seed, seed) for seed in seeds]
    tail2 = tall(t2 + b2, t2)
    tail1 = tall(t1 + b1, t1)
    tail12 = tall(t12 + b12 + b1 * t2, t12)
    return (
        d2,
        tall(e1, e1 + a0),
        tall(e2, e2 + a01 + e1 * a1),
        d1 + d2 * tail2,
        d0 + d1 * tail1 + d2 * tail12,
    )


def slopes(chunk, wide, starts, c_ref, s_ref, u1_ref, sh_ref, sl_ref):
    rows = u1_ref.shape[0]
    scale, front1, front2, adjoint1, adjoint0 = [
        v[:, chunk * wide : (chunk + 1) * wide] for v in starts
    ]

    def keep(pair, level, values):
        high, low = split(tall(*values))
        at = (3 * chunk + level) * wide
        sh_ref[tile(pair, 2), at : at + wide] = high
        sl_ref[tile(pair, 2), at : at + wide] = low

    def fwd(pair, carry):
        f1, f2 = carry
        slope2 = []
        for which in range(2):
            at = tile(2 * pair + which)
            u1_ref[at, :] = s_ref[1, at, :] * f1
            slope2.append(s_ref[2, at, :] * (scale * f2))
            f2 = f2 + f1 * c_ref[chunk, 1, at, :]
            f1 = f1 + c_ref[chunk, 0, at, :]
        keep(pair, 2, slope2)
        return f1, f2

    lax.fori_loop(0, rows // (2 * SUB), fwd, (front1, front2), unroll=16)

    def bwd(step, carry):
        g1, g0 = carry
        pair = rows // (2 * SUB) - 1 - step
        slope0, slope1 = [], []
        for which in (1, 0):
            at = tile(2 * pair + which)
            slope1.append(u1_ref[at, :] * g1)
            slope0.append(s_ref[0, at, :] * g0)
            g0 = g0 + g1 * c_ref[chunk, 1, at, :]
            g1 = g1 + scale * c_ref[chunk, 2, at, :]
        keep(pair, 0, slope0[::-1])
        keep(pair, 1, slope1[::-1])
        return g1, g0

    lax.fori_loop(0, rows // (2 * SUB), bwd, (adjoint1, adjoint0), unroll=16)


def grads_kernel(sizes, c_ref, loc_ref, xt_ref, w_ref, weight_ref, *refs):
    n_tm, n_freq, wide, levels = sizes
    chunks = c_ref.shape[0]
    sines, refs = refs[:chunks], refs[chunks:]
    own_ref, got, refs = refs[0], refs[1 : 1 + levels], refs[1 + levels :]
    blocks, refs = refs[: n_tm // 2], refs[n_tm // 2 :]
    gk_ref, gs_ref, sh_ref, sl_ref, gp_ref, u1_ref, acc_ref, flat_ref = refs
    rows, chans = acc_ref.shape
    each = chans // n_tm
    me = lax.axis_index("tm")
    core, z = me & 1, lax.axis_index("freq")

    starts = compose(loc_ref, weight_ref, own_ref, got)
    for chunk, s_ref in enumerate(sines):
        slopes(chunk, wide, starts, c_ref, s_ref, u1_ref, sh_ref, sl_ref)

    main = jnp.dot(xt_ref[...], sh_ref[...], preferred_element_type=f32)
    rest = jnp.dot(xt_ref[:chans, :], sl_ref[...], preferred_element_type=f32)
    grad = main[:chans] + main[chans:] + rest
    for chunk in range(c_ref.shape[0]):
        for level in range(3):
            at = (3 * chunk + level) * wide
            for d in range(n_tm):
                gp_ref[d, level, :, chunk * wide : (chunk + 1) * wide] = grad[
                    each * d : each * (d + 1), at : at + wide
                ]
    for d in range(n_tm):
        blocks[d // 2][d % 2] = gp_ref[jnp.bitwise_xor(me, d)]

    main = lax.dot_general(sh_ref[...], w_ref[...], NT, preferred_element_type=f32)
    rest = lax.dot_general(sl_ref[...], w_ref[:chans, :], NT, preferred_element_type=f32)
    acc_ref[...] = main[:, :chans] + main[:, chans:] + rest

    def one(k, _):
        even, odd = pair_rows(acc_ref[tile(2 * k), :], acc_ref[tile(2 * k + 1), :])
        flat_ref[0, tile(k), :] = even
        flat_ref[1, tile(k), :] = odd
        return 0

    lax.fori_loop(0, rows // (2 * SUB), one, 0, unroll=16)
    piece = rows // 2 // n_freq
    for j in range(n_freq):
        at = pl.ds(pl.multiple_of(jnp.bitwise_xor(z, j) * piece, piece), piece)
        gk_ref[j] = flat_ref[core, at, :]
        gs_ref[j] = flat_ref[1 - core, at, :]


def swap(value, axis, distance):
    count = lax.axis_size(axis)
    return lax.ppermute(value, axis, [(i, i ^ distance) for i in range(count)])


def resident(value):
    return pltpu.with_memory_space_constraint(value, pltpu.HBM)


def on_device(increments, projections, phases, groups):
    steps, batch, chans = increments.shape
    freqs = phases.shape[1]
    n_tm, n_freq = lax.axis_size("tm"), lax.axis_size("freq")
    amplitude = math.sqrt(2.0 / (steps * n_tm))
    rows = 2 * steps * batch
    mine = freqs // 2
    wide = min(WIDE, mine)
    chunks = mine // wide
    each = chans // n_tm
    chips = n_tm // 2
    x = increments.reshape(rows // 2, chans)
    p = jnp.transpose(projections, (1, 0, 2))
    y = swap(x, "tm", 1)
    x, weights, turns, weight = call(
        prepare_kernel,
        "prepare",
        1.9,
        [STAY] * 4,
        [
            pltpu.VMEM((rows // 2, chans), f32),
            pltpu.VMEM((2 * chans, 3 * mine), bf16),
            pltpu.VMEM((4 * chans, 3 * mine), bf16),
            pltpu.VMEM((SUB, mine), f32),
        ],
        [
            pltpu.VMEM((chunks, 3, chans, wide), f32),
            pltpu.VMEM((3, freqs), f32),
            pltpu.SMEM((batch,), jnp.int32),
            pltpu.SemaphoreType.DMA((3 + chunks,)),
        ],
        resident(x),
        resident(p),
        resident(phases),
        resident(groups),
    )

    def waves_body(*refs):
        waves_kernel(amplitude, wide, *refs)

    big = pltpu.VMEM((chunks, 3, rows, wide), f32)
    cosines, halves, squares, local, own, flat = call(
        waves_body,
        "waves",
        8.0,
        [VECTORS] * 3,
        [
            big,
            big,
            big,
            pltpu.VMEM((6 * SUB, mine), f32),
            jax.ShapeDtypeStruct((3 * SUB, mine), f32),
            pltpu.VMEM((rows, chans), f32),
        ],
        [pltpu.VMEM((rows, 4 * chans), bf16)] + [pltpu.VMEM((rows // 4, 3 * wide), f32)] * 2,
        x,
        y,
        turns,
    )
    (xt,) = call(
        turn_kernel, "turn", 0.8, [VECTORS], [pltpu.VMEM((2 * chans, rows), bf16)], [], flat
    )

    def sines_of(chunk):
        def sines_body(*refs):
            sines_kernel(amplitude, chunk, *refs)

        return call(
            sines_body,
            f"sines{chunk}",
            1.2,
            [VECTORS] * 2,
            [pltpu.VMEM((3, rows, wide), f32)],
            [],
            halves,
            squares,
        )[0]

    levels = chips.bit_length() - 1
    got, sines, current = [], [], own
    for k in range(levels):
        other = swap(current, "tm", 2 << k)
        if k < levels - 1:

            def chain_body(*refs, bit=1 << k):
                chain_kernel(bit, *refs)

            if len(sines) < chunks:
                sines.append(sines_of(len(sines)))
                other, sines[-1] = lax.optimization_barrier((other, sines[-1]))
            (current,) = call(
                chain_body,
                "chain",
                0.1,
                [VECTORS] * 2,
                [jax.ShapeDtypeStruct(own.shape, f32)],
                [],
                current,
                other,
            )
            halves, current = lax.optimization_barrier((halves, current))
        got.append(other)
    sines += [sines_of(k) for k in range(len(sines), chunks)]

    def grads_body(*refs):
        grads_kernel((n_tm, n_freq, wide, levels), *refs)

    bshape = jax.ShapeDtypeStruct((2, 3, each, mine), f32)
    gshape = jax.ShapeDtypeStruct((n_freq, rows // 2 // n_freq, chans), f32)
    *blocks, kept, sent = call(
        grads_body,
        "grads",
        6.0,
        [VECTORS] * (6 + chunks + levels),
        [bshape] * chips + [gshape] * 2,
        [
            pltpu.VMEM((rows, 3 * mine), bf16),
            pltpu.VMEM((rows, 3 * mine), bf16),
            pltpu.VMEM((n_tm, 3, each, mine), f32),
            pltpu.VMEM((rows, wide), f32),
            pltpu.VMEM((rows, chans), f32),
            pltpu.VMEM((2, rows // 2, chans), f32),
        ],
        cosines,
        local,
        xt,
        weights,
        weight,
        *sines,
        own,
        *got,
    )

    pieces = kept + swap(sent, "tm", 1)
    others = [swap(pieces[j], "freq", j) for j in range(1, n_freq)]
    others[0], blocks[0] = lax.optimization_barrier((others[0], blocks[0]))
    total = blocks[0]
    for d in range(chips - 1, 0, -1):
        total = total + swap(blocks[d], "tm", 2 * d)
    result = pieces[0]
    for other in others:
        result = result + other
    grad_increments = result.reshape(steps // n_freq, batch, chans)

    here, away = total[0], swap(total[1], "tm", 1)
    even = lax.axis_index("tm") & 1 == 0
    low, high = jnp.where(even, here, away), jnp.where(even, away, here)
    grad_projections = jnp.transpose(jnp.concatenate([low, high], axis=-1), (1, 0, 2))
    return (grad_increments, grad_projections)


def solution(mesh):
    placed = (P("tm", None, None), P(None, None, "freq"), P(None, "freq"), P())
    return jax.shard_map(
        on_device,
        mesh=mesh,
        in_specs=placed,
        out_specs=(P(("tm", "freq"), None, None), P("tm", None, "freq")),
        check_vma=False,
    )
```
